32 devices in a mesh: ctx: 16 (over z, y, x), ws: 2 (over core).
Axes of the slice: x: 2, y: 2, z: 4, core: 2. Of those that a mesh axis runs over, the one named last changes fastest.
Arguments:
- tokens: bfloat16 [16384, 1536], P('ctx'), may hold values from -6 to 6
- cotangent: bfloat16 [16384, 1536], P('ctx'), may hold values from -6 to 6
- first_gain: float32 [1536], replicated, may hold values from 0.5 to 1.5
- query_weight: bfloat16 [1536, 1536], P(None, 'ws'), may hold values from -0.15625 to 0.15625
- key_projection_weight: bfloat16 [1536, 256], P(None, 'ws'), may hold values from -0.15625 to 0.15625
- value_projection_weight: bfloat16 [1536, 256], P(None, 'ws'), may hold values from -0.15625 to 0.15625
- out_weight: bfloat16 [1536, 1536], P('ws'), may hold values from -0.625 to 0.625
- second_gain: float32 [1536], replicated, may hold values from 0.5 to 1.5
- gate_weight: bfloat16 [8, 1536, 768], P(None, None, 'ws'), may hold values from -0.15625 to 0.15625
- up_weight: bfloat16 [8, 1536, 768], P(None, None, 'ws'), may hold values from -0.15625 to 0.15625
- down_weight: bfloat16 [8, 768, 1536], P(None, 'ws'), may hold values from -0.4375 to 0.4375
- segments: int32 [16384], replicated, may hold values from 0 to 16, never falling along the last dimension, each value on 1 to 2000 neighbouring positions
- live_mask: int32 [16384], replicated, may hold values 0 or 1
- routes: int32 [16384, 4], P('ctx'), may hold values from 0 to 7, all different within a row
- gate_values: float32 [16384, 4], P('ctx'), may hold values from 0.2 to 0.5
Outputs:
- output: bfloat16 [16384, 1536], P('ctx')
- token_grad: float32 [16384, 1536], P('ctx')
- first_grad: float32 [1536], P('ctx')
- query_grad: float32 [1536, 1536], P('ctx', 'ws')
- key_grad: float32 [1536, 256], P('ctx', 'ws')
- value_grad: float32 [1536, 256], P('ctx', 'ws')
- out_grad: float32 [1536, 1536], P('ws', 'ctx')
- second_grad: float32 [1536], P('ctx')
- gate_grad: float32 [8, 1536, 768], P(None, 'ctx', 'ws')
- up_grad: float32 [8, 1536, 768], P(None, 'ctx', 'ws')
- down_grad: float32 [8, 768, 1536], P(None, 'ws', 'ctx')
The draws below stay inside these ranges and needn't reach their ends.
Inputs may be any that keep to these rules, and one draw needn't show every extreme that they name: `segments`: document numbers never fall along the pack; each document holds 1 to 2000 tokens and one holds exactly 2000. `routes`: each token names 4 different experts, and every expert is named by some token.
All inputs are finite; a program needn't handle non-finite values.
Results may differ from the reference program's by a relative error of at most 0.02.
Values may be sent and summed in bfloat16 or wider, within the bound.
No kernel may reach another device: no remote copies, remote signals or barrier semaphores. Data moves between devices by JAX's collectives and lax.ppermute only.
A program may use at most 320 MiB of HBM per device.

```python
import math
import jax
import jax.numpy as jnp
import numpy as np
from jax import lax

MODEL_DIMENSION = 1536
QUERY_HEAD_COUNT = 12
KEY_VALUE_HEADS = 2
HEAD_DIMENSION = 128
FF = 768
TOP = 4
EXPERTS = 8
TOK_DEV = 1024
DOC_MAX = 2000
PACKED_TOKENS = 16384
CAP = 640
SEGS = 17


def set_ends(values, stream_key, low, high):
    extent = values.shape
    index_at = [jax.random.randint(jax.random.fold_in(stream_key, axis), (), 0, extent[axis]) for axis in range(len(extent))]
    values = values.at[tuple(index_at)].set(low)
    longest = extent.index(max(extent))
    index_at[longest] = (index_at[longest] + 1) % extent[longest]
    return values.at[tuple(index_at)].set(high)


def with_spikes(values, own_key, source, target, blocks, factor):
    def block_of(position):
        return (jnp.arange(values.shape[position]) // (values.shape[position] // blocks)).reshape((-1,) + (1,) * (values.ndim - 1 - position))

    one_side = jax.random.permutation(own_key, blocks)[block_of(target)]
    second = (block_of(target) + blocks // 2) % blocks
    return jnp.where((block_of(source) == one_side) | (block_of(source) == second), factor * values, values)


def levels(rng, dims, cuts, smallest, largest):
    level, own = 1.0, jax.random.fold_in(rng, 6)
    for axis_at, shards_of in cuts:
        heights = jnp.exp(jax.random.uniform(jax.random.fold_in(own, axis_at), (shards_of,), jnp.float32, smallest / len(cuts), largest / len(cuts)))
        level = level * jnp.repeat(heights, dims[axis_at] // shards_of).reshape([-1 if axis == axis_at else 1 for axis in range(len(dims))])
    return level


def picks_of(own_key, rows, number_of, top, lift):
    order = jax.random.permutation(jax.random.fold_in(own_key, 1), number_of)
    pull = order
    for power in range(3):
        pull = pull * pull // number_of
    pull = pull * lift // number_of
    tickets = jax.random.randint(jax.random.fold_in(own_key, 2), (rows, number_of), 0, 4096) + pull
    sure = jax.random.permutation(jax.random.fold_in(own_key, 3), rows)[jnp.arange(number_of) % rows]
    tickets = jnp.where(jnp.arange(rows)[:, None] == sure[None, :], 1 << 14, tickets)
    merit = tickets * number_of + jnp.arange(number_of)
    return lax.top_k(merit.astype(jnp.int32), top)[1].astype(jnp.int32)


def profile(count, total, bound, lean):
    portions = [(1 << 20) // math.isqrt(standing ** lean) + 1 for standing in range(2, count + 1)]
    surplus, given = total - bound - (count - 1), [1] * (count - 1)
    while surplus > 0:
        candidates = [i for i in range(count - 1) if given[i] < bound]
        whole, remaining = sum([portions[i] for i in candidates]), surplus
        for i in candidates:
            more = min(bound - given[i], max(1, remaining * portions[i] // whole), surplus)
            given[i] = given[i] + more
            surplus = surplus - more
    return np.array([bound] + given)


def uneven(key, number_of, total, limit, lean):
    if number_of == 2:
        one = jax.random.randint(key, (), max(1, total - limit), min(limit, total - 1) + 1)
        return jnp.stack([one, total - one])
    tallies = jnp.asarray(profile(number_of, total, limit, lean), jnp.int32)
    pairs = (number_of - 1) // 2
    giver, receiver = tallies[1:1 + 2 * pairs:2], tallies[2:2 + 2 * pairs:2]
    room = jnp.minimum(giver - 1, limit - receiver)
    shifted = jax.random.randint(jax.random.fold_in(key, 1), (pairs,), 0, 1 << 20) % (room + 1)
    tallies = tallies.at[1:1 + 2 * pairs:2].set(giver - shifted).at[2:2 + 2 * pairs:2].set(receiver + shifted)
    return tallies[jax.random.permutation(jax.random.fold_in(key, 2), number_of)]


def bell_draw(own_key, extent, deviation, limit, cuts=(), held_as=jnp.bfloat16):
    drawn = deviation * jax.random.normal(own_key, extent, jnp.float32)
    if cuts:
        drawn = drawn * levels(own_key, extent, cuts, -0.22, 0.18)
    return jnp.clip(drawn, -limit, limit).astype(held_as)


def gaussian_with(own_key, dims, width, reach, split, heavy, kind=jnp.bfloat16):
    values = width * jax.random.normal(own_key, dims, jnp.float32)
    if split:
        values = values * levels(own_key, dims, split, -0.22, 0.18)
    return jnp.clip(with_spikes(values, jax.random.fold_in(own_key, 3), *heavy), -reach, reach).astype(kind)


def setup_inputs(seed: int = 0) -> dict:
    key_list = jax.random.split(jax.random.key(seed), 16)
    tokens = bell_draw(key_list[0], (PACKED_TOKENS, MODEL_DIMENSION), 1.0, 6.0, ((0, 16),))
    cotangent = gaussian_with(key_list[1], (PACKED_TOKENS, MODEL_DIMENSION), 1.0, 6.0, ((0, 16),), (0, 1, 16, 2.0))
    first_gain = jnp.clip(1.0 + 0.1 * jax.random.normal(key_list[2], (MODEL_DIMENSION,), jnp.float32), 0.5, 1.5)
    query_weight = bell_draw(key_list[3], (MODEL_DIMENSION, QUERY_HEAD_COUNT * HEAD_DIMENSION), MODEL_DIMENSION ** -0.5, 0.15625, ((1, 2),))
    key_projection_weight = bell_draw(key_list[4], (MODEL_DIMENSION, KEY_VALUE_HEADS * HEAD_DIMENSION), MODEL_DIMENSION ** -0.5, 0.15625, ((1, 2),))
    value_projection_weight = bell_draw(key_list[5], (MODEL_DIMENSION, KEY_VALUE_HEADS * HEAD_DIMENSION), MODEL_DIMENSION ** -0.5, 0.15625, ((1, 2),))
    out_weight = bell_draw(key_list[6], (QUERY_HEAD_COUNT * HEAD_DIMENSION, MODEL_DIMENSION), (QUERY_HEAD_COUNT * HEAD_DIMENSION // 16) ** -0.5, 0.625, ((0, 2),))
    second_gain = jnp.clip(1.0 + 0.1 * jax.random.normal(key_list[7], (MODEL_DIMENSION,), jnp.float32), 0.5, 1.5)
    gate_weight = bell_draw(key_list[8], (EXPERTS, MODEL_DIMENSION, FF), MODEL_DIMENSION ** -0.5, 0.15625, ((2, 2),))
    up_weight = bell_draw(key_list[9], (EXPERTS, MODEL_DIMENSION, FF), MODEL_DIMENSION ** -0.5, 0.15625, ((2, 2),))
    down_weight = bell_draw(key_list[10], (EXPERTS, FF, MODEL_DIMENSION), (FF // 4) ** -0.5, 0.4375, ((1, 2),))
    segments = jnp.searchsorted(jnp.cumsum(uneven(key_list[11], SEGS, PACKED_TOKENS, DOC_MAX, 1)), jnp.arange(PACKED_TOKENS), side="right").astype(jnp.int32)
    live_mask = set_ends((jax.random.randint(key_list[12], (PACKED_TOKENS,), 0, 16) < 15).astype(jnp.int32), jax.random.fold_in(key_list[12], 1), 0, 1)
    routes = picks_of(key_list[13], PACKED_TOKENS, EXPERTS, TOP, 4096)
    gate_values = jnp.clip(0.2 + 0.3 * jax.random.uniform(key_list[14], (PACKED_TOKENS, TOP), jnp.float32) ** levels(key_list[14], (PACKED_TOKENS, TOP), ((0, 16),), -0.2, 0.2), 0.2, 0.5)
    return dict(tokens=tokens, cotangent=cotangent, first_gain=first_gain, query_weight=query_weight, key_projection_weight=key_projection_weight, value_projection_weight=value_projection_weight, out_weight=out_weight, second_gain=second_gain, gate_weight=gate_weight, up_weight=up_weight, down_weight=down_weight, segments=segments, live_mask=live_mask, routes=routes, gate_values=gate_values)


eps = 1e-06
rope_base = 1000000.0
masked_score = -1e+30
highest = lax.Precision.HIGHEST

@jax.custom_vjp
def reduced_precision(v):
    return lax.optimization_barrier(v.astype(jnp.bfloat16)).astype(jnp.float32)

@jax.custom_vjp
def reduced_precision_backward(v):
    return v

def low_keep(v):
    return (reduced_precision(v), None)

def low_pass(kept, grad):
    return (grad,)

def back_keep(v):
    return (v, None)

def back_low(kept, grad):
    return (reduced_precision(grad),)
reduced_precision.defvjp(low_keep, low_pass)
reduced_precision_backward.defvjp(back_keep, back_low)

def matrix_product(left, right):
    return jnp.dot(left, right, precision=highest)

def normalize(value, gain):
    return value * lax.rsqrt(lax.optimization_barrier(jnp.mean(value * value, axis=-1, keepdims=True)) + eps) * gain

def rope_tables(positions):
    half_size = HEAD_DIMENSION // 2
    frequency = rope_base ** (-2.0 * jnp.arange(half_size, dtype=jnp.float32) / HEAD_DIMENSION)
    angles = positions.astype(jnp.float32)[:, None] * frequency[None, :]
    return (jnp.cos(angles)[:, None, :], jnp.sin(angles)[:, None, :])

def rotate(value, cosine, sine_table):
    half_size = value.shape[-1] // 2
    first_half = value[..., :half_size]
    second_half = value[..., half_size:]
    return jnp.concatenate([first_half * cosine - second_half * sine_table, second_half * cosine + first_half * sine_table], axis=-1)

def route_tables(routes, live_rows, gate_rows):
    row_count = routes.shape[0]
    top_count = routes.shape[1]
    expert_ids = routes.reshape(-1)
    pair_live = jnp.repeat(live_rows, top_count)
    one_hot = (expert_ids[:, None] == jnp.arange(EXPERTS, dtype=jnp.int32)[None, :]).astype(jnp.int32) * pair_live[:, None]
    earlier = jnp.cumsum(one_hot, axis=0) - one_hot
    slot_rank = lax.optimization_barrier(jnp.sum(earlier * one_hot, axis=1))
    kept_pair = (pair_live == 1) & (slot_rank < CAP)
    slot_index = jnp.where(kept_pair, expert_ids * CAP + slot_rank, EXPERTS * CAP).astype(jnp.int32)
    pair_owner = jnp.repeat(jnp.arange(row_count, dtype=jnp.int32), top_count)
    pair_weight = gate_rows.reshape(-1) * kept_pair.astype(gate_rows.dtype)
    slot_token = jnp.zeros((EXPERTS * CAP + 1,), jnp.int32).at[slot_index].set(pair_owner)[:EXPERTS * CAP]
    slot_used = jnp.zeros((EXPERTS * CAP + 1,), jnp.int32).at[slot_index].set(1)[:EXPERTS * CAP]
    slot_gate = jnp.zeros((EXPERTS * CAP + 1,), gate_rows.dtype).at[slot_index].set(pair_weight)[:EXPERTS * CAP]
    return (slot_index, pair_weight, slot_token, slot_used, slot_gate)

def attention(query_token_rows, key_rows, value_token_rows, segments, live_mask):
    query_tile_block = min(1024, PACKED_TOKENS)
    key_span = min(PACKED_TOKENS, query_tile_block * ((DOC_MAX + query_tile_block - 2) // query_tile_block + 1))
    head_groups = QUERY_HEAD_COUNT // KEY_VALUE_HEADS
    score_scale = HEAD_DIMENSION ** (-0.5)

    def attend_block(block_id):
        query_offset = block_id * query_tile_block
        key_start = jnp.maximum(query_offset + query_tile_block - key_span, 0).astype(jnp.int32)
        query_portion = lax.dynamic_slice_in_dim(query_token_rows, query_offset, query_tile_block, 0).reshape(query_tile_block, KEY_VALUE_HEADS, head_groups, HEAD_DIMENSION)
        key_part = lax.dynamic_slice_in_dim(key_rows, key_start, key_span, 0)
        value_part = lax.dynamic_slice_in_dim(value_token_rows, key_start, key_span, 0)
        query_pos = query_offset + jnp.arange(query_tile_block, dtype=jnp.int32)
        key_pos = key_start + jnp.arange(key_span, dtype=jnp.int32)
        query_seg = lax.dynamic_slice_in_dim(segments, query_offset, query_tile_block, 0)
        key_seg = lax.dynamic_slice_in_dim(segments, key_start, key_span, 0)
        key_live = lax.dynamic_slice_in_dim(live_mask, key_start, key_span, 0)
        allowed = (key_pos[None, :] <= query_pos[:, None]) & (key_seg[None, :] == query_seg[:, None]) & ((key_live[None, :] == 1) | (key_pos[None, :] == query_pos[:, None]))
        scores = jnp.einsum('qcgd,kcd->cgqk', query_portion, key_part, precision=highest) * score_scale
        scores = reduced_precision_backward(jnp.where(allowed[None, None], scores, masked_score))
        probs = reduced_precision(jax.nn.softmax(scores, axis=-1))
        mixed = jnp.einsum('cgqk,kcd->qcgd', probs, value_part, precision=highest)
        return mixed.reshape(query_tile_block, QUERY_HEAD_COUNT * HEAD_DIMENSION)
    blocks = lax.map(jax.checkpoint(attend_block), jnp.arange(PACKED_TOKENS // query_tile_block, dtype=jnp.int32))
    return blocks.reshape(PACKED_TOKENS, QUERY_HEAD_COUNT * HEAD_DIMENSION)

def reference(tokens, cotangent, first_gain, query_weight, key_projection_weight, value_projection_weight, out_weight, second_gain, gate_weight, up_weight, down_weight, segments, live_mask, routes, gate_values):
    positions = jnp.arange(PACKED_TOKENS, dtype=jnp.int32)
    cosine, sine_table = rope_tables(positions)
    block_count = PACKED_TOKENS // TOK_DEV
    gate_rows = gate_values.astype(jnp.float32)

    def forward(tokens_float, gain_one, query_matrix, key_projected, value_projected, out_matrix, gain_two, gate_matrix, up_matrix, down_matrix):
        activation = reduced_precision(normalize(tokens_float, gain_one))
        query_raw = reduced_precision_backward(matrix_product(activation, query_matrix)).reshape(PACKED_TOKENS, QUERY_HEAD_COUNT, HEAD_DIMENSION)
        key_unrotated = reduced_precision_backward(matrix_product(activation, key_projected)).reshape(PACKED_TOKENS, KEY_VALUE_HEADS, HEAD_DIMENSION)
        value_token_rows = reduced_precision(reduced_precision_backward(matrix_product(activation, value_projected))).reshape(PACKED_TOKENS, KEY_VALUE_HEADS, HEAD_DIMENSION)
        query_token_rows = reduced_precision(rotate(query_raw, cosine, sine_table))
        key_rows = reduced_precision(rotate(key_unrotated, cosine, sine_table))
        mixed = reduced_precision(reduced_precision_backward(attention(query_token_rows, key_rows, value_token_rows, segments, live_mask)))
        residual = tokens_float + reduced_precision_backward(matrix_product(mixed, out_matrix))
        second = reduced_precision(normalize(residual, gain_two))

        def expert_block(inputs):
            normed, route_rows, live_rows, gate_part_rows = inputs
            slot_index, pair_weight, slot_token, slot_used, slot_gate = route_tables(route_rows, live_rows, gate_part_rows)
            slot_rows = (normed[slot_token] * slot_used[:, None].astype(normed.dtype)).reshape(EXPERTS, CAP, MODEL_DIMENSION)
            gate_part = reduced_precision_backward(jnp.einsum('ecd,edf->ecf', slot_rows, gate_matrix, precision=highest))
            up_part = reduced_precision_backward(jnp.einsum('ecd,edf->ecf', slot_rows, up_matrix, precision=highest))
            hidden = reduced_precision(jax.nn.gelu(gate_part, approximate=True) * up_part)
            result = reduced_precision_backward(jnp.einsum('ecf,efd->ecd', hidden, down_matrix, precision=highest))
            flat = jnp.concatenate([result.reshape(EXPERTS * CAP, MODEL_DIMENSION), jnp.zeros((1, MODEL_DIMENSION), jnp.float32)], axis=0)
            return lax.optimization_barrier(jnp.sum((flat[slot_index] * pair_weight[:, None]).reshape(TOK_DEV, TOP, MODEL_DIMENSION), axis=1))
        combined = lax.map(jax.checkpoint(expert_block), (second.reshape(block_count, TOK_DEV, MODEL_DIMENSION), routes.reshape(block_count, TOK_DEV, TOP), live_mask.reshape(block_count, TOK_DEV), gate_rows.reshape(block_count, TOK_DEV, TOP)))
        return residual + combined.reshape(PACKED_TOKENS, MODEL_DIMENSION)
    floats = (tokens.astype(jnp.float32), first_gain.astype(jnp.float32), query_weight.astype(jnp.float32), key_projection_weight.astype(jnp.float32), value_projection_weight.astype(jnp.float32), out_weight.astype(jnp.float32), second_gain.astype(jnp.float32), gate_weight.astype(jnp.float32), up_weight.astype(jnp.float32), down_weight.astype(jnp.float32))
    output, pullback = jax.vjp(forward, *floats)
    grads = pullback(cotangent.astype(jnp.float32))
    return (output.astype(jnp.bfloat16), grads[0], grads[1], grads[2], grads[3], grads[4], grads[5], grads[6], grads[7], grads[8], grads[9])
```

```python
import jax
import jax.numpy as jnp
from jax import lax
from jax.sharding import PartitionSpec as P

HEAD_DIMENSION = 128
TOP = 4
EXPERTS = 8
DOC_MAX = 2000
CAP = 640


eps = 1e-06
rope_base = 1000000.0
masked_score = -1e30


def shifted(shard, axis, by):
    size = lax.axis_size(axis)
    pairs = [(i, i + by) for i in range(size) if 0 <= i + by < size]
    return lax.ppermute(shard, axis, pairs)


def normalize(value):
    factor = lax.rsqrt(jnp.mean(value * value, axis=-1, keepdims=True) + eps)
    return (value * factor, factor)


def normalize_back(grad_normed, normed, factor):
    return factor * (grad_normed - normed * jnp.mean(grad_normed * normed, axis=-1, keepdims=True))


def rope_tables(positions):
    half_size = HEAD_DIMENSION // 2
    frequency = rope_base ** (-2.0 * jnp.arange(half_size, dtype=jnp.float32) / HEAD_DIMENSION)
    angles = positions.astype(jnp.float32)[:, None] * frequency[None, :]
    return (jnp.cos(angles)[:, None, :], jnp.sin(angles)[:, None, :])


def rotate(value, cosine, sine_table):
    half_size = value.shape[-1] // 2
    first_half = value[..., :half_size]
    second_half = value[..., half_size:]
    return jnp.concatenate(
        [
            first_half * cosine - second_half * sine_table,
            second_half * cosine + first_half * sine_table,
        ],
        axis=-1,
    )


def rotate_back(grad, cosine, sine_table):
    half_size = grad.shape[-1] // 2
    first_half = grad[..., :half_size]
    second_half = grad[..., half_size:]
    return jnp.concatenate(
        [
            first_half * cosine + second_half * sine_table,
            second_half * cosine - first_half * sine_table,
        ],
        axis=-1,
    )


def smooth_gate(inner):
    return jax.nn.gelu(inner, approximate=True)


def swap_sum(part):
    low = part.astype(jnp.bfloat16)
    other = lax.ppermute(low, "ws", [(0, 1), (1, 0)])
    return low.astype(jnp.float32) + other.astype(jnp.float32)


def halve(part, bit, axis):
    size = lax.axis_size("ctx")
    mine = (lax.axis_index("ctx") >> bit) & 1
    send = lax.dynamic_index_in_dim(part, 1 - mine, axis, keepdims=False)
    keep = lax.dynamic_index_in_dim(part, mine, axis, keepdims=False)
    arrived = lax.ppermute(send, "ctx", [(i, i ^ (1 << bit)) for i in range(size)])
    return keep.astype(jnp.float32) + arrived.astype(jnp.float32)


def scatter_sum(part, order):
    size = lax.axis_size("ctx")
    bits = size.bit_length() - 1
    rows, columns = part.shape
    value = part.astype(jnp.bfloat16).reshape((2,) * bits + (rows // size, columns))
    left = list(range(bits - 1, -1, -1))
    for step, bit in enumerate(order):
        axis = left.index(bit)
        left.remove(bit)
        value = halve(value, bit, axis)
        if step < bits - 1:
            value = value.astype(jnp.bfloat16)
    return value


def orders(bits):
    low = list(range(bits))
    return (low, [1, 0] + low[2:], [2, 0, 1] + low[3:])


def keep_same(carried):
    return carried


def gate_table(routes, live_rows, gate_rows):
    chosen = routes[:, :, None] == jnp.arange(EXPERTS, dtype=jnp.int32)[None, None, :]
    one_hot = jnp.any(chosen, axis=1).astype(jnp.int32) * live_rows[:, None]
    rank = jnp.cumsum(one_hot, axis=0) - one_hot
    kept = (one_hot == 1) & (rank < CAP)
    gates = jnp.sum(jnp.where(chosen, gate_rows[:, :, None], 0.0), axis=1)
    return jnp.where(kept, gates, 0.0)


def body(
    tokens,
    cotangent,
    first_gain,
    query_weight,
    key_projection_weight,
    value_projection_weight,
    out_weight,
    second_gain,
    gate_weight,
    up_weight,
    down_weight,
    segments,
    live_mask,
    routes,
    gate_values,
):
    row_count = tokens.shape[0]
    model_width = tokens.shape[1]
    total_rows = segments.shape[0]
    key_heads = key_projection_weight.shape[1] // HEAD_DIMENSION
    query_heads = query_weight.shape[1] // HEAD_DIMENSION
    head_groups = query_heads // key_heads
    key_width = key_heads * HEAD_DIMENSION
    score_scale = HEAD_DIMENSION ** (-0.5)
    devices = lax.axis_size("ctx")
    cycle_index = lax.axis_index("ctx")
    first_row = cycle_index * row_count
    query_pos = first_row + jnp.arange(row_count, dtype=jnp.int32)
    query_seg = lax.dynamic_slice_in_dim(segments, first_row, row_count, 0)
    own_live = lax.dynamic_slice_in_dim(live_mask, first_row, row_count, 0)
    cosine, sine_table = rope_tables(query_pos)
    tokens_float = tokens.astype(jnp.float32)
    normed_one, factor_one = normalize(tokens_float)
    activation = (normed_one * first_gain).astype(jnp.bfloat16)
    query_raw = jnp.dot(activation, query_weight, preferred_element_type=jnp.float32).reshape(
        row_count, query_heads, HEAD_DIMENSION
    )
    queries = (
        rotate(query_raw, cosine, sine_table)
        .astype(jnp.bfloat16)
        .reshape(row_count, key_heads, head_groups, HEAD_DIMENSION)
    )
    key_unrotated = jnp.dot(
        activation, key_projection_weight, preferred_element_type=jnp.float32
    ).reshape(row_count, key_heads, HEAD_DIMENSION)
    key_rows = rotate(key_unrotated, cosine, sine_table).astype(jnp.bfloat16)
    value_token_rows = jnp.dot(
        activation, value_projection_weight, preferred_element_type=jnp.float32
    ).astype(jnp.bfloat16)
    own_block = jnp.concatenate([key_rows.reshape(row_count, key_width), value_token_rows], axis=1)
    reach_blocks = min(devices, (DOC_MAX + row_count - 2) // row_count + 1)

    key_blocks = jnp.stack([own_block] + [shifted(own_block, "ctx", by) for by in range(1, reach_blocks)])
    own_slot = 0

    def block_start(block_id):
        return (cycle_index - block_id) * row_count

    def useful(block_id):
        start = block_start(block_id)
        last_seg = segments[jnp.clip(start + row_count - 1, 0, total_rows - 1)]
        return (start >= 0) & (start <= first_row + row_count - 1) & (last_seg >= query_seg[0])

    def block_scores(block_id):
        start = block_start(block_id)
        safe_start = jnp.clip(start, 0, total_rows - row_count)
        key_seg = lax.dynamic_slice_in_dim(segments, safe_start, row_count, 0)
        key_live = lax.dynamic_slice_in_dim(live_mask, safe_start, row_count, 0)
        key_pos = start + jnp.arange(row_count, dtype=jnp.int32)
        stacked = key_blocks[block_id]
        key_part = stacked[:, :key_width].reshape(row_count, key_heads, HEAD_DIMENSION)
        value_part = stacked[:, key_width:].reshape(row_count, key_heads, HEAD_DIMENSION)
        allowed = (
            (key_pos[None, :] >= 0)
            & (key_pos[None, :] <= query_pos[:, None])
            & (key_seg[None, :] == query_seg[:, None])
            & ((key_live[None, :] == 1) | (key_pos[None, :] == query_pos[:, None]))
        )
        raw_scores = (
            jnp.einsum("qcgd,kcd->cgqk", queries, key_part, preferred_element_type=jnp.float32)
            * score_scale
        )
        return (jnp.where(allowed[None, None], raw_scores, masked_score), key_part, value_part)

    first_scores, spare_keys, spare_values = block_scores(own_slot)
    row_max = jnp.max(first_scores, axis=-1)
    row_sum = jnp.sum(jnp.exp(first_scores - row_max[..., None]), axis=-1)

    def stats_step(running, block_id):

        def stats_update(carried):
            old_max, old_sum = carried
            scores, unused_keys, unused_values = block_scores(block_id)
            new_max = jnp.maximum(old_max, jnp.max(scores, axis=-1))
            new_sum = old_sum * jnp.exp(old_max - new_max) + jnp.sum(
                jnp.exp(scores - new_max[..., None]), axis=-1
            )
            return (new_max, new_sum)

        return (
            lax.cond(useful(block_id) & (block_id != own_slot), stats_update, keep_same, running),
            None,
        )

    block_ids = jnp.arange(reach_blocks, dtype=jnp.int32)
    (row_max, row_sum), spare_stats = lax.scan(stats_step, (row_max, row_sum), block_ids)
    log_total = row_max + jnp.log(row_sum)

    def mix_step(mixed_sum, block_id):

        def mix_update(carried):
            scores, key_part, value_part = block_scores(block_id)
            weights = jnp.exp(scores - log_total[..., None]).astype(jnp.bfloat16)
            return carried + jnp.einsum(
                "cgqk,kcd->cgqd", weights, value_part, preferred_element_type=jnp.float32
            )

        return (lax.cond(useful(block_id), mix_update, keep_same, mixed_sum), None)

    attn_heads, spare_mix = lax.scan(
        mix_step,
        jnp.zeros((key_heads, head_groups, row_count, HEAD_DIMENSION), jnp.float32),
        block_ids,
    )
    attn_low = attn_heads.astype(jnp.bfloat16)
    out_heads = out_weight.reshape(key_heads, head_groups, HEAD_DIMENSION, model_width)
    attn_part = jnp.einsum("cgqd,cgde->qe", attn_low, out_heads, preferred_element_type=jnp.float32)
    residual = tokens_float + swap_sum(attn_part)
    normed_two, factor_two = normalize(residual)
    act_two = (normed_two * second_gain).astype(jnp.bfloat16)
    gates = gate_table(routes, own_live, gate_values)[:, :, None]
    gate_part = jnp.einsum("td,edf->tef", act_two, gate_weight, preferred_element_type=jnp.float32)
    up_part = jnp.einsum("td,edf->tef", act_two, up_weight, preferred_element_type=jnp.float32)
    back_part = jnp.einsum("td,efd->tef", cotangent, down_weight, preferred_element_type=jnp.float32)
    activated, gelu_back = jax.vjp(smooth_gate, gate_part)
    hidden = (activated * up_part * gates).astype(jnp.bfloat16)
    grad_hidden = back_part * gates
    grad_gate_part = gelu_back(grad_hidden * up_part)[0].astype(jnp.bfloat16)
    grad_up_part = (grad_hidden * activated).astype(jnp.bfloat16)
    flat_width = EXPERTS * hidden.shape[2]
    flat_hidden = hidden.reshape(row_count, flat_width)
    flat_gate = grad_gate_part.reshape(row_count, flat_width)
    flat_up = grad_up_part.reshape(row_count, flat_width)
    grad_gate = jnp.einsum("td,tf->df", act_two, flat_gate, preferred_element_type=jnp.float32)
    grad_up = jnp.einsum("td,tf->df", act_two, flat_up, preferred_element_type=jnp.float32)
    grad_down = jnp.einsum("td,tf->df", cotangent, flat_hidden, preferred_element_type=jnp.float32)
    combined = jnp.einsum("tef,efd->td", hidden, down_weight, preferred_element_type=jnp.float32)
    output = residual + swap_sum(combined)
    grad_out = cotangent.astype(jnp.float32)
    grad_act_two = jnp.einsum(
        "tef,edf->td", grad_gate_part, gate_weight, preferred_element_type=jnp.float32
    ) + jnp.einsum("tef,edf->td", grad_up_part, up_weight, preferred_element_type=jnp.float32)
    grad_act_two = swap_sum(grad_act_two)
    grad_second = jnp.sum(grad_act_two * normed_two, axis=0)
    grad_residual = grad_out + normalize_back(grad_act_two * second_gain, normed_two, factor_two)
    residual_low = grad_residual.astype(jnp.bfloat16)
    grad_out_weight = jnp.einsum(
        "cgqd,qe->ecgd", attn_low, residual_low, preferred_element_type=jnp.float32
    ).reshape(model_width, query_heads * HEAD_DIMENSION)
    grad_heads = jnp.einsum(
        "qe,cgde->cgqd", residual_low, out_heads, preferred_element_type=jnp.float32
    ).astype(jnp.bfloat16)
    row_delta = jnp.sum(grad_heads.astype(jnp.float32) * attn_heads, axis=-1)

    def grad_step(grad_query, block_id):

        def grad_update(carried):
            scores, key_part, value_part = block_scores(block_id)
            weights = jnp.exp(scores - log_total[..., None])
            grad_weights = jnp.einsum(
                "cgqd,kcd->cgqk", grad_heads, value_part, preferred_element_type=jnp.float32
            )
            grad_scores = (weights * (grad_weights - row_delta[..., None])).astype(jnp.bfloat16)
            new_query = (
                carried
                + jnp.einsum(
                    "cgqk,kcd->qcgd", grad_scores, key_part, preferred_element_type=jnp.float32
                )
                * score_scale
            )
            grad_key_part = (
                jnp.einsum(
                    "cgqk,qcgd->kcd", grad_scores, queries, preferred_element_type=jnp.float32
                )
                * score_scale
            )
            grad_value_part = jnp.einsum(
                "cgqk,cgqd->kcd",
                weights.astype(jnp.bfloat16),
                grad_heads,
                preferred_element_type=jnp.float32,
            )
            joined = jnp.concatenate(
                [
                    grad_key_part.reshape(row_count, key_width),
                    grad_value_part.reshape(row_count, key_width),
                ],
                axis=1,
            )
            return (new_query, joined)

        def skip(carried):
            return (carried, jnp.zeros((row_count, 2 * key_width), jnp.float32))

        return lax.cond(useful(block_id), grad_update, skip, grad_query)

    grad_query, pieces = lax.scan(
        grad_step,
        jnp.zeros((row_count, key_heads, head_groups, HEAD_DIMENSION), jnp.float32),
        block_ids,
    )

    block_grad = pieces[0]
    for by in range(1, reach_blocks):
        block_grad = block_grad + shifted(pieces[by].astype(jnp.bfloat16), "ctx", -by).astype(jnp.float32)
    grad_key_rows = (
        rotate_back(
            block_grad[:, :key_width].reshape(row_count, key_heads, HEAD_DIMENSION),
            cosine,
            sine_table,
        )
        .astype(jnp.bfloat16)
        .reshape(row_count, key_width)
    )
    grad_value_rows = block_grad[:, key_width:].astype(jnp.bfloat16)
    grad_query_rows = (
        rotate_back(grad_query.reshape(row_count, query_heads, HEAD_DIMENSION), cosine, sine_table)
        .astype(jnp.bfloat16)
        .reshape(row_count, query_heads * HEAD_DIMENSION)
    )
    grad_query_weight = jnp.einsum(
        "td,tf->df", activation, grad_query_rows, preferred_element_type=jnp.float32
    )
    grad_key_weight = jnp.einsum(
        "td,tf->df", activation, grad_key_rows, preferred_element_type=jnp.float32
    )
    grad_value_weight = jnp.einsum(
        "td,tf->df", activation, grad_value_rows, preferred_element_type=jnp.float32
    )
    grad_act = jnp.einsum(
        "tf,df->td", grad_query_rows, query_weight, preferred_element_type=jnp.float32
    )
    grad_act = grad_act + jnp.einsum(
        "tf,df->td", grad_key_rows, key_projection_weight, preferred_element_type=jnp.float32
    )
    grad_act = grad_act + jnp.einsum(
        "tf,df->td", grad_value_rows, value_projection_weight, preferred_element_type=jnp.float32
    )
    grad_act = swap_sum(grad_act)
    grad_first = jnp.sum(grad_act * normed_one, axis=0)
    grad_tokens = grad_residual + normalize_back(grad_act * first_gain, normed_one, factor_one)
    bits = devices.bit_length() - 1
    one, two, three = orders(bits)
    own_gate = scatter_sum(grad_gate, one)
    own_up = scatter_sum(grad_up, two)
    own_down = scatter_sum(grad_down, three)
    own_out = scatter_sum(grad_out_weight, three)
    pad = jnp.zeros((model_width, HEAD_DIMENSION - 2), jnp.float32)
    last = jnp.concatenate(
        [grad_query_weight, grad_key_weight, grad_value_weight, grad_first[:, None], grad_second[:, None], pad],
        axis=1,
    )
    own_last = scatter_sum(last, one)
    query_width = query_weight.shape[1]
    gain_at = query_width + 2 * key_width
    own_rows = own_last.shape[0]
    return (
        output.astype(jnp.bfloat16),
        grad_tokens,
        own_last[:, gain_at],
        own_last[:, :query_width],
        own_last[:, query_width : query_width + key_width],
        own_last[:, query_width + key_width : gain_at],
        own_out.T,
        own_last[:, gain_at + 1],
        own_gate.reshape(own_rows, EXPERTS, -1).transpose(1, 0, 2),
        own_up.reshape(own_rows, EXPERTS, -1).transpose(1, 0, 2),
        own_down.reshape(own_rows, EXPERTS, -1).transpose(1, 2, 0),
    )


def solution(mesh):
    return jax.shard_map(
        body,
        mesh=mesh,
        in_specs=(
            P("ctx", None),
            P("ctx", None),
            P(),
            P(None, "ws"),
            P(None, "ws"),
            P(None, "ws"),
            P("ws", None),
            P(),
            P(None, None, "ws"),
            P(None, None, "ws"),
            P(None, "ws", None),
            P(),
            P(),
            P("ctx", None),
            P("ctx", None),
        ),
        out_specs=(
            P("ctx", None),
            P("ctx", None),
            P("ctx"),
            P("ctx", "ws"),
            P("ctx", "ws"),
            P("ctx", "ws"),
            P("ws", "ctx"),
            P("ctx"),
            P(None, "ctx", "ws"),
            P(None, "ctx", "ws"),
            P(None, "ws", "ctx"),
        ),
        check_vma=False,
    )
```

```python
import jax
import jax.numpy as jnp
from jax import lax
from jax.experimental import pallas as pl
from jax.experimental.pallas import tpu as pltpu
from jax.sharding import PartitionSpec as P

HEAD_DIMENSION = 128
EXPERTS = 8
DOC_MAX = 2000
CAP = 640
LANES = 128

eps = 1e-06
rope_base = 1000000.0
masked_score = -1e30
far_position = 1 << 30
log2_e = 1.4426950408889634
tanh_scale = 0.7978845608028654
tanh_cubic = 0.044715

low_type = jnp.bfloat16
sum_type = jnp.float32
any_space = pl.BlockSpec(memory_space=pl.ANY)


def dot(left, right):
    return jnp.dot(left, right, preferred_element_type=sum_type)


def dot_rows(left, right):
    return lax.dot_general(left, right, (((1,), (1,)), ((), ())), preferred_element_type=sum_type)


def dot_columns(left, right):
    return lax.dot_general(left, right, (((0,), (0,)), ((), ())), preferred_element_type=sum_type)


def whole(shape):
    return pl.BlockSpec(shape, lambda *index: (0,) * len(shape))


def by_rows(block, shape):
    return pl.BlockSpec((block,) + shape[1:], lambda row, *rest: (row,) + (0,) * (len(shape) - 1))


def like(shape, kind=low_type):
    return jax.ShapeDtypeStruct(shape, kind)


def settings(megabytes):
    return pltpu.CompilerParams(vmem_limit_bytes=megabytes * 2**20)


def normalize(value):
    factor = lax.rsqrt(jnp.mean(value * value, axis=-1, keepdims=True) + eps)
    return value * factor, factor


def normalize_back(grad_normed, normed, factor):
    return factor * (grad_normed - normed * jnp.mean(grad_normed * normed, axis=-1, keepdims=True))


def key_value_kernel(token_ref, gain_ref, key_ref, value_ref, cos_ref, sin_ref, act_ref, out_ref):
    normed, factor = normalize(token_ref[...].astype(sum_type))
    act = (normed * gain_ref[...]).astype(low_type)
    act_ref[...] = act
    keys = dot(act, key_ref[...])
    width = keys.shape[1]
    for head in range(width // HEAD_DIMENSION):
        at = slice(head * HEAD_DIMENSION, (head + 1) * HEAD_DIMENSION)
        part = keys[:, at]
        turned = pltpu.roll(part, HEAD_DIMENSION // 2, 1)
        out_ref[:, at] = (part * cos_ref[...] + turned * sin_ref[...]).astype(low_type)
    out_ref[:, width:] = dot(act, value_ref[...]).astype(low_type)


def project_keys(tokens, gain, key_weight, value_weight, cosine, sine, block=256):
    rows, width = tokens.shape
    joined = key_weight.shape[1] + value_weight.shape[1]
    return pl.pallas_call(
        key_value_kernel,
        grid=(rows // block,),
        in_specs=[
            by_rows(block, tokens.shape),
            whole((1, width)),
            whole(key_weight.shape),
            whole(value_weight.shape),
            by_rows(block, cosine.shape),
            by_rows(block, sine.shape),
        ],
        out_specs=[by_rows(block, (rows, width)), by_rows(block, (rows, joined))],
        out_shape=[like((rows, width)), like((rows, joined))],
        compiler_params=settings(32),
        name="norm_keys_values",
    )(tokens, gain, key_weight, value_weight, cosine, sine)


def query_kernel(act_ref, weight_ref, cos_ref, sin_ref, out_ref):
    raw = dot(act_ref[...], weight_ref[...])
    half = HEAD_DIMENSION // 2
    cosine, sine = cos_ref[...], sin_ref[...]
    for head in range(out_ref.shape[0]):
        part = raw[:, head * HEAD_DIMENSION : (head + 1) * HEAD_DIMENSION].T
        one, two = part[:half], part[half:]
        out_ref[head, :half] = (one * cosine - two * sine).astype(low_type)
        out_ref[head, half:] = (two * cosine + one * sine).astype(low_type)


def project_queries(act, weight, cosine, sine, block=256):
    rows, width = act.shape
    heads = weight.shape[1] // HEAD_DIMENSION
    half = HEAD_DIMENSION // 2
    columns = pl.BlockSpec((half, block), lambda row: (0, row))
    return pl.pallas_call(
        query_kernel,
        grid=(rows // block,),
        in_specs=[by_rows(block, act.shape), whole(weight.shape), columns, columns],
        out_specs=pl.BlockSpec((heads, HEAD_DIMENSION, block), lambda row: (0, 0, row)),
        out_shape=like((heads, HEAD_DIMENSION, rows)),
        compiler_params=settings(32),
        name="queries",
    )(act, weight, cosine, sine)


def repeat_lanes(block, times):
    return jnp.concatenate([block] * times, axis=1) if times > 1 else block


def join_heads(ref):
    return jnp.concatenate([ref[head] for head in range(ref.shape[0])], axis=1)


def allowed_pairs(place_ref, rows, low, high, start, own_at, own):
    size, count = rows.size, low.shape[1]
    place = repeat_lanes(place_ref[rows, :], count // LANES)
    allowed = (place >= low) & (place <= high)
    if own:
        position = start - own_at + lax.broadcasted_iota(jnp.int32, (size, count), 0)
        allowed = allowed | (position == high)
    return allowed


def over_keys(first_ref, step, own_at, query_block, key_block):
    tile = pl.program_id(0)
    own_first = (own_at + tile * query_block) // key_block
    for extra in range(max(1, query_block // key_block)):
        step(own_first + extra, True)

    def loop(index, carried):
        step(index, False)
        return carried

    lax.fori_loop(first_ref[tile], own_first, loop, 0)


def mix_kernel(
    first_ref, query_ref, key_ref, value_ref, place_ref, low_ref, out_ref, mixed_ref, log_ref,
    max_s, sum_s, mix_s, *, key_block, own_at, scale,
):
    heads, query_block = query_ref.shape[0], query_ref.shape[2]
    count = heads * query_block
    tile = pl.program_id(0)
    queries = join_heads(query_ref)
    low = repeat_lanes(low_ref[...], heads)
    high = repeat_lanes(
        tile * query_block + lax.broadcasted_iota(jnp.int32, (1, query_block), 1), heads
    )
    max_s[...] = jnp.full(max_s.shape, masked_score, sum_type)
    sum_s[...] = jnp.zeros(sum_s.shape, sum_type)
    mix_s[...] = jnp.zeros(mix_s.shape, sum_type)

    def step(index, own):
        start = pl.multiple_of(index * key_block, key_block)
        rows = pl.ds(start, key_block)
        raw = dot(key_ref[rows, :], queries)
        allowed = allowed_pairs(place_ref, rows, low, high, start, own_at, own)
        scores = jnp.where(allowed, raw * (scale * log2_e), masked_score)
        old = max_s[...]
        new = jnp.maximum(old, jnp.max(scores, axis=0, keepdims=True))
        weights = jnp.exp2(scores - new)
        fade = jnp.exp2(old - new)
        sum_s[...] = sum_s[...] * fade + jnp.sum(weights, axis=0, keepdims=True)
        max_s[...] = new
        mix_s[...] = mix_s[...] * fade + dot(value_ref[:, rows], weights.astype(low_type))

    over_keys(first_ref, step, own_at, query_block, key_block)
    total = sum_s[...]
    mixed = mix_s[...] * (1.0 / total)
    logs = max_s[...] + jnp.log2(total)
    for head in range(heads):
        at = slice(head * query_block, (head + 1) * query_block)
        out_ref[head] = mixed[:, at]
        mixed_ref[:, head * HEAD_DIMENSION : (head + 1) * HEAD_DIMENSION] = mixed[:, at].T.astype(
            low_type
        )
        log_ref[head] = logs[:, at]


def tile_of(query_block):
    def column(shape):
        return pl.BlockSpec(
            shape[:-1] + (query_block,), lambda tile, *rest: (0,) * (len(shape) - 1) + (tile,)
        )

    return column


def attend(first, queries, keys, values_turned, place, low, query_block, key_block):
    heads, depth, rows = queries.shape
    column = tile_of(query_block)
    count = heads * query_block
    return pl.pallas_call(
        lambda *refs: mix_kernel(
            *refs, key_block=key_block, own_at=keys.shape[0] - rows, scale=depth**-0.5
        ),
        grid_spec=pltpu.PrefetchScalarGridSpec(
            num_scalar_prefetch=1,
            grid=(rows // query_block,),
            in_specs=[
                column(queries.shape),
                whole(keys.shape),
                whole(values_turned.shape),
                whole(place.shape),
                column(low.shape),
            ],
            out_specs=[
                column(queries.shape),
                by_rows(query_block, (rows, heads * depth)),
                column((heads, 1, rows)),
            ],
            scratch_shapes=[
                pltpu.VMEM((1, count), sum_type),
                pltpu.VMEM((1, count), sum_type),
                pltpu.VMEM((depth, count), sum_type),
            ],
        ),
        out_shape=[
            like(queries.shape, sum_type),
            like((rows, heads * depth)),
            like((heads, 1, rows), sum_type),
        ],
        compiler_params=settings(48),
        name="attention",
    )(first, queries, keys, values_turned, place, low)


def mix_back_kernel(
    first_ref, query_ref, key_ref, key_turned_ref, value_ref, place_ref, low_ref, mixed_ref,
    grad_ref, log_ref, cos_ref, sin_ref, out_ref, far_ref, own_ref, query_s, key_s, value_s,
    *, key_block, own_at, scale, tiles,
):
    heads, depth, query_block = query_ref.shape
    tile = pl.program_id(0)
    queries, grads, logs = join_heads(query_ref), join_heads(grad_ref), join_heads(log_ref)
    delta = jnp.sum(grads.astype(sum_type) * join_heads(mixed_ref), axis=0, keepdims=True)
    low = repeat_lanes(low_ref[...], heads)
    high = repeat_lanes(
        tile * query_block + lax.broadcasted_iota(jnp.int32, (1, query_block), 1), heads
    )

    @pl.when(tile == 0)
    def clear():
        key_s[...] = jnp.zeros(key_s.shape, sum_type)
        value_s[...] = jnp.zeros(value_s.shape, sum_type)

    query_s[...] = jnp.zeros(query_s.shape, sum_type)

    def step(index, own):
        start = pl.multiple_of(index * key_block, key_block)
        rows = pl.ds(start, key_block)
        raw = dot(key_ref[rows, :], queries)
        allowed = allowed_pairs(place_ref, rows, low, high, start, own_at, own)
        weights = jnp.exp2(jnp.where(allowed, raw * (scale * log2_e), masked_score) - logs)
        grad_weights = dot(value_ref[rows, :], grads)
        grad_scores = (weights * (grad_weights - delta)).astype(low_type)
        value_s[rows, :] += dot_rows(weights.astype(low_type), grads)
        key_s[rows, :] += dot_rows(grad_scores, queries)
        query_s[...] += dot(key_turned_ref[:, rows], grad_scores)

    over_keys(first_ref, step, own_at, query_block, key_block)
    half = depth // 2
    cosine, sine = repeat_lanes(cos_ref[...], heads), repeat_lanes(sin_ref[...], heads)
    grad_query = query_s[...] * scale
    one, two = grad_query[:half], grad_query[half:]
    turned = jnp.concatenate([one * cosine + two * sine, two * cosine - one * sine], axis=0)
    for head in range(heads):
        part = turned[:, head * query_block : (head + 1) * query_block]
        out_ref[:, head * depth : (head + 1) * depth] = part.T.astype(low_type)

    @pl.when(tile == tiles - 1)
    def finish():
        far_ref[:, :depth] = (key_s[:own_at, :] * scale).astype(low_type)
        far_ref[:, depth:] = value_s[:own_at, :].astype(low_type)
        own_ref[:, :depth] = key_s[own_at:, :] * scale
        own_ref[:, depth:] = value_s[own_at:, :]


def attend_back(
    first, queries, keys, keys_turned, values, place, low, mixed, grads, logs, cosine, sine,
    query_block, key_block,
):
    heads, depth, rows = queries.shape
    key_rows = keys.shape[0]
    column = tile_of(query_block)
    return pl.pallas_call(
        lambda *refs: mix_back_kernel(
            *refs,
            key_block=key_block,
            own_at=key_rows - rows,
            scale=depth**-0.5,
            tiles=rows // query_block,
        ),
        grid_spec=pltpu.PrefetchScalarGridSpec(
            num_scalar_prefetch=1,
            grid=(rows // query_block,),
            in_specs=[
                column(queries.shape),
                whole(keys.shape),
                whole(keys_turned.shape),
                whole(values.shape),
                whole(place.shape),
                column(low.shape),
                column(mixed.shape),
                column(grads.shape),
                column(logs.shape),
                column(cosine.shape),
                column(sine.shape),
            ],
            out_specs=[
                by_rows(query_block, (rows, heads * depth)),
                whole((key_rows - rows, 2 * depth)),
                whole((rows, 2 * depth)),
            ],
            scratch_shapes=[
                pltpu.VMEM((depth, heads * query_block), sum_type),
                pltpu.VMEM((key_rows, depth), sum_type),
                pltpu.VMEM((key_rows, depth), sum_type),
            ],
        ),
        out_shape=[
            like((rows, heads * depth)),
            like((key_rows - rows, 2 * depth)),
            like((rows, 2 * depth), sum_type),
        ],
        compiler_params=settings(56),
        name="attention_back",
    )(first, queries, keys, keys_turned, values, place, low, mixed, grads, logs, cosine, sine)


def product_kernel(left_ref, right_ref, out_ref):
    out_ref[...] = dot(left_ref[...], right_ref[...]).astype(out_ref.dtype)


def product(left, right, name, block=256):
    rows = left.shape[0]
    out = (rows, right.shape[1])
    return pl.pallas_call(
        product_kernel,
        grid=(rows // block,),
        in_specs=[by_rows(block, left.shape), whole(right.shape)],
        out_specs=by_rows(block, out),
        out_shape=like(out),
        compiler_params=settings(32),
        name=name,
    )(left, right)


def second_norm_kernel(token_ref, own_ref, other_ref, gain_ref, sum_ref, act_ref):
    mixed = own_ref[...].astype(sum_type) + other_ref[...].astype(sum_type)
    residual = token_ref[...].astype(sum_type) + mixed
    sum_ref[...] = residual
    act_ref[...] = (normalize(residual)[0] * gain_ref[...]).astype(low_type)


def second_norm(tokens, own, other, gain, block=256):
    rows = by_rows(block, tokens.shape)
    return pl.pallas_call(
        second_norm_kernel,
        grid=(tokens.shape[0] // block,),
        in_specs=[rows, rows, rows, whole(gain.shape)],
        out_specs=[rows, rows],
        out_shape=[like(tokens.shape, sum_type), like(tokens.shape)],
        compiler_params=settings(32),
        name="residual_norm",
    )(tokens, own, other, gain)


def second_back_kernel(
    own_ref, other_ref, sum_ref, grad_ref, gain_ref, weight_ref, total_ref, low_ref, heads_ref
):
    grad_act = own_ref[...].astype(sum_type) + other_ref[...].astype(sum_type)
    normed, factor = normalize(sum_ref[...])

    total = grad_ref[...].astype(sum_type) + normalize_back(
        grad_act * gain_ref[...], normed, factor
    )
    total_ref[...] = total
    low = total.astype(low_type)
    low_ref[...] = low
    turned = dot_rows(weight_ref[...], low).astype(low_type)
    heads_ref[...] = turned.reshape(heads_ref.shape)


def second_back(own, other, residual, cotangent, gain, out_weight, block=256):
    rows = by_rows(block, own.shape)
    heads = out_weight.shape[0] // HEAD_DIMENSION
    shape = (heads, HEAD_DIMENSION, own.shape[0])
    return pl.pallas_call(
        second_back_kernel,
        grid=(own.shape[0] // block,),
        in_specs=[rows, rows, rows, rows, whole(gain.shape), whole(out_weight.shape)],
        out_specs=[rows, rows, tile_of(block)(shape)],
        out_shape=[like(own.shape, sum_type), like(own.shape), like(shape)],
        compiler_params=settings(40),
        name="residual_back",
    )(own, other, residual, cotangent, gain, out_weight)


def act_back_kernel(query_ref, pair_ref, query_weight_ref, key_weight_ref, value_weight_ref, out_ref):
    width = key_weight_ref.shape[1]
    total = dot_rows(query_ref[...], query_weight_ref[...])
    total += dot_rows(pair_ref[:, :width], key_weight_ref[...])
    total += dot_rows(pair_ref[:, width:], value_weight_ref[...])
    out_ref[...] = total.astype(low_type)


def act_back(queries, pairs, query_weight, key_weight, value_weight, block=256):
    out = (queries.shape[0], query_weight.shape[0])
    return pl.pallas_call(
        act_back_kernel,
        grid=(out[0] // block,),
        in_specs=[
            by_rows(block, queries.shape),
            by_rows(block, pairs.shape),
            whole(query_weight.shape),
            whole(key_weight.shape),
            whole(value_weight.shape),
        ],
        out_specs=by_rows(block, out),
        out_shape=like(out),
        compiler_params=settings(32),
        name="activation_back",
    )(queries, pairs, query_weight, key_weight, value_weight)


def first_back_kernel(own_ref, other_ref, token_ref, total_ref, gain_ref, out_ref):
    grad_act = own_ref[...].astype(sum_type) + other_ref[...].astype(sum_type)
    normed, factor = normalize(token_ref[...].astype(sum_type))
    out_ref[...] = total_ref[...] + normalize_back(grad_act * gain_ref[...], normed, factor)


def first_back(own, other, tokens, total, gain, block=256):
    rows = by_rows(block, own.shape)
    return pl.pallas_call(
        first_back_kernel,
        grid=(own.shape[0] // block,),
        in_specs=[rows, rows, rows, rows, whole(gain.shape)],
        out_specs=rows,
        out_shape=like(own.shape, sum_type),
        compiler_params=settings(32),
        name="norm_back",
    )(own, other, tokens, total, gain)


def slot_of(rest, bit, first):
    return ((rest >> first) << (first + 1)) | (bit << first) | (rest & ((1 << first) - 1))


def place_slots(me, total_ref, send_ref, keep_ref, first, columns=slice(None)):
    for rest in range(send_ref.shape[0]):
        for bit, ref in ((1, send_ref), (0, keep_ref)):
            ref[rest] = total_ref[slot_of(rest, bit, first) ^ me, :, columns].astype(low_type)


def grad_kernel(me_ref, left_ref, right_ref, *refs, firsts):
    total_s = refs[-1]
    total_s[...] = dot_columns(left_ref[...], right_ref[...]).reshape(total_s.shape)
    width = total_s.shape[2] // len(firsts)
    for index, first in enumerate(firsts):
        columns = slice(index * width, (index + 1) * width)
        place_slots(me_ref[0], total_s, refs[2 * index], refs[2 * index + 1], first, columns)


def grad_parts(me, left, right, devices, firsts, name):
    rows, width = left.shape[1] // devices, right.shape[1]
    half = (devices // 2, rows, width // len(firsts))
    return pl.pallas_call(
        lambda *refs: grad_kernel(*refs, firsts=firsts),
        grid_spec=pltpu.PrefetchScalarGridSpec(
            num_scalar_prefetch=1,
            grid=(1,),
            in_specs=[whole(left.shape), whole(right.shape)],
            out_specs=[whole(half)] * (2 * len(firsts)),
            scratch_shapes=[pltpu.VMEM((devices, rows, width), sum_type)],
        ),
        out_shape=[like(half)] * (2 * len(firsts)),
        compiler_params=settings(48),
        name=name,
    )(me, left, right)


def expert_kernel(
    me_ref, act_hbm, grad_hbm, gates_ref, gate_hbm, up_hbm, down_hbm, *refs, experts, firsts, later
):
    refs = refs[2:] if later else refs
    outs, (hidden_hbm, inner_hbm) = refs[:6], refs[6:8]
    act_s, grad_s, wide_s, down_s, raw_s, back_s, hidden_s, inner_s, total_s, stage_s = refs[8:18]
    act_sem, wide_sems, down_sems, pass_sems, out_sems = refs[18:]
    rows, hidden, me = act_s.shape[0], gate_hbm.shape[2], me_ref[0]
    first_expert, count = experts

    def fetch(source, target, sem):
        copy = pltpu.make_async_copy(source, target, sem)
        copy.start()
        return copy

    def fetch_wide(expert):
        slot = expert % 2
        return [
            fetch(gate_hbm.at[first_expert + expert], wide_s.at[slot, :, :hidden], wide_sems.at[expert, 0]),
            fetch(up_hbm.at[first_expert + expert], wide_s.at[slot, :, hidden:], wide_sems.at[expert, 1]),
        ]

    def fetch_down(expert):
        pair, at = expert // 2, expert % 2 * hidden
        target = down_s.at[pair % 2, at : at + hidden]
        return [fetch(down_hbm.at[first_expert + expert], target, down_sems.at[expert])]

    def arrive(copies):
        for copy in copies:
            copy.wait()

    def pointwise(expert):
        slot = expert % 2
        at = slice(slot * hidden, (slot + 1) * hidden)
        for start in range(0, rows, 256):
            block = pl.ds(start, 256)
            inner = raw_s[slot, block, :hidden]
            up = raw_s[slot, block, hidden:]
            lane = lax.broadcasted_iota(jnp.int32, (256, LANES), 1)
            mine = lane == first_expert + expert
            gate = jnp.sum(jnp.where(mine, gates_ref[block, :], 0.0), axis=1, keepdims=True)
            square = inner * inner
            bent = jnp.tanh(tanh_scale * inner * (1.0 + tanh_cubic * square))
            half = 0.5 * (1.0 + bent)
            gelu = inner * half
            slope = half + (0.5 * tanh_scale) * inner * (1.0 - bent * bent) * (
                1.0 + (3.0 * tanh_cubic) * square
            )
            back = back_s[block, at] * gate
            hidden_s[block, at] = (gelu * up * gate).astype(low_type)
            inner_s[slot, block, :hidden] = (back * up * slope).astype(low_type)
            inner_s[slot, block, hidden:] = (back * gelu).astype(low_type)

    given = []

    def gradient(left_s, right, chain, part):
        total_s[...] = dot_columns(left_s[...], right).reshape(total_s.shape)
        send_s, keep_s = stage_s.at[chain, part, 0], stage_s.at[chain, part, 1]
        place_slots(me, total_s, send_s, keep_s, firsts[chain])
        columns = pl.ds(part * 2 * hidden, 2 * hidden)
        for side, source in enumerate((send_s, keep_s)):
            target = outs[2 * chain + side].at[:, :, columns]
            given.append(fetch(source, target, out_sems.at[chain, part, side]))

    act_in = [fetch(act_hbm, act_s, act_sem.at[0])]
    wide_in = {0: fetch_wide(0)}
    grad_in = [fetch(grad_hbm, grad_s, act_sem.at[1])]
    down_in = {expert: fetch_down(expert) for expert in range(2)}
    wide_in[1] = fetch_wide(1)
    for expert in range(2, min(4, count)):
        down_in[expert] = fetch_down(expert)
    arrive(act_in)
    passed = []
    for pair in range(count // 2):
        one, two = 2 * pair, 2 * pair + 1
        arrive(wide_in[one])
        raw_s[0] = dot(act_s[...], wide_s[0])
        if one + 2 < count:
            wide_in[one + 2] = fetch_wide(one + 2)
        if pair == 0:
            arrive(grad_in)
        arrive(down_in[one] + down_in[two])
        back_s[...] = dot_rows(grad_s[...], down_s[pair % 2])
        arrive(wide_in[two])
        raw_s[1] = dot(act_s[...], wide_s[1])
        if two + 2 < count:
            wide_in[two + 2] = fetch_wide(two + 2)
        arrive(passed)
        pointwise(0 + one)
        chain = min(one // (count // 2), 1)
        gradient(act_s, inner_s[0], chain, one % (count // 2))
        pointwise(two)
        at = first_expert // 2 + pair
        passed = [
            fetch(hidden_s, hidden_hbm.at[at], pass_sems.at[pair, 0]),
            fetch(inner_s, inner_hbm.at[pl.ds(2 * at, 2)], pass_sems.at[pair, 1]),
        ]
        chain = min(two // (count // 2), 1)
        gradient(act_s, inner_s[1], chain, two % (count // 2))
        gradient(grad_s, hidden_s[...], 2, pair)
    arrive(passed)
    arrive(given)


def expert_group(
    experts, me, act, cotangent, gates, gate_weight, up_weight, down_weight, earlier, devices, firsts
):
    rows, model = act.shape
    hidden = gate_weight.shape[2]
    parts = experts[1] // 2
    half = (devices // 2, model // devices, 2 * hidden)
    joined = half[:2] + (parts * 2 * hidden,)
    hidden_all = like((EXPERTS // 2, rows, 2 * hidden))
    inner_all = like((EXPERTS, rows, 2 * hidden))
    later = earlier is not None
    return pl.pallas_call(
        lambda *refs: expert_kernel(*refs, experts=experts, firsts=firsts, later=later),
        grid_spec=pltpu.PrefetchScalarGridSpec(
            num_scalar_prefetch=1,
            grid=(1,),
            in_specs=[any_space, any_space, whole(gates.shape)]
            + [any_space] * (3 + (2 if later else 0)),
            out_specs=[any_space] * 8,
            scratch_shapes=[
                pltpu.VMEM((rows, model), low_type),
                pltpu.VMEM((rows, model), low_type),
                pltpu.VMEM((2, model, 2 * hidden), low_type),
                pltpu.VMEM((2, 2 * hidden, model), low_type),
                pltpu.VMEM((2, rows, 2 * hidden), sum_type),
                pltpu.VMEM((rows, 2 * hidden), sum_type),
                pltpu.VMEM((rows, 2 * hidden), low_type),
                pltpu.VMEM((2, rows, 2 * hidden), low_type),
                pltpu.VMEM((devices, model // devices, 2 * hidden), sum_type),
                pltpu.VMEM((3, parts, 2) + half, low_type),
                pltpu.SemaphoreType.DMA((2,)),
                pltpu.SemaphoreType.DMA((experts[1], 2)),
                pltpu.SemaphoreType.DMA((experts[1],)),
                pltpu.SemaphoreType.DMA((parts, 2)),
                pltpu.SemaphoreType.DMA((3, parts, 2)),
            ],
        ),
        out_shape=[like(joined)] * 6 + [hidden_all, inner_all],
        input_output_aliases={7: 6, 8: 7} if later else {},
        compiler_params=settings(58),
        name="experts",
    )(me, act, cotangent, gates, gate_weight, up_weight, down_weight, *(earlier or ()))


def inner_back_kernel(inner_ref, gate_ref, up_ref, out_ref, total_s):
    expert = pl.program_id(0)
    hidden = gate_ref.shape[2]

    @pl.when(expert == 0)
    def clear():
        total_s[...] = jnp.zeros(total_s.shape, sum_type)

    weight = jnp.concatenate([gate_ref[0], up_ref[0]], axis=1)
    total_s[...] += dot_rows(inner_ref[0], weight)

    @pl.when(expert == EXPERTS - 1)
    def finish():
        out_ref[...] = total_s[...].astype(low_type)


def inner_back(inner, gate_weight, up_weight):
    rows, model = inner.shape[1], gate_weight.shape[1]
    one = lambda shape: pl.BlockSpec((1,) + shape[1:], lambda expert: (expert, 0, 0))
    return pl.pallas_call(
        inner_back_kernel,
        grid=(EXPERTS,),
        in_specs=[one(inner.shape), one(gate_weight.shape), one(up_weight.shape)],
        out_specs=whole((rows, model)),
        out_shape=like((rows, model)),
        scratch_shapes=[pltpu.VMEM((rows, model), sum_type)],
        compiler_params=settings(48),
        name="expert_back",
    )(inner, gate_weight, up_weight)


def expert_out_kernel(hidden_ref, down_ref, out_ref, total_s):
    pair = pl.program_id(0)

    @pl.when(pair == 0)
    def clear():
        total_s[...] = jnp.zeros(total_s.shape, sum_type)

    total_s[...] += dot(hidden_ref[0], down_ref[...])

    @pl.when(pair == EXPERTS // 2 - 1)
    def finish():
        out_ref[...] = total_s[...].astype(low_type)


def expert_out(hidden, down_weight):
    rows, model = hidden.shape[1], down_weight.shape[2]
    flat = down_weight.reshape(-1, model)
    return pl.pallas_call(
        expert_out_kernel,
        grid=(EXPERTS // 2,),
        in_specs=[
            pl.BlockSpec((1,) + hidden.shape[1:], lambda pair: (pair, 0, 0)),
            pl.BlockSpec((hidden.shape[2], model), lambda pair: (pair, 0)),
        ],
        out_specs=whole((rows, model)),
        out_shape=like((rows, model)),
        scratch_shapes=[pltpu.VMEM((rows, model), sum_type)],
        compiler_params=settings(48),
        name="expert_out",
    )(hidden, flat)


def shifted(shard, by):
    size = lax.axis_size("ctx")
    return lax.ppermute(
        shard, "ctx", [(i, i + by) for i in range(size) if 0 <= i + by < size]
    )


def swapped(part):
    return lax.ppermute(part, "ws", [(0, 1), (1, 0)])


def without(slot, bits):
    for bit in sorted(bits, reverse=True):
        slot = ((slot >> (bit + 1)) << bit) | (slot & ((1 << bit) - 1))
    return slot


def with_zeros(index, bits):
    for bit in sorted(bits):
        index = ((index >> bit) << (bit + 1)) | (index & ((1 << bit) - 1))
    return index


class Chain:
    def __init__(self, send, keep, order):
        self.left = list(order)
        self.done = []
        self.parts = [keep]
        self.held = [(order[0],)]
        self.waiting = send

    def launch(self):
        bit = self.left.pop(0)
        self.done.append(bit)
        size = lax.axis_size("ctx")
        self.parts.append(
            lax.ppermute(self.waiting, "ctx", [(i, i ^ (1 << bit)) for i in range(size)])
        )
        self.held.append(tuple(self.done))
        self.waiting = None


def combine_kernel(*refs, counts):
    outs = refs[len(refs) - len(counts) :]
    at = 0
    for out, count in zip(outs, counts):
        total = refs[at][...].astype(sum_type)
        for ref in refs[at + 1 : at + count]:
            total += ref[...].astype(sum_type)
        out[...] = total.astype(out.dtype)
        at += count


def part_spec(part, held, done, bit):
    def index(tile):
        slot = with_zeros(tile, list(done) + [bit]) | (1 << bit)
        return (without(slot, held), 0, 0)

    return pl.BlockSpec((1,) + part.shape[1:], index)


def step_chains(chains):
    if not chains:
        return
    slots = lax.axis_size("ctx") >> (len(chains[0].done) + 1)
    specs, operands, outs, out_specs = [], [], [], []
    for chain in chains:
        for part, held in zip(chain.parts, chain.held):
            specs.append(part_spec(part, held, chain.done, chain.left[0]))
            operands.append(part)
        block = (1,) + part.shape[1:]
        out_specs.append(pl.BlockSpec(block, lambda tile: (tile, 0, 0)))
        outs.append(like((slots,) + part.shape[1:]))
    counts = tuple(len(chain.parts) for chain in chains)
    sends = pl.pallas_call(
        lambda *refs: combine_kernel(*refs, counts=counts),
        grid=(slots,),
        in_specs=specs,
        out_specs=out_specs,
        out_shape=outs,
        compiler_params=settings(24),
        name="sum_parts",
    )(*operands)
    for chain, send in zip(chains, sends):
        chain.waiting = send


def end_kernel(*refs, counts, finals):
    outs = refs[len(refs) - finals :]
    totals, at = [], 0
    for count in counts:
        total = refs[at][0].astype(sum_type)
        for ref in refs[at + 1 : at + count]:
            total += ref[0].astype(sum_type)
        totals.append(total)
        at += count
    return totals, outs


def end_experts_kernel(*refs, counts):
    totals, (gate_ref, up_ref, down_ref) = end_kernel(*refs, counts=counts, finals=3)
    experts, _, hidden = gate_ref.shape
    for expert in range(experts):
        at = expert % (experts // 2) * 2 * hidden
        total = totals[expert // (experts // 2)]
        gate_ref[expert] = total[:, at : at + hidden]
        up_ref[expert] = total[:, at + hidden : at + 2 * hidden]
        down_ref[expert] = totals[2][:, expert * hidden : (expert + 1) * hidden].T


def end_other_kernel(*refs, counts, turned):
    totals, outs = end_kernel(*refs, counts=counts, finals=len(counts))
    for total, out, turn in zip(totals, outs, turned):
        out[...] = total.T if turn else total


def all_parts(chains):
    return [part for chain in chains for part in chain.parts]


def end_experts(chains, experts, hidden, earlier):
    operands = all_parts(chains)
    counts = tuple(len(chain.parts) for chain in chains)
    _, rows, wide = operands[0].shape
    own = pl.BlockSpec((1, rows, wide), lambda tile: (0, 0, 0))
    shapes = [(EXPERTS, rows, hidden), (EXPERTS, rows, hidden), (EXPERTS, hidden, rows)]
    extra = len(earlier)
    at = experts[0] // experts[1]

    def run(*refs):
        end_experts_kernel(*(refs[: len(operands)] + refs[len(operands) + extra :]), counts=counts)

    return pl.pallas_call(
        run,
        grid=(1,),
        in_specs=[own] * len(operands) + [any_space] * extra,
        out_specs=[
            pl.BlockSpec((experts[1],) + shape[1:], lambda tile: (at, 0, 0)) for shape in shapes
        ],
        out_shape=[like(shape, sum_type) for shape in shapes],
        input_output_aliases={len(operands) + k: k for k in range(extra)},
        compiler_params=settings(24),
        name="expert_gradients",
    )(*operands, *earlier)


def end_others(chains, turned):
    operands = all_parts(chains)
    counts = tuple(len(chain.parts) for chain in chains)
    own = [pl.BlockSpec((1,) + part.shape[1:], lambda tile: (0, 0, 0)) for part in operands]
    shapes = [
        chain.parts[0].shape[:0:-1] if turn else chain.parts[0].shape[1:]
        for chain, turn in zip(chains, turned)
    ]
    return pl.pallas_call(
        lambda *refs: end_other_kernel(*refs, counts=counts, turned=turned),
        grid=(1,),
        in_specs=own,
        out_specs=[whole(shape) for shape in shapes],
        out_shape=[like(shape, sum_type) for shape in shapes],
        compiler_params=settings(24),
        name="other_gradients",
    )(*operands)


def hook(anchor, fresh=(), advance=()):
    moving = [chain for group in advance for chain in group]
    anchor, parts = lax.optimization_barrier((anchor, [chain.parts for chain in moving]))
    for chain, kept in zip(moving, parts):
        chain.parts = kept
    for group in advance:
        step_chains(group)
    ready = list(moving) + list(fresh)
    anchor, sends = lax.optimization_barrier((anchor, [chain.waiting for chain in ready]))
    for chain, send in zip(ready, sends):
        chain.waiting = send
        chain.launch()
    return anchor


def chain_orders(bits):
    low = list(range(bits))
    return (low, [1, 0] + low[2:], [2, 0, 1] + low[3:])


def gate_table(routes, live_rows, gate_rows):
    chosen = routes[:, :, None] == jnp.arange(EXPERTS, dtype=jnp.int32)[None, None, :]
    one_hot = jnp.any(chosen, axis=1).astype(jnp.int32) * live_rows[:, None]
    rank = jnp.cumsum(one_hot, axis=0) - one_hot
    kept = (one_hot == 1) & (rank < CAP)
    gates = jnp.sum(jnp.where(chosen, gate_rows[:, :, None], 0.0), axis=1)
    return jnp.pad(jnp.where(kept, gates, 0.0), ((0, 0), (0, LANES - EXPERTS)))


def body(
    tokens,
    cotangent,
    first_gain,
    query_weight,
    key_projection_weight,
    value_projection_weight,
    out_weight,
    second_gain,
    gate_weight,
    up_weight,
    down_weight,
    segments,
    live_mask,
    routes,
    gate_values,
):
    rows, model = tokens.shape
    devices = lax.axis_size("ctx")
    bits = devices.bit_length() - 1
    index = lax.axis_index("ctx")
    me = index.astype(jnp.int32).reshape(1)
    first_row = index * rows
    query_block, key_block = 256, 256
    gain_one, gain_two = first_gain[None, :], second_gain[None, :]
    orders = chain_orders(bits)
    firsts = tuple(order[0] for order in orders)

    half = HEAD_DIMENSION // 2
    frequency = rope_base ** (-2.0 * jnp.arange(half, dtype=sum_type) / HEAD_DIMENSION)
    positions = (first_row + jnp.arange(rows, dtype=jnp.int32)).astype(sum_type)
    angles = frequency[:, None] * positions[None, :]
    cosine, sine = jnp.cos(angles), jnp.sin(angles)
    cosine_rows, sine_rows = cosine.T, sine.T
    cosine_full = jnp.concatenate([cosine_rows, cosine_rows], axis=1)
    sine_full = jnp.concatenate([-sine_rows, sine_rows], axis=1)

    activation, own_pair = project_keys(
        tokens, gain_one, key_projection_weight, value_projection_weight, cosine_full, sine_full
    )
    reach = min(devices, (DOC_MAX + rows - 2) // rows + 1)
    pairs = [shifted(own_pair, by) for by in range(reach - 1, 0, -1)] + [own_pair]
    queries = project_queries(activation, query_weight, cosine, sine)
    gates = gate_table(routes, lax.dynamic_slice_in_dim(live_mask, first_row, rows, 0), gate_values)

    span = reach * rows
    own_at = span - rows
    padded_segments = jnp.concatenate([jnp.full((own_at,), -1, jnp.int32), segments])
    padded_live = jnp.concatenate([jnp.zeros((own_at,), jnp.int32), live_mask])
    key_segments = lax.dynamic_slice_in_dim(padded_segments, first_row, span, 0)
    key_live = lax.dynamic_slice_in_dim(padded_live, first_row, span, 0)
    key_place = jnp.arange(span, dtype=jnp.int32) - own_at
    begins = jnp.concatenate([jnp.ones((1,), bool), key_segments[1:] != key_segments[:-1]])
    low = lax.cummax(jnp.where(begins, key_place, -own_at))[own_at:]
    place = jnp.broadcast_to(
        jnp.where(key_live == 1, key_place, far_position)[:, None], (span, LANES)
    )
    first_block = (low[::query_block] + own_at) // key_block
    low = low[None, :]
    queries, gates, low, place = lax.optimization_barrier((queries, gates, low, place))

    joined = jnp.concatenate(pairs, axis=0)
    key_width = key_projection_weight.shape[1]
    keys, values = joined[:, :key_width], joined[:, key_width:]
    mixed_turned, mixed, logs = attend(
        first_block, queries, keys, values.T, place, low, query_block, key_block
    )
    part = product(mixed, out_weight, "attention_out")
    residual, act_two = second_norm(tokens, part, swapped(part), gain_two)

    earlier, groups = None, []
    split = ((0, 4), (4, 4))
    for number, experts in enumerate(split):
        outs = expert_group(
            experts, me, act_two, cotangent, gates, gate_weight, up_weight, down_weight, earlier, devices,
            firsts,
        )
        groups.append([Chain(outs[2 * k], outs[2 * k + 1], orders[k]) for k in range(3)])
        earlier = outs[6:]
        act_two, earlier = hook((act_two, earlier), groups[number], groups[:number])
    hidden_all, inner_all = earlier

    def advancing(*some):
        return [group for group in some if group[0].left]

    back = inner_back(inner_all, gate_weight, up_weight)
    back_other = swapped(back)
    out_part = expert_out(hidden_all, down_weight)
    out_part, back_other = hook((out_part, back_other), (), advancing(groups[0]))
    out_other = swapped(out_part)
    total, total_low, grad_heads = second_back(
        back, back_other, residual, cotangent, gain_two, out_weight
    )
    send, keep = grad_parts(me, total_low, mixed, devices, firsts[:1], "out_grad")
    out_group = [Chain(send, keep, orders[0])]
    output = (
        residual + (out_part.astype(sum_type) + out_other.astype(sum_type))
    ).astype(low_type)
    grad_heads = hook(grad_heads, out_group, ())

    grad_queries, far, own = attend_back(
        first_block, queries, keys, keys.T, values, place, low, mixed_turned, grad_heads, logs,
        cosine, sine, query_block, key_block,
    )
    returned = [
        shifted(far[at * rows : (at + 1) * rows], at + 1 - reach) for at in range(reach - 1)
    ]
    grad_queries, own = hook(
        (grad_queries, own), (), advancing(groups[1], groups[0])
    )
    parts = grad_parts(me, activation, grad_queries, devices, firsts, "query_grad")
    query_group = [Chain(parts[2 * k], parts[2 * k + 1], orders[k]) for k in range(3)]
    grad_queries, own = hook((grad_queries, own), query_group, advancing(out_group))
    pair_grad = own + sum(piece.astype(sum_type) for piece in returned)
    grad_keys = pair_grad[:, :key_width]
    turned = jnp.concatenate([grad_keys[:, half:], grad_keys[:, :half]], axis=1)
    grad_pairs = jnp.concatenate(
        [grad_keys * cosine_full - turned * sine_full, pair_grad[:, key_width:]], axis=1
    ).astype(low_type)
    send, keep = grad_parts(me, activation, grad_pairs, devices, firsts[:1], "key_value_grad")
    pair_group = [Chain(send, keep, orders[0])]
    grad_pairs = hook(grad_pairs, pair_group, ())
    grad_act = act_back(
        grad_queries, grad_pairs, query_weight, key_projection_weight, value_projection_weight
    )
    grad_act = hook(grad_act, (), advancing(query_group, groups[1], out_group))
    act_other = swapped(grad_act)
    act_other = hook(act_other, (), advancing(pair_group, query_group))
    token_grad = first_back(grad_act, act_other, tokens, total, gain_one)
    token_grad = hook(token_grad, (), advancing(pair_group, query_group, groups[1], out_group))

    everything = [*groups, out_group, pair_group, query_group]
    while any(group[0].left for group in everything):
        token_grad = hook(token_grad, (), advancing(*everything))
    own_rows = model // devices
    ended = ()
    for experts, group in zip(split, groups):
        ended = end_experts(group, experts, gate_weight.shape[2], ended)
    gate_grad, up_grad, down_grad = ended
    out_grad, pair_grads, *query_parts = end_others(
        out_group + pair_group + query_group, (True, False, False, False, False)
    )
    query_grad = jnp.concatenate(query_parts, axis=1)
    key_grad, value_grad = pair_grads[:, :key_width], pair_grads[:, key_width:]

    def own_part(weight):
        return lax.dynamic_slice_in_dim(weight, index * own_rows, own_rows, 0).astype(sum_type)

    first_part = (
        jnp.sum(query_grad * own_part(query_weight), axis=1)
        + jnp.sum(key_grad * own_part(key_projection_weight), axis=1)
        + jnp.sum(value_grad * own_part(value_projection_weight), axis=1)
    )
    own_gate = lax.dynamic_slice_in_dim(gate_weight, index * own_rows, own_rows, 1).astype(sum_type)
    own_up = lax.dynamic_slice_in_dim(up_weight, index * own_rows, own_rows, 1).astype(sum_type)
    second_part = jnp.sum(gate_grad * own_gate + up_grad * own_up, axis=(0, 2))
    gain_parts = jnp.stack([first_part, second_part])
    gains = jnp.stack([first_gain, second_gain])
    gain_grads = (gain_parts + swapped(gain_parts)) / lax.dynamic_slice_in_dim(
        gains, index * own_rows, own_rows, 1
    )
    grad_first, grad_second = gain_grads[0], gain_grads[1]
    return (
        output,
        token_grad,
        grad_first,
        query_grad,
        key_grad,
        value_grad,
        out_grad,
        grad_second,
        gate_grad,
        up_grad,
        down_grad,
    )


def solution(mesh):
    return jax.shard_map(
        body,
        mesh=mesh,
        in_specs=(
            P("ctx", None),
            P("ctx", None),
            P(),
            P(None, "ws"),
            P(None, "ws"),
            P(None, "ws"),
            P("ws", None),
            P(),
            P(None, None, "ws"),
            P(None, None, "ws"),
            P(None, "ws", None),
            P(),
            P(),
            P("ctx", None),
            P("ctx", None),
        ),
        out_specs=(
            P("ctx", None),
            P("ctx", None),
            P("ctx"),
            P("ctx", "ws"),
            P("ctx", "ws"),
            P("ctx", "ws"),
            P("ws", "ctx"),
            P("ctx"),
            P(None, "ctx", "ws"),
            P(None, "ctx", "ws"),
            P(None, "ws", "ctx"),
        ),
        check_vma=False,
    )
```

```python
import jax
import jax.numpy as jnp
from jax import lax
from jax.experimental import pallas as pl
from jax.experimental.pallas import tpu as pltpu
from jax.sharding import PartitionSpec as P

HEAD_DIMENSION = 128
EXPERTS = 8
DOC_MAX = 2000
CAP = 640
LANES = 128

eps = 1e-06
rope_base = 1000000.0
masked_score = -1e30
far_position = 1 << 30
log2_e = 1.4426950408889634
tanh_scale = 0.7978845608028654
tanh_cubic = 0.044715

low_type = jnp.bfloat16
sum_type = jnp.float32
any_space = pl.BlockSpec(memory_space=pl.ANY)


def dot(left, right):
    return jnp.dot(left, right, preferred_element_type=sum_type)


def dot_rows(left, right):
    return lax.dot_general(left, right, (((1,), (1,)), ((), ())), preferred_element_type=sum_type)


def dot_columns(left, right):
    return lax.dot_general(left, right, (((0,), (0,)), ((), ())), preferred_element_type=sum_type)


def whole(shape):
    return pl.BlockSpec(shape, lambda *index: (0,) * len(shape))


def by_rows(block, shape):
    return pl.BlockSpec((block,) + shape[1:], lambda row, *rest: (row,) + (0,) * (len(shape) - 1))


def like(shape, kind=low_type):
    return jax.ShapeDtypeStruct(shape, kind)


def settings(megabytes):
    return pltpu.CompilerParams(vmem_limit_bytes=megabytes * 2**20)


light = pl.CostEstimate(flops=1000, transcendentals=0, bytes_accessed=1000)


def kernel_call(body, **options):
    return pl.pallas_call(body, cost_estimate=light, **options)


def normalize(value):
    factor = lax.rsqrt(jnp.mean(value * value, axis=-1, keepdims=True) + eps)
    return value * factor, factor


def normalize_back(grad_normed, normed, factor):
    return factor * (grad_normed - normed * jnp.mean(grad_normed * normed, axis=-1, keepdims=True))


def table_kernel(
    segment_ref, own_segment_ref, live_ref, route_ref, value_ref, place_ref, low_ref, gates_ref
):
    span, own_at = segment_ref.shape[0], segment_ref.shape[0] - own_segment_ref.shape[1]
    rows = own_segment_ref.shape[1]
    before = (segment_ref[...] < own_segment_ref[...]).astype(jnp.int32)
    low_ref[...] = jnp.sum(before, axis=0, keepdims=True) - own_at
    position = lax.broadcasted_iota(jnp.int32, (span, LANES), 0) - own_at
    live = jnp.broadcast_to(live_ref[...], (span, LANES)) == 1
    place_ref[...] = jnp.where(live, position, far_position)
    lane = lax.broadcasted_iota(jnp.int32, (rows, LANES), 1)
    chosen = jnp.zeros((rows, LANES), sum_type)
    gates = jnp.zeros((rows, LANES), sum_type)
    for top in range(route_ref.shape[1]):
        here = lane == route_ref[:, top : top + 1]
        chosen = jnp.where(here, 1.0, chosen)
        gates = jnp.where(here, value_ref[:, top : top + 1], gates)
    chosen = jnp.where(live[own_at:], chosen, 0.0)
    earlier = lax.broadcasted_iota(jnp.int32, (rows, rows), 1) < lax.broadcasted_iota(
        jnp.int32, (rows, rows), 0
    )
    rank = dot(earlier.astype(low_type), chosen.astype(low_type))
    gates_ref[...] = jnp.where((chosen > 0.5) & (rank < CAP), gates, 0.0)


def tables(key_segments, own_segments, key_live, routes, gate_values):
    span, rows = key_segments.shape[0], own_segments.shape[1]
    shapes = [like((span, LANES), jnp.int32), like((1, rows), jnp.int32), like((rows, LANES), sum_type)]
    operands = (key_segments, own_segments, key_live, routes, gate_values)
    return kernel_call(
        table_kernel,
        grid=(1,),
        in_specs=[whole(operand.shape) for operand in operands],
        out_specs=[whole(shape.shape) for shape in shapes],
        out_shape=shapes,
        compiler_params=settings(32),
        name="tables",
    )(*operands)


def full_tables(cos_ref, sin_ref):
    cosine, sine = cos_ref[...].T, sin_ref[...].T
    return jnp.concatenate([cosine, cosine], axis=1), jnp.concatenate([-sine, sine], axis=1)


def key_value_kernel(token_ref, gain_ref, key_ref, value_ref, cos_ref, sin_ref, act_ref, out_ref):
    normed, factor = normalize(token_ref[...].astype(sum_type))
    act = (normed * gain_ref[...]).astype(low_type)
    act_ref[...] = act
    keys = dot(act, key_ref[...])
    width = keys.shape[1]
    cosine, sine = full_tables(cos_ref, sin_ref)
    turned = pltpu.roll(keys, HEAD_DIMENSION // 2, 1)
    out_ref[:, :width] = (keys * cosine + turned * sine).astype(low_type)
    out_ref[:, width:] = dot(act, value_ref[...]).astype(low_type)


def project_keys(tokens, gain, key_weight, value_weight, cosine, sine, block=256):
    rows, width = tokens.shape
    joined = key_weight.shape[1] + value_weight.shape[1]
    columns = pl.BlockSpec((cosine.shape[0], block), lambda row: (0, row))
    return kernel_call(
        key_value_kernel,
        grid=(rows // block,),
        in_specs=[
            by_rows(block, tokens.shape),
            whole((1, width)),
            whole(key_weight.shape),
            whole(value_weight.shape),
            columns,
            columns,
        ],
        out_specs=[by_rows(block, (rows, width)), by_rows(block, (rows, joined))],
        out_shape=[like((rows, width)), like((rows, joined))],
        compiler_params=settings(32),
        name="norm_keys_values",
    )(tokens, gain, key_weight, value_weight, cosine, sine)


def query_kernel(act_ref, weight_ref, cos_ref, sin_ref, out_ref):
    raw = dot(act_ref[...], weight_ref[...])
    half = HEAD_DIMENSION // 2
    cosine, sine = cos_ref[...], sin_ref[...]
    for head in range(out_ref.shape[0]):
        part = raw[:, head * HEAD_DIMENSION : (head + 1) * HEAD_DIMENSION].T
        one, two = part[:half], part[half:]
        out_ref[head, :half] = (one * cosine - two * sine).astype(low_type)
        out_ref[head, half:] = (two * cosine + one * sine).astype(low_type)


def project_queries(act, weight, cosine, sine, block=256):
    rows, width = act.shape
    heads = weight.shape[1] // HEAD_DIMENSION
    half = HEAD_DIMENSION // 2
    columns = pl.BlockSpec((half, block), lambda row: (0, row))
    return kernel_call(
        query_kernel,
        grid=(rows // block,),
        in_specs=[by_rows(block, act.shape), whole(weight.shape), columns, columns],
        out_specs=pl.BlockSpec((heads, HEAD_DIMENSION, block), lambda row: (0, 0, row)),
        out_shape=like((heads, HEAD_DIMENSION, rows)),
        compiler_params=settings(32),
        name="queries",
    )(act, weight, cosine, sine)


def repeat_lanes(block, times):
    return jnp.concatenate([block] * times, axis=1) if times > 1 else block


def join_heads(ref):
    return jnp.concatenate([ref[head] for head in range(ref.shape[0])], axis=1)


def allowed_pairs(place_ref, rows, low, high, start, own_at, own):
    size, count = rows.size, low.shape[1]
    place = repeat_lanes(place_ref[rows, :], count // LANES)
    allowed = (place >= low) & (place <= high)
    if own:
        position = start - own_at + lax.broadcasted_iota(jnp.int32, (size, count), 0)
        allowed = allowed | (position == high)
    return allowed


def over_keys(first_ref, step, own_at, query_block, key_block, tile):
    own_first = (own_at + tile * query_block) // key_block
    for extra in range(max(1, query_block // key_block)):
        step(own_first + extra, True)

    def loop(index, carried):
        step(index, False)
        return carried

    lax.fori_loop(first_ref[tile], own_first, loop, 0)


def mix_kernel(
    first_ref, query_ref, place_ref, low_ref, *refs, key_block, own_at, scale,
):
    pieces, (out_ref, mixed_ref, log_ref) = refs[:-8], refs[-8:-5]
    key_s, value_s, max_s, sum_s, mix_s = refs[-5:]
    heads, depth, query_block = query_ref.shape
    count = heads * query_block
    tile = pl.program_id(0)

    @pl.when(tile == 0)
    def gather():
        for number, piece in enumerate(pieces):
            at = slice(number * piece.shape[0], (number + 1) * piece.shape[0])
            key_s[at, :] = piece[:, :depth]
            value_s[:, at] = piece[:, depth:].astype(sum_type).T.astype(low_type)

    queries = join_heads(query_ref)
    low = repeat_lanes(low_ref[...], heads)
    high = repeat_lanes(
        tile * query_block + lax.broadcasted_iota(jnp.int32, (1, query_block), 1), heads
    )
    max_s[...] = jnp.full(max_s.shape, masked_score, sum_type)
    sum_s[...] = jnp.zeros(sum_s.shape, sum_type)
    mix_s[...] = jnp.zeros(mix_s.shape, sum_type)

    def step(index, own):
        start = pl.multiple_of(index * key_block, key_block)
        rows = pl.ds(start, key_block)
        raw = dot(key_s[rows, :], queries)
        allowed = allowed_pairs(place_ref, rows, low, high, start, own_at, own)
        scores = jnp.where(allowed, raw * (scale * log2_e), masked_score)
        old = max_s[...]
        new = jnp.maximum(old, jnp.max(scores, axis=0, keepdims=True))
        weights = jnp.exp2(scores - new)
        fade = jnp.exp2(old - new)
        sum_s[...] = sum_s[...] * fade + jnp.sum(weights, axis=0, keepdims=True)
        max_s[...] = new
        mix_s[...] = mix_s[...] * fade + dot(value_s[:, rows], weights.astype(low_type))

    over_keys(first_ref, step, own_at, query_block, key_block, tile)
    total = sum_s[...]
    mixed = mix_s[...] * (1.0 / total)
    logs = max_s[...] + jnp.log2(total)
    for head in range(heads):
        at = slice(head * query_block, (head + 1) * query_block)
        out_ref[head] = mixed[:, at]
        mixed_ref[:, head * depth : (head + 1) * depth] = mixed[:, at].T.astype(low_type)
        log_ref[head] = logs[:, at]


def tile_of(query_block):
    def column(shape):
        return pl.BlockSpec(
            shape[:-1] + (query_block,), lambda tile, *rest: (0,) * (len(shape) - 1) + (tile,)
        )

    return column


def attend(first, queries, pieces, place, low, query_block, key_block):
    heads, depth, rows = queries.shape
    column = tile_of(query_block)
    count = heads * query_block
    span = place.shape[0]
    return kernel_call(
        lambda *refs: mix_kernel(*refs, key_block=key_block, own_at=span - rows, scale=depth**-0.5),
        grid_spec=pltpu.PrefetchScalarGridSpec(
            num_scalar_prefetch=1,
            grid=(rows // query_block,),
            in_specs=[column(queries.shape), whole(place.shape), column(low.shape)]
            + [whole(piece.shape) for piece in pieces],
            out_specs=[
                column(queries.shape),
                by_rows(query_block, (rows, heads * depth)),
                column((heads, 1, rows)),
            ],
            scratch_shapes=[
                pltpu.VMEM((span, depth), low_type),
                pltpu.VMEM((depth, span), low_type),
                pltpu.VMEM((1, count), sum_type),
                pltpu.VMEM((1, count), sum_type),
                pltpu.VMEM((depth, count), sum_type),
            ],
        ),
        out_shape=[
            like(queries.shape, sum_type),
            like((rows, heads * depth)),
            like((heads, 1, rows), sum_type),
        ],
        compiler_params=settings(62),
        name="attention",
    )(first, queries, place, low, *pieces)


def mix_back_kernel(
    first_ref, query_ref, place_ref, low_ref, mixed_ref, grad_ref, log_ref, cos_ref, sin_ref, *refs,
    reach, key_block, own_at, scale, tiles, offset, final,
):
    pieces, refs = refs[:reach], refs[reach:]
    earlier, refs = (refs[:2], refs[3:]) if offset else ((), refs)
    out_ref, *end_refs = refs[:-6]
    key_s, turned_s, value_s, query_sum, key_sum, value_sum = refs[-6:]
    heads, depth, query_block = query_ref.shape
    tile = pl.program_id(0) + offset
    queries, grads, logs = join_heads(query_ref), join_heads(grad_ref), join_heads(log_ref)
    delta = jnp.sum(grads.astype(sum_type) * join_heads(mixed_ref), axis=0, keepdims=True)
    low = repeat_lanes(low_ref[...], heads)
    high = repeat_lanes(
        tile * query_block + lax.broadcasted_iota(jnp.int32, (1, query_block), 1), heads
    )

    @pl.when(pl.program_id(0) == 0)
    def gather():
        for number, piece in enumerate(pieces):
            at = slice(number * piece.shape[0], (number + 1) * piece.shape[0])
            key_s[at, :] = piece[:, :depth]
            turned_s[:, at] = piece[:, :depth].astype(sum_type).T.astype(low_type)
            value_s[at, :] = piece[:, depth:]
        if offset:
            key_sum[...] = earlier[0][...]
            value_sum[...] = earlier[1][...]
        else:
            key_sum[...] = jnp.zeros(key_sum.shape, sum_type)
            value_sum[...] = jnp.zeros(value_sum.shape, sum_type)

    query_sum[...] = jnp.zeros(query_sum.shape, sum_type)

    def step(index, own):
        start = pl.multiple_of(index * key_block, key_block)
        rows = pl.ds(start, key_block)
        raw = dot(key_s[rows, :], queries)
        allowed = allowed_pairs(place_ref, rows, low, high, start, own_at, own)
        weights = jnp.exp2(jnp.where(allowed, raw * (scale * log2_e), masked_score) - logs)
        grad_weights = dot(value_s[rows, :], grads)
        grad_scores = (weights * (grad_weights - delta)).astype(low_type)
        value_sum[rows, :] += dot_rows(weights.astype(low_type), grads)
        key_sum[rows, :] += dot_rows(grad_scores, queries)
        query_sum[...] += dot(turned_s[:, rows], grad_scores)

    over_keys(first_ref, step, own_at, query_block, key_block, tile)
    half = depth // 2
    cosine, sine = repeat_lanes(cos_ref[...], heads), repeat_lanes(sin_ref[...], heads)
    grad_query = query_sum[...] * scale
    one, two = grad_query[:half], grad_query[half:]
    turned = jnp.concatenate([one * cosine + two * sine, two * cosine - one * sine], axis=0)
    for head in range(heads):
        part = turned[:, head * query_block : (head + 1) * query_block]
        out_ref[:, head * depth : (head + 1) * depth] = part.T.astype(low_type)

    @pl.when(pl.program_id(0) == tiles - 1)
    def finish():
        if final:
            for number, ref in enumerate(end_refs):
                at = slice(number * ref.shape[0], (number + 1) * ref.shape[0])
                ref[:, :depth] = (key_sum[at, :] * scale).astype(ref.dtype)
                ref[:, depth:] = value_sum[at, :].astype(ref.dtype)
        else:
            end_refs[0][...] = key_sum[...]
            end_refs[1][...] = value_sum[...]


def attend_back(
    first, queries, pieces, place, low, mixed, grads, logs, cosine, sine, query_block, key_block, part, earlier
):
    heads, depth, rows = queries.shape
    span = place.shape[0]
    offset, tiles = part[0], part[1] - part[0]
    final = part[1] * query_block == rows

    def column(shape):
        return pl.BlockSpec(
            shape[:-1] + (query_block,),
            lambda tile, *rest: (0,) * (len(shape) - 1) + (tile + offset,),
        )

    extra = [whole((span, depth)), whole((span, depth)), any_space] if offset else []
    ends = (
        [like((rows, 2 * depth))] * (len(pieces) - 1) + [like((rows, 2 * depth), sum_type)]
        if final
        else [like((span, depth), sum_type)] * 2
    )
    operands = [queries, place, low, mixed, grads, logs, cosine, sine, *pieces]
    return kernel_call(
        lambda *refs: mix_back_kernel(
            *refs,
            reach=len(pieces),
            key_block=key_block,
            own_at=span - rows,
            scale=depth**-0.5,
            tiles=tiles,
            offset=offset,
            final=final,
        ),
        grid_spec=pltpu.PrefetchScalarGridSpec(
            num_scalar_prefetch=1,
            grid=(tiles,),
            in_specs=[
                column(queries.shape),
                whole(place.shape),
                column(low.shape),
                column(mixed.shape),
                column(grads.shape),
                column(logs.shape),
                column(cosine.shape),
                column(sine.shape),
            ]
            + [whole(piece.shape) for piece in pieces]
            + extra,
            out_specs=[
                pl.BlockSpec((query_block, heads * depth), lambda tile, *rest: (tile + offset, 0)),
                *[whole(end.shape) for end in ends],
            ],
            scratch_shapes=[
                pltpu.VMEM((span, depth), low_type),
                pltpu.VMEM((depth, span), low_type),
                pltpu.VMEM((span, depth), low_type),
                pltpu.VMEM((depth, heads * query_block), sum_type),
                pltpu.VMEM((span, depth), sum_type),
                pltpu.VMEM((span, depth), sum_type),
            ],
        ),
        out_shape=[like((rows, heads * depth)), *ends],
        input_output_aliases={len(operands) + 3: 0} if offset else {},
        compiler_params=settings(62),
        name="attention_back",
    )(first, *operands, *(((earlier[1], earlier[2], earlier[0])) if offset else ()))


def product_kernel(left_ref, right_ref, out_ref):
    out_ref[...] = dot(left_ref[...], right_ref[...]).astype(out_ref.dtype)


def product(left, right, name, block=256):
    rows = left.shape[0]
    out = (rows, right.shape[1])
    return kernel_call(
        product_kernel,
        grid=(rows // block,),
        in_specs=[by_rows(block, left.shape), whole(right.shape)],
        out_specs=by_rows(block, out),
        out_shape=like(out),
        compiler_params=settings(32),
        name=name,
    )(left, right)


def second_norm_kernel(token_ref, own_ref, other_ref, gain_ref, sum_ref, act_ref):
    mixed = own_ref[...].astype(sum_type) + other_ref[...].astype(sum_type)
    residual = token_ref[...].astype(sum_type) + mixed
    sum_ref[...] = residual
    act_ref[...] = (normalize(residual)[0] * gain_ref[...]).astype(low_type)


def second_norm(tokens, own, other, gain, block=256):
    rows = by_rows(block, tokens.shape)
    return kernel_call(
        second_norm_kernel,
        grid=(tokens.shape[0] // block,),
        in_specs=[rows, rows, rows, whole(gain.shape)],
        out_specs=[rows, rows],
        out_shape=[like(tokens.shape, sum_type), like(tokens.shape)],
        compiler_params=settings(62),
        name="residual_norm",
    )(tokens, own, other, gain)


def second_back_kernel(
    own_ref, other_ref, sum_ref, grad_ref, gain_ref, weight_ref, total_ref, low_ref, heads_ref
):
    grad_act = own_ref[...].astype(sum_type) + other_ref[...].astype(sum_type)
    normed, factor = normalize(sum_ref[...])

    total = grad_ref[...].astype(sum_type) + normalize_back(
        grad_act * gain_ref[...], normed, factor
    )
    total_ref[...] = total
    low = total.astype(low_type)
    low_ref[...] = low
    turned = dot_rows(weight_ref[...], low).astype(low_type)
    heads_ref[...] = turned.reshape(heads_ref.shape)


def second_back(own, other, residual, cotangent, gain, out_weight, block=256):
    rows = by_rows(block, own.shape)
    heads = out_weight.shape[0] // HEAD_DIMENSION
    shape = (heads, HEAD_DIMENSION, own.shape[0])
    return kernel_call(
        second_back_kernel,
        grid=(own.shape[0] // block,),
        in_specs=[rows, rows, rows, rows, whole(gain.shape), whole(out_weight.shape)],
        out_specs=[rows, rows, tile_of(block)(shape)],
        out_shape=[like(own.shape, sum_type), like(own.shape), like(shape)],
        compiler_params=settings(62),
        name="residual_back",
    )(own, other, residual, cotangent, gain, out_weight)


def act_back_kernel(query_ref, pair_ref, query_weight_ref, key_weight_ref, value_weight_ref, out_ref):
    width = key_weight_ref.shape[1]
    total = dot_rows(query_ref[...], query_weight_ref[...])
    total += dot_rows(pair_ref[:, :width], key_weight_ref[...])
    total += dot_rows(pair_ref[:, width:], value_weight_ref[...])
    out_ref[...] = total.astype(low_type)


def act_back(queries, pairs, query_weight, key_weight, value_weight, block=256):
    out = (queries.shape[0], query_weight.shape[0])
    return kernel_call(
        act_back_kernel,
        grid=(out[0] // block,),
        in_specs=[
            by_rows(block, queries.shape),
            by_rows(block, pairs.shape),
            whole(query_weight.shape),
            whole(key_weight.shape),
            whole(value_weight.shape),
        ],
        out_specs=by_rows(block, out),
        out_shape=like(out),
        compiler_params=settings(32),
        name="activation_back",
    )(queries, pairs, query_weight, key_weight, value_weight)


def last_rows_kernel(
    own_ref, other_ref, token_ref, total_ref, gain_ref, sum_ref, out_own_ref, out_other_ref, grad_ref, out_ref
):
    grad_act = own_ref[...].astype(sum_type) + other_ref[...].astype(sum_type)
    normed, factor = normalize(token_ref[...].astype(sum_type))
    grad_ref[...] = total_ref[...] + normalize_back(grad_act * gain_ref[...], normed, factor)
    mixed = out_own_ref[...].astype(sum_type) + out_other_ref[...].astype(sum_type)
    out_ref[...] = (sum_ref[...] + mixed).astype(low_type)


def last_rows(own, other, tokens, total, gain, residual, out_own, out_other, block=256):
    rows = by_rows(block, own.shape)
    return kernel_call(
        last_rows_kernel,
        grid=(own.shape[0] // block,),
        in_specs=[rows, rows, rows, rows, whole(gain.shape), rows, rows, rows],
        out_specs=[rows, rows],
        out_shape=[like(own.shape, sum_type), like(own.shape)],
        compiler_params=settings(62),
        name="last_rows",
    )(own, other, tokens, total, gain, residual, out_own, out_other)


def slot_of(rest, bit, first):
    return ((rest >> first) << (first + 1)) | (bit << first) | (rest & ((1 << first) - 1))


def place_slots(me, total_ref, send_ref, keep_ref, first, columns=slice(None)):
    for rest in range(send_ref.shape[0]):
        for bit, ref in ((1, send_ref), (0, keep_ref)):
            ref[rest] = total_ref[slot_of(rest, bit, first) ^ me, :, columns].astype(low_type)


def grad_kernel(me_ref, left_ref, right_ref, *refs, firsts):
    total_s = refs[-1]
    total_s[...] = dot_columns(left_ref[...], right_ref[...]).reshape(total_s.shape)
    width = total_s.shape[2] // len(firsts)
    for index, first in enumerate(firsts):
        columns = slice(index * width, (index + 1) * width)
        place_slots(me_ref[0], total_s, refs[2 * index], refs[2 * index + 1], first, columns)


def grad_parts(me, left, right, devices, firsts, name):
    rows, width = left.shape[1] // devices, right.shape[1]
    half = (devices // 2, rows, width // len(firsts))
    return kernel_call(
        lambda *refs: grad_kernel(*refs, firsts=firsts),
        grid_spec=pltpu.PrefetchScalarGridSpec(
            num_scalar_prefetch=1,
            grid=(1,),
            in_specs=[whole(left.shape), whole(right.shape)],
            out_specs=[whole(half)] * (2 * len(firsts)),
            scratch_shapes=[pltpu.VMEM((devices, rows, width), sum_type)],
        ),
        out_shape=[like(half)] * (2 * len(firsts)),
        compiler_params=settings(62),
        name=name,
    )(me, left, right)


def pair_grad_kernel(me_ref, act_ref, own_ref, cos_ref, sin_ref, *refs, reach, firsts):
    pieces, refs = refs[:reach], refs[reach:]
    out_ref, total_s = refs[0], refs[-1]
    total = own_ref[...]
    for piece in pieces:
        total += piece[...].astype(sum_type)
    width = HEAD_DIMENSION
    keys = total[:, :width]
    cosine, sine = full_tables(cos_ref, sin_ref)
    turned = pltpu.roll(keys, width // 2, 1)
    pairs = jnp.concatenate([keys * cosine - turned * sine, total[:, width:]], axis=1).astype(low_type)
    out_ref[...] = pairs
    total_s[...] = dot_columns(act_ref[...], pairs).reshape(total_s.shape)
    for index, first in enumerate(firsts):
        columns = slice(index * width, (index + 1) * width)
        place_slots(me_ref[0], total_s, refs[2 * index + 1], refs[2 * index + 2], first, columns)


def pair_grads(me, act, own, pieces, cosine, sine, devices, firsts):
    rows = act.shape[1] // devices
    half = (devices // 2, rows, HEAD_DIMENSION)
    operands = (act, own, cosine, sine, *pieces)
    return kernel_call(
        lambda *refs: pair_grad_kernel(*refs, reach=len(pieces), firsts=firsts),
        grid_spec=pltpu.PrefetchScalarGridSpec(
            num_scalar_prefetch=1,
            grid=(1,),
            in_specs=[whole(operand.shape) for operand in operands],
            out_specs=[whole(own.shape)] + [whole(half)] * 4,
            scratch_shapes=[pltpu.VMEM((devices, rows, 2 * HEAD_DIMENSION), sum_type)],
        ),
        out_shape=[like(own.shape)] + [like(half)] * 4,
        compiler_params=settings(62),
        name="key_value_grad",
    )(me, *operands)


def expert_kernel(
    me_ref, act_hbm, grad_hbm, gates_ref, gate_hbm, up_hbm, down_hbm, *refs, experts, firsts, later
):
    refs = refs[2:] if later else refs
    outs, (hidden_hbm, inner_hbm), refs = refs[:6], refs[6:8], refs[8:]
    act_s, grad_s, wide_s, down_s, raw_s, back_s, hidden_s, inner_s, stage_s = refs[:9]
    act_sem, wide_sems, down_sems, pass_sems, out_sems, *total_s = refs[9:]
    rows, hidden, me = act_s.shape[0], gate_hbm.shape[2], me_ref[0]
    first_expert, count = experts

    def fetch(source, target, sem):
        copy = pltpu.make_async_copy(source, target, sem)
        copy.start()
        return copy

    def fetch_wide(expert):
        slot = expert % 2
        return [
            fetch(gate_hbm.at[first_expert + expert], wide_s.at[slot, :, :hidden], wide_sems.at[expert, 0]),
            fetch(up_hbm.at[first_expert + expert], wide_s.at[slot, :, hidden:], wide_sems.at[expert, 1]),
        ]

    def fetch_down(expert):
        pair, at = expert // 2, expert % 2 * hidden
        target = down_s.at[pair % 2, at : at + hidden]
        return [fetch(down_hbm.at[first_expert + expert], target, down_sems.at[expert])]

    def arrive(copies):
        for copy in copies:
            copy.wait()

    def pointwise(expert):
        slot = expert % 2
        at = slice(slot * hidden, (slot + 1) * hidden)
        for start in range(0, rows, 256):
            block = pl.ds(start, 256)
            inner = raw_s[slot, block, :hidden]
            up = raw_s[slot, block, hidden:]
            lane = lax.broadcasted_iota(jnp.int32, (256, LANES), 1)
            mine = lane == first_expert + expert
            gate = jnp.sum(jnp.where(mine, gates_ref[block, :], 0.0), axis=1, keepdims=True)
            square = inner * inner
            bent = jnp.tanh(tanh_scale * inner * (1.0 + tanh_cubic * square))
            half = 0.5 * (1.0 + bent)
            gelu = inner * half
            slope = half + (0.5 * tanh_scale) * inner * (1.0 - bent * bent) * (
                1.0 + (3.0 * tanh_cubic) * square
            )
            back = back_s[block, at] * gate
            hidden_s[block, at] = (gelu * up * gate).astype(low_type)
            inner_s[slot, block, :hidden] = (back * up * slope).astype(low_type)
            inner_s[slot, block, hidden:] = (back * gelu).astype(low_type)

    given = []

    def gradient(left_s, right, chain, part):
        total = dot_columns(left_s[...], right)
        columns = pl.ds(part * 2 * hidden, 2 * hidden)
        if not total_s:
            stage_s[chain, part] = total.astype(low_type).reshape(stage_s.shape[2:])
            for rest in range(stage_s.shape[2] // 2):
                for side, bit in enumerate((1, 0)):
                    source = stage_s.at[chain, part, slot_of(rest, bit, firsts[chain]) ^ me]
                    target = outs[2 * chain + side].at[rest, :, columns]
                    given.append(fetch(source, target, out_sems.at[chain, part, side]))
            return
        total_s[0][...] = total.reshape(total_s[0].shape)
        send_s, keep_s = stage_s.at[chain, part, 0], stage_s.at[chain, part, 1]
        place_slots(me, total_s[0], send_s, keep_s, firsts[chain])
        for side, source in enumerate((send_s, keep_s)):
            target = outs[2 * chain + side].at[:, :, columns]
            given.append(fetch(source, target, out_sems.at[chain, part, side]))

    wide_in = {0: fetch_wide(0)}
    head, tail = pl.ds(0, rows // 4), pl.ds(rows // 4, rows - rows // 4)
    act_in = [
        fetch(act_hbm.at[part], act_s.at[part], act_sem.at[number])
        for number, part in enumerate((head, tail))
    ]
    grad_in = [fetch(grad_hbm, grad_s, act_sem.at[2])]
    down_in = {expert: fetch_down(expert) for expert in range(2)}
    wide_in[1] = fetch_wide(1)
    for expert in range(2, min(4, count)):
        down_in[expert] = fetch_down(expert)
    passed = []
    for pair in range(count // 2):
        one, two = 2 * pair, 2 * pair + 1
        arrive(wide_in[one])
        if pair == 0:
            for part, copy in zip((head, tail), act_in):
                copy.wait()
                raw_s[0, part, :] = dot(act_s[part, :], wide_s[0])
        else:
            raw_s[0] = dot(act_s[...], wide_s[0])
        if one + 2 < count:
            wide_in[one + 2] = fetch_wide(one + 2)
        if pair == 0:
            arrive(grad_in)
        arrive(down_in[one] + down_in[two])
        back_s[...] = dot_rows(grad_s[...], down_s[pair % 2])
        arrive(wide_in[two])
        raw_s[1] = dot(act_s[...], wide_s[1])
        if two + 2 < count:
            wide_in[two + 2] = fetch_wide(two + 2)
        arrive(passed)
        pointwise(0 + one)
        chain = min(one // (count // 2), 1)
        gradient(act_s, inner_s[0], chain, one % (count // 2))
        pointwise(two)
        at = first_expert // 2 + pair
        passed = [
            fetch(hidden_s, hidden_hbm.at[at], pass_sems.at[pair, 0]),
            fetch(inner_s, inner_hbm.at[pl.ds(2 * at, 2)], pass_sems.at[pair, 1]),
        ]
        chain = min(two // (count // 2), 1)
        gradient(act_s, inner_s[1], chain, two % (count // 2))
        gradient(grad_s, hidden_s[...], 2, pair)
    arrive(passed)
    arrive(given)


def expert_group(
    experts, me, act, cotangent, gates, gate_weight, up_weight, down_weight, earlier, devices, firsts
):
    rows, model = act.shape
    hidden = gate_weight.shape[2]
    parts = experts[1] // 2
    half = (devices // 2, model // devices, 2 * hidden)
    joined = half[:2] + (parts * 2 * hidden,)
    hidden_all = like((EXPERTS // 2, rows, 2 * hidden))
    inner_all = like((EXPERTS, rows, 2 * hidden))
    later = earlier is not None
    if half[1] % 16:
        stage, totals = (3, parts, 2) + half, [pltpu.VMEM((devices,) + half[1:], sum_type)]
    else:
        stage, totals = (3, parts, devices) + half[1:], []
    return kernel_call(
        lambda *refs: expert_kernel(*refs, experts=experts, firsts=firsts, later=later),
        grid_spec=pltpu.PrefetchScalarGridSpec(
            num_scalar_prefetch=1,
            grid=(1,),
            in_specs=[any_space, any_space, whole(gates.shape)]
            + [any_space] * (3 + (2 if later else 0)),
            out_specs=[any_space] * 8,
            scratch_shapes=[
                pltpu.VMEM((rows, model), low_type),
                pltpu.VMEM((rows, model), low_type),
                pltpu.VMEM((2, model, 2 * hidden), low_type),
                pltpu.VMEM((2, 2 * hidden, model), low_type),
                pltpu.VMEM((2, rows, 2 * hidden), sum_type),
                pltpu.VMEM((rows, 2 * hidden), sum_type),
                pltpu.VMEM((rows, 2 * hidden), low_type),
                pltpu.VMEM((2, rows, 2 * hidden), low_type),
                pltpu.VMEM(stage, low_type),
                pltpu.SemaphoreType.DMA((3,)),
                pltpu.SemaphoreType.DMA((experts[1], 2)),
                pltpu.SemaphoreType.DMA((experts[1],)),
                pltpu.SemaphoreType.DMA((parts, 2)),
                pltpu.SemaphoreType.DMA((3, parts, 2)),
            ]
            + totals,
        ),
        out_shape=[like(joined)] * 6 + [hidden_all, inner_all],
        input_output_aliases={7: 6, 8: 7} if later else {},
        compiler_params=settings(62),
        name="experts",
    )(me, act, cotangent, gates, gate_weight, up_weight, down_weight, *(earlier or ()))


def inner_back_kernel(inner_ref, gate_ref, up_ref, out_ref, total_s):
    expert = pl.program_id(0)
    hidden = gate_ref.shape[2]

    @pl.when(expert == 0)
    def clear():
        total_s[...] = jnp.zeros(total_s.shape, sum_type)

    weight = jnp.concatenate([gate_ref[0], up_ref[0]], axis=1)
    total_s[...] += dot_rows(inner_ref[0], weight)

    @pl.when(expert == EXPERTS - 1)
    def finish():
        out_ref[...] = total_s[...].astype(low_type)


def inner_back(inner, gate_weight, up_weight):
    rows, model = inner.shape[1], gate_weight.shape[1]
    one = lambda shape: pl.BlockSpec((1,) + shape[1:], lambda expert: (expert, 0, 0))
    return kernel_call(
        inner_back_kernel,
        grid=(EXPERTS,),
        in_specs=[one(inner.shape), one(gate_weight.shape), one(up_weight.shape)],
        out_specs=whole((rows, model)),
        out_shape=like((rows, model)),
        scratch_shapes=[pltpu.VMEM((rows, model), sum_type)],
        compiler_params=settings(62),
        name="expert_back",
    )(inner, gate_weight, up_weight)


def expert_out_kernel(hidden_ref, down_ref, out_ref, total_s):
    pair = pl.program_id(0)

    @pl.when(pair == 0)
    def clear():
        total_s[...] = jnp.zeros(total_s.shape, sum_type)

    total_s[...] += dot(hidden_ref[0], down_ref[...])

    @pl.when(pair == EXPERTS // 2 - 1)
    def finish():
        out_ref[...] = total_s[...].astype(low_type)


def expert_out(hidden, down_weight):
    rows, model = hidden.shape[1], down_weight.shape[2]
    flat = down_weight.reshape(-1, model)
    return kernel_call(
        expert_out_kernel,
        grid=(EXPERTS // 2,),
        in_specs=[
            pl.BlockSpec((1,) + hidden.shape[1:], lambda pair: (pair, 0, 0)),
            pl.BlockSpec((hidden.shape[2], model), lambda pair: (pair, 0)),
        ],
        out_specs=whole((rows, model)),
        out_shape=like((rows, model)),
        scratch_shapes=[pltpu.VMEM((rows, model), sum_type)],
        compiler_params=settings(62),
        name="expert_out",
    )(hidden, flat)


def shifted(shard, by):
    size = lax.axis_size("ctx")
    return lax.ppermute(
        shard, "ctx", [(i, i + by) for i in range(size) if 0 <= i + by < size]
    )


def swapped(part):
    return lax.ppermute(part, "ws", [(0, 1), (1, 0)])


def without(slot, bits):
    for bit in sorted(bits, reverse=True):
        slot = ((slot >> (bit + 1)) << bit) | (slot & ((1 << bit) - 1))
    return slot


def with_zeros(index, bits):
    for bit in sorted(bits):
        index = ((index >> bit) << (bit + 1)) | (index & ((1 << bit) - 1))
    return index


def flip(array, bit):
    size = lax.axis_size("ctx")
    return lax.ppermute(array, "ctx", [(i, i ^ (1 << bit)) for i in range(size)])


class Chains:
    def __init__(self, orders):
        self.orders = orders
        self.sections = [[] for _ in orders]
        self.joined = [[] for _ in orders]
        self.done = 1
        self.waiting = None

    def first_steps(self, sends, keeps):
        self.keeps = keeps
        return [flip(send, order[0]) for send, order in zip(sends, self.orders)]

    def land(self, arrived):
        for chain, part in enumerate(arrived):
            held = self.orders[chain][:1]
            self.sections[chain].append([(self.keeps[chain], held, 0), (part, held, 0)])

    def widths(self, chain):
        return [parts[0][0].shape[2] for parts in self.sections[chain]]

    def ending(self):
        return self.done == len(self.orders[0])

    def arrays(self, chains=None):
        flat = []
        for chain in range(len(self.orders)) if chains is None else chains:
            for parts in self.sections[chain]:
                flat += parts
            flat += self.joined[chain]
        return flat

    def replace(self, arrays, chains=None):
        arrays = iter(arrays)
        fresh = lambda parts: [(next(arrays), held, column) for _, held, column in parts]
        for chain in range(len(self.orders)) if chains is None else chains:
            self.sections[chain] = [fresh(parts) for parts in self.sections[chain]]
            self.joined[chain] = fresh(self.joined[chain])

    @staticmethod
    def totals(refs, sections, joined):
        own = [[next(refs) for _ in parts] for parts in sections]
        shared = [(next(refs), column) for _, _, column in joined]
        at, found = 0, []
        for parts, refs_of in zip(sections, own):
            width = parts[0][0].shape[2]
            total = refs_of[0][0].astype(sum_type)
            for ref, (_, _, column) in zip(refs_of[1:], parts[1:]):
                total += ref[0, :, column : column + width].astype(sum_type)
            for ref, column in shared:
                total += ref[0, :, column + at : column + at + width].astype(sum_type)
            found.append(total)
            at += width
        return found

    def sums(self, refs, chains=None):
        refs = iter(refs)
        return [
            self.totals(refs, self.sections[chain], self.joined[chain])
            for chain in (range(len(self.orders)) if chains is None else chains)
        ]

    @staticmethod
    def sum_call(groups, parts_of, done_count, bits, done_bits):
        slots = lax.axis_size("ctx") >> (done_count + 1)
        specs, operands, shapes, chain = [], [], [], 0
        for group in groups:
            width = 0
            for sections, joined in group:
                for array, held, _ in parts_of[chain]:

                    def index(tile, done=done_bits[chain], bit=bits[chain], held=held):
                        slot = with_zeros(tile, list(done) + [bit]) | (1 << bit)
                        return (without(slot, held), 0, 0)

                    specs.append(pl.BlockSpec((1,) + array.shape[1:], index))
                    operands.append(array)
                width += sum(parts[0][0].shape[2] for parts in sections)
                rows = sections[0][0][0].shape[1]
                chain += 1
            shapes.append((slots, rows, width))

        def run(*refs):
            reading, outs = iter(refs[: len(operands)]), refs[len(operands) :]
            for out, group in zip(outs, groups):
                at = 0
                for sections, joined in group:
                    for total in Chains.totals(reading, sections, joined):
                        out[0, :, at : at + total.shape[1]] = total.astype(low_type)
                        at += total.shape[1]

        return kernel_call(
            run,
            grid=(slots,),
            in_specs=specs,
            out_specs=[pl.BlockSpec((1,) + shape[1:], lambda tile: (tile, 0, 0)) for shape in shapes],
            out_shape=[like(shape) for shape in shapes],
            compiler_params=settings(62),
            name="sum_parts",
        )(*operands)

    def alike(self, chains):
        bits = [self.orders[chain][self.done] for chain in chains]
        return [
            (bit, [chain for chain, other in zip(chains, bits) if other == bit])
            for bit in dict.fromkeys(bits)
        ]

    def prepare(self, apart=False):
        chains = range(len(self.orders))
        self.groups = self.alike(chains)
        if apart:
            self.groups = [(self.orders[chain][self.done], [chain]) for chain in chains]
        order = [chain for _, group in self.groups for chain in group]
        self.waiting = self.sum_call(
            [[(self.sections[chain], self.joined[chain]) for chain in group] for _, group in self.groups],
            [self.arrays([chain]) for chain in order],
            self.done,
            [self.orders[chain][self.done] for chain in order],
            [self.orders[chain][: self.done] for chain in order],
        )

    def launch(self, count=None):
        count = len(self.waiting) if count is None else count
        for send, (bit, group) in zip(self.waiting[:count], self.groups[:count]):
            array, column = flip(send, bit), 0
            for chain in group:
                held = self.orders[chain][: self.done + 1]
                self.joined[chain].append((array, held, column))
                column += sum(self.widths(chain))
        self.waiting, self.groups = self.waiting[count:], self.groups[count:]
        if not self.groups:
            self.done += 1


def end_experts(chains, hidden):
    parts = chains.arrays()
    rows = parts[0][0].shape[1]
    shapes = [(EXPERTS, rows, hidden)] * 3

    def run(*refs):
        gate_ref, up_ref, down_ref = refs[len(parts) :]
        totals = chains.sums(refs[: len(parts)])
        for pair in range(EXPERTS // 2):
            for chain in range(2):
                gate_ref[2 * pair + chain] = totals[chain][pair][:, :hidden]
                up_ref[2 * pair + chain] = totals[chain][pair][:, hidden:]
                columns = slice(chain * hidden, (chain + 1) * hidden)
                down_ref[2 * pair + chain] = totals[2][pair][:, columns]

    return kernel_call(
        run,
        grid=(1,),
        in_specs=[
            pl.BlockSpec((1,) + array.shape[1:], lambda tile: (0, 0, 0)) for array, _, _ in parts
        ],
        out_specs=[whole(shape) for shape in shapes],
        out_shape=[like(shape, sum_type) for shape in shapes],
        compiler_params=settings(62),
        name="expert_gradients",
    )(*[array for array, _, _ in parts])


def end_others(chains):
    parts = chains.arrays()
    rows = parts[0][0].shape[1]
    count = len(chains.orders)
    out_width = sum(chains.widths(chain)[0] for chain in range(count))
    shapes = [
        (rows, out_width),
        (rows, sum(chains.widths(chain)[1] for chain in range(count))),
        (rows, chains.widths(0)[2]),
        (rows, chains.widths(1)[2]),
    ]

    def run(*refs):
        out_ref, query_ref, key_ref, value_ref = refs[len(parts) :]
        totals = chains.sums(refs[: len(parts)])
        at = 0
        for found in totals:
            width = found[0].shape[1]
            out_ref[:, at : at + width] = found[0]
            query_ref[:, at : at + width] = found[1]
            at += width
        key_ref[...] = totals[0][2]
        value_ref[...] = totals[1][2]

    return kernel_call(
        run,
        grid=(1,),
        in_specs=[
            pl.BlockSpec((1,) + array.shape[1:], lambda tile: (0, 0, 0)) for array, _, _ in parts
        ],
        out_specs=[whole(shape) for shape in shapes],
        out_shape=[like(shape, sum_type) for shape in shapes],
        compiler_params=settings(62),
        name="other_gradients",
    )(*[array for array, _, _ in parts])


def tie(*values):
    return lax.optimization_barrier(values)


def advance(chains, anchor):
    if chains.ending():
        return anchor
    anchor = settle(chains, anchor)
    chains.prepare()
    anchor, chains.waiting = tie(anchor, chains.waiting)
    chains.launch()
    return anchor


def chain_arrays(chains, some=None):
    return [array for array, _, _ in chains.arrays(some)]


def settle(chains, anchor, some=None):
    anchor, arrays = tie(anchor, chain_arrays(chains, some))
    chains.replace(arrays, some)
    return anchor


def chain_orders(bits):
    rest = tuple(range(3, bits))
    return ((0, 1, 2) + rest, (1, 2, 0) + rest, (2, 0, 1) + rest)


def body(
    tokens,
    cotangent,
    first_gain,
    query_weight,
    key_projection_weight,
    value_projection_weight,
    out_weight,
    second_gain,
    gate_weight,
    up_weight,
    down_weight,
    segments,
    live_mask,
    routes,
    gate_values,
):
    rows, model = tokens.shape
    devices = lax.axis_size("ctx")
    bits = devices.bit_length() - 1
    index = lax.axis_index("ctx")
    me = index.astype(jnp.int32).reshape(1)
    first_row = index * rows
    query_block, key_block = 256, 256
    gain_one, gain_two = first_gain[None, :], second_gain[None, :]
    orders = chain_orders(bits)
    firsts = tuple(order[0] for order in orders)

    half = HEAD_DIMENSION // 2
    frequency = rope_base ** (-2.0 * jnp.arange(half, dtype=sum_type) / HEAD_DIMENSION)
    positions = (first_row + jnp.arange(rows, dtype=jnp.int32)).astype(sum_type)
    angles = frequency[:, None] * positions[None, :]
    cosine, sine = jnp.cos(angles), jnp.sin(angles)

    activation, own_pair = project_keys(
        tokens, gain_one, key_projection_weight, value_projection_weight, cosine, sine
    )
    reach = min(devices, (DOC_MAX + rows - 2) // rows + 1)
    pieces = [shifted(own_pair, by) for by in range(reach - 1, 0, -1)] + [own_pair]
    queries = project_queries(activation, query_weight, cosine, sine)
    span = reach * rows
    own_at = span - rows
    padded_segments = jnp.concatenate([jnp.full((own_at,), -1, jnp.int32), segments])
    padded_live = jnp.concatenate([jnp.zeros((own_at,), jnp.int32), live_mask])
    key_segments = lax.dynamic_slice_in_dim(padded_segments, first_row, span, 0)
    key_live = lax.dynamic_slice_in_dim(padded_live, first_row, span, 0)
    place, low, gates = tables(
        key_segments[:, None], key_segments[None, own_at:], key_live[:, None], routes, gate_values
    )
    first_block = (low[0, ::query_block] + own_at) // key_block
    queries, gates, low, place, first_block = tie(queries, gates, low, place, first_block)

    mixed_turned, mixed, logs = attend(
        first_block, queries, pieces, place, low, query_block, key_block
    )
    part = product(mixed, out_weight, "attention_out")
    residual, act_two = second_norm(tokens, part, swapped(part), gain_two)

    hidden = gate_weight.shape[2]
    experts = Chains(orders)
    earlier, flying = None, []
    for pair in range(EXPERTS // 2):
        outs = expert_group(
            (2 * pair, 2), me, act_two, cotangent, gates, gate_weight, up_weight, down_weight, earlier,
            devices, firsts,
        )
        earlier = outs[-2:]
        act_two, earlier, sends, landed = tie(act_two, earlier, outs[0:6:2], flying)
        if pair:
            experts.land(landed)
        flying = experts.first_steps(sends, outs[1:6:2])
    hidden_all, inner_all = earlier
    back = inner_back(inner_all, gate_weight, up_weight)
    back, landed = tie(back, flying)
    experts.land(landed)
    back_other = swapped(back)
    back = advance(experts, back)
    total, total_low, grad_heads = second_back(
        back, back_other, residual, cotangent, gain_two, out_weight
    )
    rest = tuple(range(3, bits))
    others = Chains(((0, 1, 2) + rest, (1, 0, 2) + rest))
    other_firsts = (0, 1)
    outs = grad_parts(me, total_low, mixed, devices, other_firsts, "out_grad")
    grad_heads, outs = tie(grad_heads, outs)
    flying = others.first_steps(outs[0:4:2], outs[1:4:2])

    tiles = rows // query_block
    back_args = (
        queries, pieces, place, low, mixed_turned, grad_heads, logs, cosine, sine, query_block, key_block
    )
    sums = attend_back(first_block, *back_args, (0, tiles // 2), None)
    sums = advance(experts, sums)
    grad_queries, *far, own = attend_back(first_block, *back_args, (tiles // 2, tiles), sums)
    far, grad_queries = settle(experts, (far, grad_queries))
    returned = [shifted(piece, at + 1 - reach) for at, piece in enumerate(far)]
    while experts.done + 1 < bits:
        grad_queries = advance(experts, grad_queries)
    experts.prepare(apart=True)
    query_outs = grad_parts(me, activation, grad_queries, devices, other_firsts, "query_grad")
    own, returned, query_outs, experts.waiting, landed = tie(
        own, returned, query_outs, experts.waiting, flying
    )
    others.land(landed)
    flying = others.first_steps(query_outs[0:4:2], query_outs[1:4:2])
    query_keeps = others.keeps
    experts.launch(1)
    grad_pairs, *outs = pair_grads(
        me, activation, own, returned, cosine, sine, devices, other_firsts
    )
    grad_pairs, outs = tie(grad_pairs, outs)
    pair_flying = others.first_steps(outs[0:4:2], outs[1:4:2])
    pair_keeps = others.keeps
    grad_act = act_back(
        grad_queries, grad_pairs, query_weight, key_projection_weight, value_projection_weight
    )
    grad_act, landed, pair_landed = tie(grad_act, flying, pair_flying)
    others.keeps = query_keeps
    others.land(landed)
    others.keeps = pair_keeps
    others.land(pair_landed)
    grad_act = settle(experts, grad_act, (0,))
    grad_act, experts.waiting = tie(grad_act, experts.waiting)
    experts.launch(1)
    act_other = swapped(grad_act)
    hidden_all = advance(others, hidden_all)
    out_part = expert_out(hidden_all, down_weight)
    out_part, grad_act, act_other, expert_arrays, other_arrays = tie(
        out_part, grad_act, act_other, chain_arrays(experts, (1,)), chain_arrays(others)
    )
    experts.replace(expert_arrays, (1,))
    others.replace(other_arrays)
    out_part, experts.waiting = tie(out_part, experts.waiting)
    experts.launch()
    out_other = swapped(out_part)
    out_part = advance(others, out_part)
    token_grad, output = last_rows(
        grad_act, act_other, tokens, total, gain_one, residual, out_part, out_other
    )
    token_grad = settle(experts, token_grad)
    token_grad = advance(others, token_grad)
    own_rows = model // devices
    gate_grad, up_grad, down_grad = end_experts(experts, hidden)
    while not others.ending():
        token_grad = advance(others, token_grad)
    down_grad = down_grad.transpose(0, 2, 1)
    out_turned, query_grad, key_grad, value_grad = end_others(others)
    out_grad = out_turned.T

    def own_part(weight, dimension=0):
        return lax.dynamic_slice_in_dim(weight, index * own_rows, own_rows, dimension).astype(sum_type)

    first_part = (
        jnp.sum(query_grad * own_part(query_weight), axis=1)
        + jnp.sum(key_grad * own_part(key_projection_weight), axis=1)
        + jnp.sum(value_grad * own_part(value_projection_weight), axis=1)
    )
    second_part = jnp.sum(
        gate_grad * own_part(gate_weight, 1) + up_grad * own_part(up_weight, 1), axis=(0, 2)
    )
    gain_parts = jnp.stack([first_part, second_part])
    gains = jnp.stack([first_gain, second_gain])
    gain_grads = (gain_parts + swapped(gain_parts)) / lax.dynamic_slice_in_dim(
        gains, index * own_rows, own_rows, 1
    )
    grad_first, grad_second = gain_grads[0], gain_grads[1]
    return (
        output,
        token_grad,
        grad_first,
        query_grad,
        key_grad,
        value_grad,
        out_grad,
        grad_second,
        gate_grad,
        up_grad,
        down_grad,
    )


def solution(mesh):
    return jax.shard_map(
        body,
        mesh=mesh,
        in_specs=(
            P("ctx", None),
            P("ctx", None),
            P(),
            P(None, "ws"),
            P(None, "ws"),
            P(None, "ws"),
            P("ws", None),
            P(),
            P(None, None, "ws"),
            P(None, None, "ws"),
            P(None, "ws", None),
            P(),
            P(),
            P("ctx", None),
            P("ctx", None),
        ),
        out_specs=(
            P("ctx", None),
            P("ctx", None),
            P("ctx"),
            P("ctx", "ws"),
            P("ctx", "ws"),
            P("ctx", "ws"),
            P("ws", "ctx"),
            P("ctx"),
            P(None, "ctx", "ws"),
            P(None, "ctx", "ws"),
            P(None, "ws", "ctx"),
        ),
        check_vma=False,
    )
```

```python
import jax
import jax.numpy as jnp
from jax import lax
from jax.experimental import pallas as pl
from jax.experimental.pallas import tpu as pltpu
from jax.sharding import PartitionSpec as P

HEAD_DIMENSION = 128
EXPERTS = 8
DOC_MAX = 2000
CAP = 640
LANES = 128

eps = 1e-06
rope_base = 1000000.0
masked_score = -1e30
far_position = 1 << 30
log2_e = 1.4426950408889634
tanh_scale = 0.7978845608028654
tanh_cubic = 0.044715

low_type = jnp.bfloat16
sum_type = jnp.float32
any_space = pl.BlockSpec(memory_space=pl.ANY)


def dot(left, right):
    return jnp.dot(left, right, preferred_element_type=sum_type)


def dot_rows(left, right):
    return lax.dot_general(left, right, (((1,), (1,)), ((), ())), preferred_element_type=sum_type)


def dot_columns(left, right):
    return lax.dot_general(left, right, (((0,), (0,)), ((), ())), preferred_element_type=sum_type)


def whole(shape):
    return pl.BlockSpec(shape, lambda *index: (0,) * len(shape))


def by_rows(block, shape):
    return pl.BlockSpec((block,) + shape[1:], lambda row, *rest: (row,) + (0,) * (len(shape) - 1))


def like(shape, kind=low_type):
    return jax.ShapeDtypeStruct(shape, kind)


def settings(megabytes):
    return pltpu.CompilerParams(vmem_limit_bytes=megabytes * 2**20)


light = pl.CostEstimate(flops=1000, transcendentals=0, bytes_accessed=1000)


def kernel_call(body, **options):
    return pl.pallas_call(body, cost_estimate=light, **options)


def normalize(value):
    factor = lax.rsqrt(jnp.mean(value * value, axis=-1, keepdims=True) + eps)
    return value * factor, factor


def normalize_back(grad_normed, normed, factor):
    return factor * (grad_normed - normed * jnp.mean(grad_normed * normed, axis=-1, keepdims=True))


def table_kernel(
    segment_ref, own_segment_ref, live_ref, route_ref, value_ref, place_ref, low_ref, gates_ref
):
    span, own_at = segment_ref.shape[0], segment_ref.shape[0] - own_segment_ref.shape[1]
    rows = own_segment_ref.shape[1]
    before = (segment_ref[...] < own_segment_ref[...]).astype(jnp.int32)
    low_ref[...] = jnp.sum(before, axis=0, keepdims=True) - own_at
    position = lax.broadcasted_iota(jnp.int32, (span, LANES), 0) - own_at
    live = jnp.broadcast_to(live_ref[...], (span, LANES)) == 1
    place_ref[...] = jnp.where(live, position, far_position)
    lane = lax.broadcasted_iota(jnp.int32, (rows, LANES), 1)
    chosen = jnp.zeros((rows, LANES), sum_type)
    gates = jnp.zeros((rows, LANES), sum_type)
    for top in range(route_ref.shape[1]):
        here = lane == route_ref[:, top : top + 1]
        chosen = jnp.where(here, 1.0, chosen)
        gates = jnp.where(here, value_ref[:, top : top + 1], gates)
    chosen = jnp.where(live[own_at:], chosen, 0.0)
    earlier = lax.broadcasted_iota(jnp.int32, (rows, rows), 1) < lax.broadcasted_iota(
        jnp.int32, (rows, rows), 0
    )
    rank = dot(earlier.astype(low_type), chosen.astype(low_type))
    gates_ref[...] = jnp.where((chosen > 0.5) & (rank < CAP), gates, 0.0)


def tables(key_segments, own_segments, key_live, routes, gate_values):
    span, rows = key_segments.shape[0], own_segments.shape[1]
    shapes = [like((span, LANES), jnp.int32), like((1, rows), jnp.int32), like((rows, LANES), sum_type)]
    operands = (key_segments, own_segments, key_live, routes, gate_values)
    return kernel_call(
        table_kernel,
        grid=(1,),
        in_specs=[whole(operand.shape) for operand in operands],
        out_specs=[whole(shape.shape) for shape in shapes],
        out_shape=shapes,
        compiler_params=settings(32),
        name="tables",
    )(*operands)


def full_tables(cos_ref, sin_ref):
    cosine, sine = cos_ref[...].T, sin_ref[...].T
    return jnp.concatenate([cosine, cosine], axis=1), jnp.concatenate([-sine, sine], axis=1)


def key_value_kernel(token_ref, gain_ref, key_ref, value_ref, cos_ref, sin_ref, act_ref, out_ref):
    normed, factor = normalize(token_ref[...].astype(sum_type))
    act = (normed * gain_ref[...]).astype(low_type)
    act_ref[...] = act
    keys = dot(act, key_ref[...])
    width = keys.shape[1]
    cosine, sine = full_tables(cos_ref, sin_ref)
    turned = pltpu.roll(keys, HEAD_DIMENSION // 2, 1)
    out_ref[:, :width] = (keys * cosine + turned * sine).astype(low_type)
    out_ref[:, width:] = dot(act, value_ref[...]).astype(low_type)


def project_keys(tokens, gain, key_weight, value_weight, cosine, sine, block=256):
    rows, width = tokens.shape
    joined = key_weight.shape[1] + value_weight.shape[1]
    columns = pl.BlockSpec((cosine.shape[0], block), lambda row: (0, row))
    return kernel_call(
        key_value_kernel,
        grid=(rows // block,),
        in_specs=[
            by_rows(block, tokens.shape),
            whole((1, width)),
            whole(key_weight.shape),
            whole(value_weight.shape),
            columns,
            columns,
        ],
        out_specs=[by_rows(block, (rows, width)), by_rows(block, (rows, joined))],
        out_shape=[like((rows, width)), like((rows, joined))],
        compiler_params=settings(62),
        name="norm_keys_values",
    )(tokens, gain, key_weight, value_weight, cosine, sine)


def query_kernel(act_ref, weight_ref, cos_ref, sin_ref, out_ref):
    raw = dot(act_ref[...], weight_ref[...])
    half = HEAD_DIMENSION // 2
    cosine, sine = cos_ref[...], sin_ref[...]
    for head in range(out_ref.shape[0]):
        part = raw[:, head * HEAD_DIMENSION : (head + 1) * HEAD_DIMENSION].T
        one, two = part[:half], part[half:]
        out_ref[head, :half] = (one * cosine - two * sine).astype(low_type)
        out_ref[head, half:] = (two * cosine + one * sine).astype(low_type)


def project_queries(act, weight, cosine, sine, block=256):
    rows, width = act.shape
    heads = weight.shape[1] // HEAD_DIMENSION
    half = HEAD_DIMENSION // 2
    columns = pl.BlockSpec((half, block), lambda row: (0, row))
    return kernel_call(
        query_kernel,
        grid=(rows // block,),
        in_specs=[by_rows(block, act.shape), whole(weight.shape), columns, columns],
        out_specs=pl.BlockSpec((heads, HEAD_DIMENSION, block), lambda row: (0, 0, row)),
        out_shape=like((heads, HEAD_DIMENSION, rows)),
        compiler_params=settings(32),
        name="queries",
    )(act, weight, cosine, sine)


def repeat_lanes(block, times):
    return jnp.concatenate([block] * times, axis=1) if times > 1 else block


def join_heads(ref):
    return jnp.concatenate([ref[head] for head in range(ref.shape[0])], axis=1)


def pair_bias(place_ref, rows, low, high, start, own_at, own):
    place = repeat_lanes(place_ref[rows, :], low.shape[1] // LANES)
    allowed = (place >= low) & (place <= high)
    if own:
        position = start - own_at + lax.broadcasted_iota(jnp.int32, place.shape, 0)
        allowed = allowed | (position == high)
    return jnp.where(allowed, 0.0, masked_score)


def over_keys(first_ref, step, own_at, query_block, key_block, tile):
    own_first = (own_at + tile * query_block) // key_block
    for extra in range(max(1, query_block // key_block)):
        step(own_first + extra, True)

    def loop(index, carried):
        step(index, False)
        return carried

    lax.fori_loop(first_ref[tile], own_first, loop, 0)


def mix_kernel(
    first_ref, query_ref, place_ref, low_ref, weight_ref, *refs, key_block, own_at, scale,
):
    pieces, (out_ref, mixed_ref, log_ref, part_ref) = refs[:-9], refs[-9:-5]
    key_s, value_s, max_s, sum_s, mix_s = refs[-5:]
    heads, depth, query_block = query_ref.shape
    count = heads * query_block
    tile = pl.program_id(0)

    @pl.when(tile == 0)
    def gather():
        for number, piece in enumerate(pieces):
            at = slice(number * piece.shape[0], (number + 1) * piece.shape[0])
            key_s[at, :] = piece[:, :depth]
            value_s[:, at] = piece[:, depth:].astype(sum_type).T.astype(low_type)

    queries = join_heads(query_ref)
    low = low_ref[...]
    high = tile * query_block + lax.broadcasted_iota(jnp.int32, (1, query_block), 1)
    max_s[...] = jnp.full(max_s.shape, masked_score, sum_type)
    sum_s[...] = jnp.zeros(sum_s.shape, sum_type)
    mix_s[...] = jnp.zeros(mix_s.shape, sum_type)

    def step(index, own):
        start = pl.multiple_of(index * key_block, key_block)
        rows = pl.ds(start, key_block)
        keys, values = key_s[rows, :], value_s[:, rows]
        bias = pair_bias(place_ref, rows, low, high, start, own_at, own)
        groups = 3
        width = heads // groups * query_block
        wide_bias = repeat_lanes(bias, heads // groups)
        raws = [dot(keys, queries[:, g * width : (g + 1) * width]) for g in range(groups)]
        for group, raw in enumerate(raws):
            at = slice(group * width, (group + 1) * width)
            scores = raw * (scale * log2_e) + wide_bias
            old = max_s[:, at]
            new = jnp.maximum(old, jnp.max(scores, axis=0, keepdims=True))
            weights = jnp.exp2(scores - new)
            fade = jnp.exp2(old - new)
            sum_s[:, at] = sum_s[:, at] * fade + jnp.sum(weights, axis=0, keepdims=True)
            max_s[:, at] = new
            mix_s[:, at] = mix_s[:, at] * fade + dot(values, weights.astype(low_type))

    over_keys(first_ref, step, own_at, query_block, key_block, tile)
    total = sum_s[...]
    mixed = mix_s[...] * (1.0 / total)
    logs = max_s[...] + jnp.log2(total)
    for head in range(heads):
        at = slice(head * query_block, (head + 1) * query_block)
        out_ref[head] = mixed[:, at]
        mixed_ref[:, head * depth : (head + 1) * depth] = mixed[:, at].T.astype(low_type)
        log_ref[head] = logs[:, at]
    part_ref[...] = dot(mixed_ref[...], weight_ref[...]).astype(low_type)


def tile_of(query_block):
    def column(shape):
        return pl.BlockSpec(
            shape[:-1] + (query_block,), lambda tile, *rest: (0,) * (len(shape) - 1) + (tile,)
        )

    return column


def attend(first, queries, pieces, place, low, out_weight, query_block, key_block):
    heads, depth, rows = queries.shape
    column = tile_of(query_block)
    count = heads * query_block
    span = place.shape[0]
    return kernel_call(
        lambda *refs: mix_kernel(*refs, key_block=key_block, own_at=span - rows, scale=depth**-0.5),
        grid_spec=pltpu.PrefetchScalarGridSpec(
            num_scalar_prefetch=1,
            grid=(rows // query_block,),
            in_specs=[column(queries.shape), whole(place.shape), column(low.shape), whole(out_weight.shape)]
            + [whole(piece.shape) for piece in pieces],
            out_specs=[
                column(queries.shape),
                by_rows(query_block, (rows, heads * depth)),
                column((heads, 1, rows)),
                by_rows(query_block, (rows, out_weight.shape[1])),
            ],
            scratch_shapes=[
                pltpu.VMEM((span, depth), low_type),
                pltpu.VMEM((depth, span), low_type),
                pltpu.VMEM((1, count), sum_type),
                pltpu.VMEM((1, count), sum_type),
                pltpu.VMEM((depth, count), sum_type),
            ],
        ),
        out_shape=[
            like(queries.shape, sum_type),
            like((rows, heads * depth)),
            like((heads, 1, rows), sum_type),
            like((rows, out_weight.shape[1])),
        ],
        compiler_params=settings(62),
        name="attention",
    )(first, queries, place, low, out_weight, *pieces)


def mix_back_kernel(
    first_ref, query_ref, place_ref, low_ref, mixed_ref, grad_ref, log_ref, cos_ref, sin_ref, *refs,
    reach, key_block, own_at, scale, tiles, offset, final,
):
    pieces, refs = refs[:reach], refs[reach:]
    earlier, refs = (refs[:2], refs[3:]) if offset else ((), refs)
    out_ref, *end_refs = refs[:-6]
    key_s, turned_s, value_s, query_sum, key_sum, value_sum = refs[-6:]
    heads, depth, query_block = query_ref.shape
    tile = pl.program_id(0) + offset
    queries, grads, logs = join_heads(query_ref), join_heads(grad_ref), join_heads(log_ref)
    delta = jnp.sum(grads.astype(sum_type) * join_heads(mixed_ref), axis=0, keepdims=True)
    low = low_ref[...]
    high = tile * query_block + lax.broadcasted_iota(jnp.int32, (1, query_block), 1)

    @pl.when(pl.program_id(0) == 0)
    def gather():
        for number, piece in enumerate(pieces):
            at = slice(number * piece.shape[0], (number + 1) * piece.shape[0])
            key_s[at, :] = piece[:, :depth]
            turned_s[:, at] = piece[:, :depth].astype(sum_type).T.astype(low_type)
            value_s[at, :] = piece[:, depth:]
        if offset:
            key_sum[...] = earlier[0][...]
            value_sum[...] = earlier[1][...]
        else:
            key_sum[...] = jnp.zeros(key_sum.shape, sum_type)
            value_sum[...] = jnp.zeros(value_sum.shape, sum_type)

    query_sum[...] = jnp.zeros(query_sum.shape, sum_type)

    def step(index, own):
        start = pl.multiple_of(index * key_block, key_block)
        rows = pl.ds(start, key_block)
        keys, values, turned = key_s[rows, :], value_s[rows, :], turned_s[:, rows]
        bias = pair_bias(place_ref, rows, low, high, start, own_at, own)
        groups = 3
        width = heads // groups * query_block
        wide_bias = repeat_lanes(bias, heads // groups)
        parts = [slice(g * width, (g + 1) * width) for g in range(groups)]
        raws = [(dot(keys, queries[:, at]), dot(values, grads[:, at])) for at in parts]
        for at, (raw, grad_weights) in zip(parts, raws):
            weights = jnp.exp2(raw * (scale * log2_e) + (wide_bias - logs[:, at]))
            grad_scores = (weights * (grad_weights - delta[:, at])).astype(low_type)
            value_sum[rows, :] += dot_rows(weights.astype(low_type), grads[:, at])
            key_sum[rows, :] += dot_rows(grad_scores, queries[:, at])
            query_sum[:, at] += dot(turned, grad_scores)

    over_keys(first_ref, step, own_at, query_block, key_block, tile)
    half = depth // 2
    cosine, sine = repeat_lanes(cos_ref[...], heads), repeat_lanes(sin_ref[...], heads)
    grad_query = query_sum[...] * scale
    one, two = grad_query[:half], grad_query[half:]
    turned = jnp.concatenate([one * cosine + two * sine, two * cosine - one * sine], axis=0)
    for head in range(heads):
        part = turned[:, head * query_block : (head + 1) * query_block]
        out_ref[:, head * depth : (head + 1) * depth] = part.T.astype(low_type)

    @pl.when(pl.program_id(0) == tiles - 1)
    def finish():
        if final:
            for number, ref in enumerate(end_refs):
                at = slice(number * ref.shape[0], (number + 1) * ref.shape[0])
                ref[:, :depth] = (key_sum[at, :] * scale).astype(ref.dtype)
                ref[:, depth:] = value_sum[at, :].astype(ref.dtype)
        else:
            end_refs[0][...] = key_sum[...]
            end_refs[1][...] = value_sum[...]


def attend_back(
    first, queries, pieces, place, low, mixed, grads, logs, cosine, sine, query_block, key_block, part, earlier
):
    heads, depth, rows = queries.shape
    span = place.shape[0]
    offset, tiles = part[0], part[1] - part[0]
    final = part[1] * query_block == rows

    def column(shape):
        return pl.BlockSpec(
            shape[:-1] + (query_block,),
            lambda tile, *rest: (0,) * (len(shape) - 1) + (tile + offset,),
        )

    extra = [whole((span, depth)), whole((span, depth)), any_space] if offset else []
    ends = (
        [like((rows, 2 * depth))] * (len(pieces) - 1) + [like((rows, 2 * depth), sum_type)]
        if final
        else [like((span, depth), sum_type)] * 2
    )
    operands = [queries, place, low, mixed, grads, logs, cosine, sine, *pieces]
    return kernel_call(
        lambda *refs: mix_back_kernel(
            *refs,
            reach=len(pieces),
            key_block=key_block,
            own_at=span - rows,
            scale=depth**-0.5,
            tiles=tiles,
            offset=offset,
            final=final,
        ),
        grid_spec=pltpu.PrefetchScalarGridSpec(
            num_scalar_prefetch=1,
            grid=(tiles,),
            in_specs=[
                column(queries.shape),
                whole(place.shape),
                column(low.shape),
                column(mixed.shape),
                column(grads.shape),
                column(logs.shape),
                column(cosine.shape),
                column(sine.shape),
            ]
            + [whole(piece.shape) for piece in pieces]
            + extra,
            out_specs=[
                pl.BlockSpec((query_block, heads * depth), lambda tile, *rest: (tile + offset, 0)),
                *[whole(end.shape) for end in ends],
            ],
            scratch_shapes=[
                pltpu.VMEM((span, depth), low_type),
                pltpu.VMEM((depth, span), low_type),
                pltpu.VMEM((span, depth), low_type),
                pltpu.VMEM((depth, heads * query_block), sum_type),
                pltpu.VMEM((span, depth), sum_type),
                pltpu.VMEM((span, depth), sum_type),
            ],
        ),
        out_shape=[like((rows, heads * depth)), *ends],
        input_output_aliases={len(operands) + 3: 0} if offset else {},
        compiler_params=settings(62),
        name="attention_back",
    )(first, *operands, *(((earlier[1], earlier[2], earlier[0])) if offset else ()))


def residual_of(token_ref, own_ref, other_ref):
    mixed = own_ref[...].astype(sum_type) + other_ref[...].astype(sum_type)
    return token_ref[...].astype(sum_type) + mixed


def second_norm_kernel(token_ref, own_ref, other_ref, gain_ref, act_ref):
    residual = residual_of(token_ref, own_ref, other_ref)
    act_ref[...] = (normalize(residual)[0] * gain_ref[...]).astype(low_type)


def second_norm(tokens, own, other, gain, block=256):
    rows = by_rows(block, tokens.shape)
    return kernel_call(
        second_norm_kernel,
        grid=(tokens.shape[0] // block,),
        in_specs=[rows, rows, rows, whole(gain.shape)],
        out_specs=rows,
        out_shape=like(tokens.shape),
        compiler_params=settings(62),
        name="residual_norm",
    )(tokens, own, other, gain)


def second_back_kernel(
    own_ref, other_ref, token_ref, part_ref, part_other_ref, grad_ref, gain_ref, weight_ref,
    total_ref, low_ref, heads_ref,
):
    grad_act = own_ref[...].astype(sum_type) + other_ref[...].astype(sum_type)
    normed, factor = normalize(residual_of(token_ref, part_ref, part_other_ref))

    total = grad_ref[...].astype(sum_type) + normalize_back(
        grad_act * gain_ref[...], normed, factor
    )
    total_ref[...] = total
    low = total.astype(low_type)
    low_ref[...] = low
    turned = dot_rows(weight_ref[...], low).astype(low_type)
    heads_ref[...] = turned.reshape(heads_ref.shape)


def second_back(own, other, residual_parts, cotangent, gain, out_weight, block=256):
    rows = by_rows(block, own.shape)
    heads = out_weight.shape[0] // HEAD_DIMENSION
    shape = (heads, HEAD_DIMENSION, own.shape[0])
    return kernel_call(
        second_back_kernel,
        grid=(own.shape[0] // block,),
        in_specs=[rows] * 6 + [whole(gain.shape), whole(out_weight.shape)],
        out_specs=[rows, rows, tile_of(block)(shape)],
        out_shape=[like(own.shape, sum_type), like(own.shape), like(shape)],
        compiler_params=settings(62),
        name="residual_back",
    )(own, other, *residual_parts, cotangent, gain, out_weight)


def act_back_kernel(query_ref, pair_ref, query_weight_ref, key_weight_ref, value_weight_ref, out_ref):
    width = key_weight_ref.shape[1]
    total = dot_rows(query_ref[...], query_weight_ref[...])
    total += dot_rows(pair_ref[:, :width], key_weight_ref[...])
    total += dot_rows(pair_ref[:, width:], value_weight_ref[...])
    out_ref[...] = total.astype(low_type)


def act_back(queries, pairs, query_weight, key_weight, value_weight, block=256):
    out = (queries.shape[0], query_weight.shape[0])
    return kernel_call(
        act_back_kernel,
        grid=(out[0] // block,),
        in_specs=[
            by_rows(block, queries.shape),
            by_rows(block, pairs.shape),
            whole(query_weight.shape),
            whole(key_weight.shape),
            whole(value_weight.shape),
        ],
        out_specs=by_rows(block, out),
        out_shape=like(out),
        compiler_params=settings(32),
        name="activation_back",
    )(queries, pairs, query_weight, key_weight, value_weight)


def last_rows_kernel(
    own_ref, other_ref, total_ref, gain_ref, token_ref, part_ref, part_other_ref, out_own_ref, out_other_ref,
    grad_ref, out_ref,
):
    grad_act = own_ref[...].astype(sum_type) + other_ref[...].astype(sum_type)
    normed, factor = normalize(token_ref[...].astype(sum_type))
    grad_ref[...] = total_ref[...] + normalize_back(grad_act * gain_ref[...], normed, factor)
    mixed = out_own_ref[...].astype(sum_type) + out_other_ref[...].astype(sum_type)
    out_ref[...] = (residual_of(token_ref, part_ref, part_other_ref) + mixed).astype(low_type)


def last_rows(own, other, total, gain, residual_parts, out_own, out_other, block=256):
    rows = by_rows(block, own.shape)
    return kernel_call(
        last_rows_kernel,
        grid=(own.shape[0] // block,),
        in_specs=[rows] * 3 + [whole(gain.shape)] + [rows] * 5,
        out_specs=[rows, rows],
        out_shape=[like(own.shape, sum_type), like(own.shape)],
        compiler_params=settings(62),
        name="last_rows",
    )(own, other, total, gain, *residual_parts, out_own, out_other)


def slot_of(rest, bit, first):
    return ((rest >> first) << (first + 1)) | (bit << first) | (rest & ((1 << first) - 1))


def place_slots(me, total_ref, send_ref, keep_ref, first, columns=slice(None)):
    for rest in range(send_ref.shape[0]):
        for bit, ref in ((1, send_ref), (0, keep_ref)):
            ref[rest] = total_ref[slot_of(rest, bit, first) ^ me, :, columns].astype(low_type)


def grad_kernel(me_ref, left_ref, right_ref, *refs, firsts):
    total_s = refs[-1]
    total_s[...] = dot_columns(left_ref[...], right_ref[...]).reshape(total_s.shape)
    width = total_s.shape[2] // len(firsts)
    for index, first in enumerate(firsts):
        columns = slice(index * width, (index + 1) * width)
        place_slots(me_ref[0], total_s, refs[2 * index], refs[2 * index + 1], first, columns)


def grad_parts(me, left, right, devices, firsts, name):
    rows, width = left.shape[1] // devices, right.shape[1]
    half = (devices // 2, rows, width // len(firsts))
    return kernel_call(
        lambda *refs: grad_kernel(*refs, firsts=firsts),
        grid_spec=pltpu.PrefetchScalarGridSpec(
            num_scalar_prefetch=1,
            grid=(1,),
            in_specs=[whole(left.shape), whole(right.shape)],
            out_specs=[whole(half)] * (2 * len(firsts)),
            scratch_shapes=[pltpu.VMEM((devices, rows, width), sum_type)],
        ),
        out_shape=[like(half)] * (2 * len(firsts)),
        compiler_params=settings(62),
        name=name,
    )(me, left, right)


def pair_grad_kernel(me_ref, act_ref, own_ref, cos_ref, sin_ref, *refs, reach, firsts):
    pieces, refs = refs[:reach], refs[reach:]
    out_ref, total_s = refs[0], refs[-1]
    total = own_ref[...]
    for piece in pieces:
        total += piece[...].astype(sum_type)
    width = HEAD_DIMENSION
    keys = total[:, :width]
    cosine, sine = full_tables(cos_ref, sin_ref)
    turned = pltpu.roll(keys, width // 2, 1)
    pairs = jnp.concatenate([keys * cosine - turned * sine, total[:, width:]], axis=1).astype(low_type)
    out_ref[...] = pairs
    total_s[...] = dot_columns(act_ref[...], pairs).reshape(total_s.shape)
    for index, first in enumerate(firsts):
        columns = slice(index * width, (index + 1) * width)
        place_slots(me_ref[0], total_s, refs[2 * index + 1], refs[2 * index + 2], first, columns)


def pair_grads(me, act, own, pieces, cosine, sine, devices, firsts):
    rows = act.shape[1] // devices
    half = (devices // 2, rows, HEAD_DIMENSION)
    operands = (act, own, cosine, sine, *pieces)
    return kernel_call(
        lambda *refs: pair_grad_kernel(*refs, reach=len(pieces), firsts=firsts),
        grid_spec=pltpu.PrefetchScalarGridSpec(
            num_scalar_prefetch=1,
            grid=(1,),
            in_specs=[whole(operand.shape) for operand in operands],
            out_specs=[whole(own.shape)] + [whole(half)] * 4,
            scratch_shapes=[pltpu.VMEM((devices, rows, 2 * HEAD_DIMENSION), sum_type)],
        ),
        out_shape=[like(own.shape)] + [like(half)] * 4,
        compiler_params=settings(62),
        name="key_value_grad",
    )(me, *operands)


def expert_kernel(
    me_ref, act_hbm, grad_hbm, gates_ref, gate_hbm, up_hbm, down_hbm, *refs, experts, firsts, later
):
    refs = refs[2:] if later else refs
    outs, (hidden_hbm, inner_hbm), refs = refs[:6], refs[6:8], refs[8:]
    act_s, grad_s, wide_s, down_s, raw_s, back_s, hidden_s, inner_s, stage_s = refs[:9]
    act_sem, wide_sems, down_sems, pass_sems, out_sems, *total_s = refs[9:]
    rows, hidden, me = act_s.shape[0], gate_hbm.shape[2], me_ref[0]
    first_expert, count = experts

    def fetch(source, target, sem):
        copy = pltpu.make_async_copy(source, target, sem)
        copy.start()
        return copy

    def fetch_wide(expert):
        slot = expert % 2
        return [
            fetch(gate_hbm.at[first_expert + expert], wide_s.at[slot, :, :hidden], wide_sems.at[expert, 0]),
            fetch(up_hbm.at[first_expert + expert], wide_s.at[slot, :, hidden:], wide_sems.at[expert, 1]),
        ]

    def fetch_down(expert):
        pair, at = expert // 2, expert % 2 * hidden
        target = down_s.at[pair % 2, at : at + hidden]
        return [fetch(down_hbm.at[first_expert + expert], target, down_sems.at[expert])]

    def arrive(copies):
        for copy in copies:
            copy.wait()

    def pointwise(expert):
        slot = expert % 2
        at = slice(slot * hidden, (slot + 1) * hidden)
        for start in range(0, rows, 256):
            block = pl.ds(start, 256)
            inner = raw_s[slot, block, :hidden]
            up = raw_s[slot, block, hidden:]
            lane = lax.broadcasted_iota(jnp.int32, (256, LANES), 1)
            mine = lane == first_expert + expert
            gate = jnp.sum(jnp.where(mine, gates_ref[block, :], 0.0), axis=1, keepdims=True)
            square = inner * inner
            bent = jnp.tanh(tanh_scale * inner * (1.0 + tanh_cubic * square))
            half = 0.5 * (1.0 + bent)
            gelu = inner * half
            slope = half + (0.5 * tanh_scale) * inner * (1.0 - bent * bent) * (
                1.0 + (3.0 * tanh_cubic) * square
            )
            back = back_s[block, at] * gate
            hidden_s[block, at] = (gelu * up * gate).astype(low_type)
            inner_s[slot, block, :hidden] = (back * up * slope).astype(low_type)
            inner_s[slot, block, hidden:] = (back * gelu).astype(low_type)

    given = []

    def gradient(left_s, right, chain, part):
        total = dot_columns(left_s[...], right)
        columns = pl.ds(part * 2 * hidden, 2 * hidden)
        if not total_s:
            stage_s[chain, part] = total.astype(low_type).reshape(stage_s.shape[2:])
            for rest in range(stage_s.shape[2] // 2):
                for side, bit in enumerate((1, 0)):
                    source = stage_s.at[chain, part, slot_of(rest, bit, firsts[chain]) ^ me]
                    target = outs[2 * chain + side].at[rest, :, columns]
                    given.append(fetch(source, target, out_sems.at[chain, part, side]))
            return
        total_s[0][...] = total.reshape(total_s[0].shape)
        send_s, keep_s = stage_s.at[chain, part, 0], stage_s.at[chain, part, 1]
        place_slots(me, total_s[0], send_s, keep_s, firsts[chain])
        for side, source in enumerate((send_s, keep_s)):
            target = outs[2 * chain + side].at[:, :, columns]
            given.append(fetch(source, target, out_sems.at[chain, part, side]))

    wide_in = {0: fetch_wide(0)}
    head, tail = pl.ds(0, rows // 4), pl.ds(rows // 4, rows - rows // 4)
    act_in = [
        fetch(act_hbm.at[part], act_s.at[part], act_sem.at[number])
        for number, part in enumerate((head, tail))
    ]
    grad_in = [fetch(grad_hbm, grad_s, act_sem.at[2])]
    down_in = {expert: fetch_down(expert) for expert in range(2)}
    wide_in[1] = fetch_wide(1)
    for expert in range(2, min(4, count)):
        down_in[expert] = fetch_down(expert)
    passed = []
    for pair in range(count // 2):
        one, two = 2 * pair, 2 * pair + 1
        arrive(wide_in[one])
        if pair == 0:
            for part, copy in zip((head, tail), act_in):
                copy.wait()
                raw_s[0, part, :] = dot(act_s[part, :], wide_s[0])
        else:
            raw_s[0] = dot(act_s[...], wide_s[0])
        if one + 2 < count:
            wide_in[one + 2] = fetch_wide(one + 2)
        if pair == 0:
            arrive(grad_in)
        arrive(down_in[one] + down_in[two])
        back_s[...] = dot_rows(grad_s[...], down_s[pair % 2])
        arrive(wide_in[two])
        raw_s[1] = dot(act_s[...], wide_s[1])
        if two + 2 < count:
            wide_in[two + 2] = fetch_wide(two + 2)
        arrive(passed)
        pointwise(0 + one)
        chain = min(one // (count // 2), 1)
        gradient(act_s, inner_s[0], chain, one % (count // 2))
        pointwise(two)
        at = first_expert // 2 + pair
        passed = [
            fetch(hidden_s, hidden_hbm.at[at], pass_sems.at[pair, 0]),
            fetch(inner_s, inner_hbm.at[pl.ds(2 * at, 2)], pass_sems.at[pair, 1]),
        ]
        chain = min(two // (count // 2), 1)
        gradient(act_s, inner_s[1], chain, two % (count // 2))
        gradient(grad_s, hidden_s[...], 2, pair)
    arrive(passed)
    arrive(given)


def expert_group(
    experts, me, act, cotangent, gates, gate_weight, up_weight, down_weight, earlier, devices, firsts
):
    rows, model = act.shape
    hidden = gate_weight.shape[2]
    parts = experts[1] // 2
    half = (devices // 2, model // devices, 2 * hidden)
    joined = half[:2] + (parts * 2 * hidden,)
    hidden_all = like((EXPERTS // 2, rows, 2 * hidden))
    inner_all = like((EXPERTS, rows, 2 * hidden))
    later = earlier is not None
    if half[1] % 16:
        stage, totals = (3, parts, 2) + half, [pltpu.VMEM((devices,) + half[1:], sum_type)]
    else:
        stage, totals = (3, parts, devices) + half[1:], []
    return kernel_call(
        lambda *refs: expert_kernel(*refs, experts=experts, firsts=firsts, later=later),
        grid_spec=pltpu.PrefetchScalarGridSpec(
            num_scalar_prefetch=1,
            grid=(1,),
            in_specs=[any_space, any_space, whole(gates.shape)]
            + [any_space] * (3 + (2 if later else 0)),
            out_specs=[any_space] * 8,
            scratch_shapes=[
                pltpu.VMEM((rows, model), low_type),
                pltpu.VMEM((rows, model), low_type),
                pltpu.VMEM((2, model, 2 * hidden), low_type),
                pltpu.VMEM((2, 2 * hidden, model), low_type),
                pltpu.VMEM((2, rows, 2 * hidden), sum_type),
                pltpu.VMEM((rows, 2 * hidden), sum_type),
                pltpu.VMEM((rows, 2 * hidden), low_type),
                pltpu.VMEM((2, rows, 2 * hidden), low_type),
                pltpu.VMEM(stage, low_type),
                pltpu.SemaphoreType.DMA((3,)),
                pltpu.SemaphoreType.DMA((experts[1], 2)),
                pltpu.SemaphoreType.DMA((experts[1],)),
                pltpu.SemaphoreType.DMA((parts, 2)),
                pltpu.SemaphoreType.DMA((3, parts, 2)),
            ]
            + totals,
        ),
        out_shape=[like(joined)] * 6 + [hidden_all, inner_all],
        input_output_aliases={7: 6, 8: 7} if later else {},
        compiler_params=settings(62),
        name="experts",
    )(me, act, cotangent, gates, gate_weight, up_weight, down_weight, *(earlier or ()))


def inner_back_kernel(inner_ref, gate_ref, up_ref, out_ref, total_s):
    expert = pl.program_id(0)
    hidden = gate_ref.shape[2]

    @pl.when(expert == 0)
    def clear():
        total_s[...] = jnp.zeros(total_s.shape, sum_type)

    weight = jnp.concatenate([gate_ref[0], up_ref[0]], axis=1)
    total_s[...] += dot_rows(inner_ref[0], weight)

    @pl.when(expert == EXPERTS - 1)
    def finish():
        out_ref[...] = total_s[...].astype(low_type)


def inner_back(inner, gate_weight, up_weight):
    rows, model = inner.shape[1], gate_weight.shape[1]
    one = lambda shape: pl.BlockSpec((1,) + shape[1:], lambda expert: (expert, 0, 0))
    return kernel_call(
        inner_back_kernel,
        grid=(EXPERTS,),
        in_specs=[one(inner.shape), one(gate_weight.shape), one(up_weight.shape)],
        out_specs=whole((rows, model)),
        out_shape=like((rows, model)),
        scratch_shapes=[pltpu.VMEM((rows, model), sum_type)],
        compiler_params=settings(62),
        name="expert_back",
    )(inner, gate_weight, up_weight)


def expert_out_kernel(hidden_ref, down_ref, out_ref, total_s):
    pair = pl.program_id(0)

    @pl.when(pair == 0)
    def clear():
        total_s[...] = jnp.zeros(total_s.shape, sum_type)

    total_s[...] += dot(hidden_ref[0], down_ref[...])

    @pl.when(pair == EXPERTS // 2 - 1)
    def finish():
        out_ref[...] = total_s[...].astype(low_type)


def expert_out(hidden, down_weight):
    rows, model = hidden.shape[1], down_weight.shape[2]
    flat = down_weight.reshape(-1, model)
    return kernel_call(
        expert_out_kernel,
        grid=(EXPERTS // 2,),
        in_specs=[
            pl.BlockSpec((1,) + hidden.shape[1:], lambda pair: (pair, 0, 0)),
            pl.BlockSpec((hidden.shape[2], model), lambda pair: (pair, 0)),
        ],
        out_specs=whole((rows, model)),
        out_shape=like((rows, model)),
        scratch_shapes=[pltpu.VMEM((rows, model), sum_type)],
        compiler_params=settings(62),
        name="expert_out",
    )(hidden, flat)


def shifted(shard, by):
    size = lax.axis_size("ctx")
    return lax.ppermute(
        shard, "ctx", [(i, i + by) for i in range(size) if 0 <= i + by < size]
    )


def swapped(part):
    return lax.ppermute(part, "ws", [(0, 1), (1, 0)])


def without(slot, bits):
    for bit in sorted(bits, reverse=True):
        slot = ((slot >> (bit + 1)) << bit) | (slot & ((1 << bit) - 1))
    return slot


def with_zeros(index, bits):
    for bit in sorted(bits):
        index = ((index >> bit) << (bit + 1)) | (index & ((1 << bit) - 1))
    return index


def flip(array, bit):
    size = lax.axis_size("ctx")
    return lax.ppermute(array, "ctx", [(i, i ^ (1 << bit)) for i in range(size)])


class Chains:
    def __init__(self, orders):
        self.orders = orders
        self.sections = [[] for _ in orders]
        self.joined = [[] for _ in orders]
        self.done = 1
        self.waiting = None

    def first_steps(self, sends, keeps):
        self.keeps = keeps
        return [flip(send, order[0]) for send, order in zip(sends, self.orders)]

    def land(self, arrived):
        for chain, part in enumerate(arrived):
            held = self.orders[chain][:1]
            self.sections[chain].append([(self.keeps[chain], held, 0), (part, held, 0)])

    def widths(self, chain):
        return [parts[0][0].shape[2] for parts in self.sections[chain]]

    def ending(self):
        return self.done == len(self.orders[0])

    def arrays(self, chains=None):
        flat = []
        for chain in range(len(self.orders)) if chains is None else chains:
            for parts in self.sections[chain]:
                flat += parts
            flat += self.joined[chain]
        return flat

    def replace(self, arrays, chains=None):
        arrays = iter(arrays)
        fresh = lambda parts: [(next(arrays), held, column) for _, held, column in parts]
        for chain in range(len(self.orders)) if chains is None else chains:
            self.sections[chain] = [fresh(parts) for parts in self.sections[chain]]
            self.joined[chain] = fresh(self.joined[chain])

    @staticmethod
    def totals(refs, sections, joined):
        own = [[next(refs) for _ in parts] for parts in sections]
        shared = [(next(refs), column) for _, _, column in joined]
        at, found = 0, []
        for parts, refs_of in zip(sections, own):
            width = parts[0][0].shape[2]
            total = refs_of[0][0].astype(sum_type)
            for ref, (_, _, column) in zip(refs_of[1:], parts[1:]):
                total += ref[0, :, column : column + width].astype(sum_type)
            for ref, column in shared:
                total += ref[0, :, column + at : column + at + width].astype(sum_type)
            found.append(total)
            at += width
        return found

    def sums(self, refs, chains=None):
        refs = iter(refs)
        return [
            self.totals(refs, self.sections[chain], self.joined[chain])
            for chain in (range(len(self.orders)) if chains is None else chains)
        ]

    @staticmethod
    def sum_call(groups, parts_of, done_count, bits, done_bits):
        slots = lax.axis_size("ctx") >> (done_count + 1)
        specs, operands, shapes, chain = [], [], [], 0
        for group in groups:
            width = 0
            for sections, joined in group:
                for array, held, _ in parts_of[chain]:

                    def index(tile, done=done_bits[chain], bit=bits[chain], held=held):
                        slot = with_zeros(tile, list(done) + [bit]) | (1 << bit)
                        return (without(slot, held), 0, 0)

                    specs.append(pl.BlockSpec((1,) + array.shape[1:], index))
                    operands.append(array)
                width += sum(parts[0][0].shape[2] for parts in sections)
                rows = sections[0][0][0].shape[1]
                chain += 1
            shapes.append((slots, rows, width))

        def run(*refs):
            reading, outs = iter(refs[: len(operands)]), refs[len(operands) :]
            for out, group in zip(outs, groups):
                at = 0
                for sections, joined in group:
                    for total in Chains.totals(reading, sections, joined):
                        out[0, :, at : at + total.shape[1]] = total.astype(low_type)
                        at += total.shape[1]

        return kernel_call(
            run,
            grid=(slots,),
            in_specs=specs,
            out_specs=[pl.BlockSpec((1,) + shape[1:], lambda tile: (tile, 0, 0)) for shape in shapes],
            out_shape=[like(shape) for shape in shapes],
            compiler_params=settings(62),
            name="sum_parts",
        )(*operands)

    def alike(self, chains):
        bits = [self.orders[chain][self.done] for chain in chains]
        return [
            (bit, [chain for chain, other in zip(chains, bits) if other == bit])
            for bit in dict.fromkeys(bits)
        ]

    def prepare(self, apart=False):
        chains = range(len(self.orders))
        self.groups = self.alike(chains)
        if apart:
            self.groups = [(self.orders[chain][self.done], [chain]) for chain in chains]
        order = [chain for _, group in self.groups for chain in group]
        self.waiting = self.sum_call(
            [[(self.sections[chain], self.joined[chain]) for chain in group] for _, group in self.groups],
            [self.arrays([chain]) for chain in order],
            self.done,
            [self.orders[chain][self.done] for chain in order],
            [self.orders[chain][: self.done] for chain in order],
        )

    def launch(self, count=None):
        count = len(self.waiting) if count is None else count
        for send, (bit, group) in zip(self.waiting[:count], self.groups[:count]):
            array, column = flip(send, bit), 0
            for chain in group:
                held = self.orders[chain][: self.done + 1]
                self.joined[chain].append((array, held, column))
                column += sum(self.widths(chain))
        self.waiting, self.groups = self.waiting[count:], self.groups[count:]
        if not self.groups:
            self.done += 1


def end_experts(chains, hidden):
    parts = chains.arrays()
    rows = parts[0][0].shape[1]
    shapes = [(EXPERTS, rows, hidden)] * 3

    def run(*refs):
        gate_ref, up_ref, down_ref = refs[len(parts) :]
        totals = chains.sums(refs[: len(parts)])
        for pair in range(EXPERTS // 2):
            for chain in range(2):
                gate_ref[2 * pair + chain] = totals[chain][pair][:, :hidden]
                up_ref[2 * pair + chain] = totals[chain][pair][:, hidden:]
                columns = slice(chain * hidden, (chain + 1) * hidden)
                down_ref[2 * pair + chain] = totals[2][pair][:, columns]

    return kernel_call(
        run,
        grid=(1,),
        in_specs=[
            pl.BlockSpec((1,) + array.shape[1:], lambda tile: (0, 0, 0)) for array, _, _ in parts
        ],
        out_specs=[whole(shape) for shape in shapes],
        out_shape=[like(shape, sum_type) for shape in shapes],
        compiler_params=settings(62),
        name="expert_gradients",
    )(*[array for array, _, _ in parts])


def end_others(chains):
    parts = chains.arrays()
    rows = parts[0][0].shape[1]
    count = len(chains.orders)
    out_width = sum(chains.widths(chain)[0] for chain in range(count))
    shapes = [
        (rows, out_width),
        (rows, sum(chains.widths(chain)[1] for chain in range(count))),
        (rows, chains.widths(0)[2]),
        (rows, chains.widths(1)[2]),
    ]

    def run(*refs):
        out_ref, query_ref, key_ref, value_ref = refs[len(parts) :]
        totals = chains.sums(refs[: len(parts)])
        at = 0
        for found in totals:
            width = found[0].shape[1]
            out_ref[:, at : at + width] = found[0]
            query_ref[:, at : at + width] = found[1]
            at += width
        key_ref[...] = totals[0][2]
        value_ref[...] = totals[1][2]

    return kernel_call(
        run,
        grid=(1,),
        in_specs=[
            pl.BlockSpec((1,) + array.shape[1:], lambda tile: (0, 0, 0)) for array, _, _ in parts
        ],
        out_specs=[whole(shape) for shape in shapes],
        out_shape=[like(shape, sum_type) for shape in shapes],
        compiler_params=settings(62),
        name="other_gradients",
    )(*[array for array, _, _ in parts])


def tie(*values):
    return lax.optimization_barrier(values)


def advance(chains, anchor):
    if chains.ending():
        return anchor
    anchor = settle(chains, anchor)
    chains.prepare()
    anchor, chains.waiting = tie(anchor, chains.waiting)
    chains.launch()
    return anchor


def chain_arrays(chains, some=None):
    return [array for array, _, _ in chains.arrays(some)]


def settle(chains, anchor, some=None):
    anchor, arrays = tie(anchor, chain_arrays(chains, some))
    chains.replace(arrays, some)
    return anchor


def chain_orders(bits):
    rest = tuple(range(3, bits))
    return ((0, 1, 2) + rest, (1, 2, 0) + rest, (2, 0, 1) + rest)


def body(
    tokens,
    cotangent,
    first_gain,
    query_weight,
    key_projection_weight,
    value_projection_weight,
    out_weight,
    second_gain,
    gate_weight,
    up_weight,
    down_weight,
    segments,
    live_mask,
    routes,
    gate_values,
):
    rows, model = tokens.shape
    devices = lax.axis_size("ctx")
    bits = devices.bit_length() - 1
    index = lax.axis_index("ctx")
    me = index.astype(jnp.int32).reshape(1)
    first_row = index * rows
    query_block, key_block = 256, 256
    gain_one, gain_two = first_gain[None, :], second_gain[None, :]
    orders = chain_orders(bits)
    firsts = tuple(order[0] for order in orders)

    half = HEAD_DIMENSION // 2
    frequency = rope_base ** (-2.0 * jnp.arange(half, dtype=sum_type) / HEAD_DIMENSION)
    positions = (first_row + jnp.arange(rows, dtype=jnp.int32)).astype(sum_type)
    angles = frequency[:, None] * positions[None, :]
    cosine, sine = jnp.cos(angles), jnp.sin(angles)

    activation, own_pair = project_keys(
        tokens, gain_one, key_projection_weight, value_projection_weight, cosine, sine
    )
    reach = min(devices, (DOC_MAX + rows - 2) // rows + 1)
    pieces = [shifted(own_pair, by) for by in range(reach - 1, 0, -1)] + [own_pair]
    queries = project_queries(activation, query_weight, cosine, sine)
    span = reach * rows
    own_at = span - rows
    padded_segments = jnp.concatenate([jnp.full((own_at,), -1, jnp.int32), segments])
    padded_live = jnp.concatenate([jnp.zeros((own_at,), jnp.int32), live_mask])
    key_segments = lax.dynamic_slice_in_dim(padded_segments, first_row, span, 0)
    key_live = lax.dynamic_slice_in_dim(padded_live, first_row, span, 0)
    place, low, gates = tables(
        key_segments[:, None], key_segments[None, own_at:], key_live[:, None], routes, gate_values
    )
    first_block = (low[0, ::query_block] + own_at) // key_block
    queries, gates, low, place, first_block = tie(queries, gates, low, place, first_block)

    mixed_turned, mixed, logs, part = attend(
        first_block, queries, pieces, place, low, out_weight, query_block, key_block
    )
    residual_parts = (tokens, part, swapped(part))
    act_two = second_norm(*residual_parts, gain_two)

    hidden = gate_weight.shape[2]
    experts = Chains(orders)
    earlier, flying = None, []
    for pair in range(EXPERTS // 2):
        outs = expert_group(
            (2 * pair, 2), me, act_two, cotangent, gates, gate_weight, up_weight, down_weight, earlier,
            devices, firsts,
        )
        earlier = outs[-2:]
        act_two, earlier, sends, landed = tie(act_two, earlier, outs[0:6:2], flying)
        if pair:
            experts.land(landed)
        flying = experts.first_steps(sends, outs[1:6:2])
    hidden_all, inner_all = earlier
    back = inner_back(inner_all, gate_weight, up_weight)
    back, landed = tie(back, flying)
    experts.land(landed)
    back_other = swapped(back)
    back = advance(experts, back)
    total, total_low, grad_heads = second_back(
        back, back_other, residual_parts, cotangent, gain_two, out_weight
    )
    rest = tuple(range(3, bits))
    others = Chains(((0, 1, 2) + rest, (1, 0, 2) + rest))
    other_firsts = (0, 1)
    out_outs = grad_parts(me, total_low, mixed, devices, other_firsts, "out_grad")
    grad_heads, out_outs = tie(grad_heads, out_outs)

    tiles = rows // query_block
    back_args = (
        queries, pieces, place, low, mixed_turned, grad_heads, logs, cosine, sine, query_block, key_block
    )
    sums = attend_back(first_block, *back_args, (0, tiles // 2), None)
    sums = advance(experts, sums)
    grad_queries, *far, own = attend_back(first_block, *back_args, (tiles // 2, tiles), sums)
    far, grad_queries = settle(experts, (far, grad_queries))
    returned = [shifted(piece, at + 1 - reach) for at, piece in enumerate(far)]
    while experts.done + 1 < bits:
        grad_queries = advance(experts, grad_queries)
    experts.prepare(apart=True)
    query_outs = grad_parts(me, activation, grad_queries, devices, other_firsts, "query_grad")
    own, returned, query_outs, experts.waiting = tie(own, returned, query_outs, experts.waiting)
    out_flying = others.first_steps(out_outs[0:4:2], out_outs[1:4:2])
    out_keeps = others.keeps
    flying = others.first_steps(query_outs[0:4:2], query_outs[1:4:2])
    query_keeps = others.keeps
    experts.launch(1)
    grad_pairs, *outs = pair_grads(
        me, activation, own, returned, cosine, sine, devices, other_firsts
    )
    grad_pairs, outs, landed = tie(grad_pairs, outs, out_flying)
    others.keeps = out_keeps
    others.land(landed)
    pair_flying = others.first_steps(outs[0:4:2], outs[1:4:2])
    pair_keeps = others.keeps
    grad_act = act_back(
        grad_queries, grad_pairs, query_weight, key_projection_weight, value_projection_weight
    )
    grad_act, landed, pair_landed = tie(grad_act, flying, pair_flying)
    others.keeps = query_keeps
    others.land(landed)
    others.keeps = pair_keeps
    others.land(pair_landed)
    grad_act = settle(experts, grad_act, (0,))
    grad_act, experts.waiting = tie(grad_act, experts.waiting)
    experts.launch(1)
    act_other = swapped(grad_act)
    hidden_all = advance(others, hidden_all)
    out_part = expert_out(hidden_all, down_weight)
    out_part = settle(experts, out_part, (1,))
    out_part, grad_act, act_other, other_arrays = tie(
        out_part, grad_act, act_other, chain_arrays(others)
    )
    others.replace(other_arrays)
    out_part, experts.waiting = tie(out_part, experts.waiting)
    experts.launch()
    out_other = swapped(out_part)
    out_part = advance(others, out_part)
    token_grad, output = last_rows(
        grad_act, act_other, total, gain_one, residual_parts, out_part, out_other
    )
    token_grad = settle(experts, token_grad)
    token_grad = advance(others, token_grad)
    own_rows = model // devices
    gate_grad, up_grad, down_grad = end_experts(experts, hidden)
    while not others.ending():
        token_grad = advance(others, token_grad)
    down_grad = down_grad.transpose(0, 2, 1)
    out_turned, query_grad, key_grad, value_grad = end_others(others)
    out_grad = out_turned.T

    def own_part(weight, dimension=0):
        return lax.dynamic_slice_in_dim(weight, index * own_rows, own_rows, dimension).astype(sum_type)

    first_part = (
        jnp.sum(query_grad * own_part(query_weight), axis=1)
        + jnp.sum(key_grad * own_part(key_projection_weight), axis=1)
        + jnp.sum(value_grad * own_part(value_projection_weight), axis=1)
    )
    second_part = jnp.sum(
        gate_grad * own_part(gate_weight, 1) + up_grad * own_part(up_weight, 1), axis=(0, 2)
    )
    gain_parts = jnp.stack([first_part, second_part])
    gains = jnp.stack([first_gain, second_gain])
    gain_grads = (gain_parts + swapped(gain_parts)) / lax.dynamic_slice_in_dim(
        gains, index * own_rows, own_rows, 1
    )
    grad_first, grad_second = gain_grads[0], gain_grads[1]
    return (
        output,
        token_grad,
        grad_first,
        query_grad,
        key_grad,
        value_grad,
        out_grad,
        grad_second,
        gate_grad,
        up_grad,
        down_grad,
    )


def solution(mesh):
    return jax.shard_map(
        body,
        mesh=mesh,
        in_specs=(
            P("ctx", None),
            P("ctx", None),
            P(),
            P(None, "ws"),
            P(None, "ws"),
            P(None, "ws"),
            P("ws", None),
            P(),
            P(None, None, "ws"),
            P(None, None, "ws"),
            P(None, "ws", None),
            P(),
            P(),
            P("ctx", None),
            P("ctx", None),
        ),
        out_specs=(
            P("ctx", None),
            P("ctx", None),
            P("ctx"),
            P("ctx", "ws"),
            P("ctx", "ws"),
            P("ctx", "ws"),
            P("ws", "ctx"),
            P("ctx"),
            P(None, "ctx", "ws"),
            P(None, "ctx", "ws"),
            P(None, "ws", "ctx"),
        ),
        check_vma=False,
    )
```

```python
import jax
import jax.numpy as jnp
from jax import lax
from jax.experimental import pallas as pl
from jax.experimental.pallas import tpu as pltpu
from jax.sharding import PartitionSpec as P

HEAD_DIMENSION = 128
EXPERTS = 8
DOC_MAX = 2000
CAP = 640
LANES = 128

eps = 1e-06
rope_base = 1000000.0
masked_score = -1e30
far_position = 1 << 30
log2_e = 1.4426950408889634
tanh_scale = 0.7978845608028654
tanh_cubic = 0.044715

low_type = jnp.bfloat16
sum_type = jnp.float32
any_space = pl.BlockSpec(memory_space=pl.ANY)


def dot(left, right):
    return jnp.dot(left, right, preferred_element_type=sum_type)


def dot_rows(left, right):
    return lax.dot_general(left, right, (((1,), (1,)), ((), ())), preferred_element_type=sum_type)


def dot_columns(left, right):
    return lax.dot_general(left, right, (((0,), (0,)), ((), ())), preferred_element_type=sum_type)


def whole(shape):
    return pl.BlockSpec(shape, lambda *index: (0,) * len(shape))


def by_rows(block, shape):
    return pl.BlockSpec((block,) + shape[1:], lambda row, *rest: (row,) + (0,) * (len(shape) - 1))


def like(shape, kind=low_type):
    return jax.ShapeDtypeStruct(shape, kind)


def settings(megabytes):
    return pltpu.CompilerParams(vmem_limit_bytes=megabytes * 2**20)


light = pl.CostEstimate(flops=1000, transcendentals=0, bytes_accessed=1000)


def kernel_call(body, **options):
    return pl.pallas_call(body, cost_estimate=light, **options)


def normalize(value):
    factor = lax.rsqrt(jnp.mean(value * value, axis=-1, keepdims=True) + eps)
    return value * factor, factor


def normalize_back(grad_normed, normed, factor):
    return factor * (grad_normed - normed * jnp.mean(grad_normed * normed, axis=-1, keepdims=True))


def table_kernel(
    segment_ref, own_segment_ref, live_ref, route_ref, value_ref, place_ref, low_ref, gates_ref
):
    span, own_at = segment_ref.shape[0], segment_ref.shape[0] - own_segment_ref.shape[1]
    rows = own_segment_ref.shape[1]
    before = (segment_ref[...] < own_segment_ref[...]).astype(jnp.int32)
    low_ref[...] = jnp.sum(before, axis=0, keepdims=True) - own_at
    position = lax.broadcasted_iota(jnp.int32, (span, LANES), 0) - own_at
    live = jnp.broadcast_to(live_ref[...], (span, LANES)) == 1
    place_ref[...] = jnp.where(live, position, far_position)
    lane = lax.broadcasted_iota(jnp.int32, (rows, LANES), 1)
    chosen = jnp.zeros((rows, LANES), sum_type)
    gates = jnp.zeros((rows, LANES), sum_type)
    for top in range(route_ref.shape[1]):
        here = lane == route_ref[:, top : top + 1]
        chosen = jnp.where(here, 1.0, chosen)
        gates = jnp.where(here, value_ref[:, top : top + 1], gates)
    chosen = jnp.where(live[own_at:], chosen, 0.0)
    earlier = lax.broadcasted_iota(jnp.int32, (rows, rows), 1) < lax.broadcasted_iota(
        jnp.int32, (rows, rows), 0
    )
    rank = dot(earlier.astype(low_type), chosen.astype(low_type))
    gates_ref[...] = jnp.where((chosen > 0.5) & (rank < CAP), gates, 0.0)


def tables(key_segments, own_segments, key_live, routes, gate_values):
    span, rows = key_segments.shape[0], own_segments.shape[1]
    shapes = [like((span, LANES), jnp.int32), like((1, rows), jnp.int32), like((rows, LANES), sum_type)]
    operands = (key_segments, own_segments, key_live, routes, gate_values)
    return kernel_call(
        table_kernel,
        grid=(1,),
        in_specs=[whole(operand.shape) for operand in operands],
        out_specs=[whole(shape.shape) for shape in shapes],
        out_shape=shapes,
        compiler_params=settings(32),
        name="tables",
    )(*operands)


def full_tables(cos_ref, sin_ref):
    cosine, sine = cos_ref[...].T, sin_ref[...].T
    return jnp.concatenate([cosine, cosine], axis=1), jnp.concatenate([-sine, sine], axis=1)


def key_value_kernel(token_ref, gain_ref, key_ref, value_ref, cos_ref, sin_ref, act_ref, out_ref):
    normed, factor = normalize(token_ref[...].astype(sum_type))
    act = (normed * gain_ref[...]).astype(low_type)
    act_ref[...] = act
    keys = dot(act, key_ref[...])
    width = keys.shape[1]
    cosine, sine = full_tables(cos_ref, sin_ref)
    turned = pltpu.roll(keys, HEAD_DIMENSION // 2, 1)
    out_ref[:, :width] = (keys * cosine + turned * sine).astype(low_type)
    out_ref[:, width:] = dot(act, value_ref[...]).astype(low_type)


def project_keys(tokens, gain, key_weight, value_weight, cosine, sine, block=256):
    rows, width = tokens.shape
    joined = key_weight.shape[1] + value_weight.shape[1]
    columns = pl.BlockSpec((cosine.shape[0], block), lambda row: (0, row))
    return kernel_call(
        key_value_kernel,
        grid=(rows // block,),
        in_specs=[
            by_rows(block, tokens.shape),
            whole((1, width)),
            whole(key_weight.shape),
            whole(value_weight.shape),
            columns,
            columns,
        ],
        out_specs=[by_rows(block, (rows, width)), by_rows(block, (rows, joined))],
        out_shape=[like((rows, width)), like((rows, joined))],
        compiler_params=settings(62),
        name="norm_keys_values",
    )(tokens, gain, key_weight, value_weight, cosine, sine)


def query_kernel(act_ref, weight_ref, cos_ref, sin_ref, out_ref):
    raw = dot(act_ref[...], weight_ref[...])
    half = HEAD_DIMENSION // 2
    cosine, sine = cos_ref[...], sin_ref[...]
    for head in range(out_ref.shape[0]):
        part = raw[:, head * HEAD_DIMENSION : (head + 1) * HEAD_DIMENSION].T
        one, two = part[:half], part[half:]
        out_ref[head, :half] = (one * cosine - two * sine).astype(low_type)
        out_ref[head, half:] = (two * cosine + one * sine).astype(low_type)


def project_queries(act, weight, cosine, sine, block=256):
    rows, width = act.shape
    heads = weight.shape[1] // HEAD_DIMENSION
    half = HEAD_DIMENSION // 2
    columns = pl.BlockSpec((half, block), lambda row: (0, row))
    return kernel_call(
        query_kernel,
        grid=(rows // block,),
        in_specs=[by_rows(block, act.shape), whole(weight.shape), columns, columns],
        out_specs=pl.BlockSpec((heads, HEAD_DIMENSION, block), lambda row: (0, 0, row)),
        out_shape=like((heads, HEAD_DIMENSION, rows)),
        compiler_params=settings(32),
        name="queries",
    )(act, weight, cosine, sine)


def repeat_lanes(block, times):
    return jnp.concatenate([block] * times, axis=1) if times > 1 else block


def join_heads(ref):
    return jnp.concatenate([ref[head] for head in range(ref.shape[0])], axis=1)


def pair_bias(place_ref, rows, low, high, start, own_at, own):
    place = repeat_lanes(place_ref[rows, :], low.shape[1] // LANES)
    allowed = (place >= low) & (place <= high)
    if own:
        position = start - own_at + lax.broadcasted_iota(jnp.int32, place.shape, 0)
        allowed = allowed | (position == high)
    return jnp.where(allowed, 0.0, masked_score)


def over_keys(first_ref, step, own_at, query_block, key_block, tile):
    own_first = (own_at + tile * query_block) // key_block
    for extra in range(max(1, query_block // key_block)):
        step(own_first + extra, True)

    def loop(index, carried):
        step(index, False)
        return carried

    lax.fori_loop(first_ref[tile], own_first, loop, 0)


def mix_kernel(
    first_ref, query_ref, place_ref, low_ref, weight_ref, *refs, key_block, own_at, scale,
):
    pieces, (out_ref, mixed_ref, log_ref, part_ref) = refs[:-9], refs[-9:-5]
    key_s, value_s, max_s, sum_s, mix_s = refs[-5:]
    heads, depth, query_block = query_ref.shape
    count = heads * query_block
    tile = pl.program_id(0)

    @pl.when(tile == 0)
    def gather():
        for number, piece in enumerate(pieces):
            at = slice(number * piece.shape[0], (number + 1) * piece.shape[0])
            key_s[at, :] = piece[:, :depth]
            value_s[:, at] = piece[:, depth:].astype(sum_type).T.astype(low_type)

    queries = join_heads(query_ref)
    low = low_ref[...]
    high = tile * query_block + lax.broadcasted_iota(jnp.int32, (1, query_block), 1)
    max_s[...] = jnp.full(max_s.shape, masked_score, sum_type)
    sum_s[...] = jnp.zeros(sum_s.shape, sum_type)
    mix_s[...] = jnp.zeros(mix_s.shape, sum_type)

    def step(index, own):
        start = pl.multiple_of(index * key_block, key_block)
        rows = pl.ds(start, key_block)
        keys, values = key_s[rows, :], value_s[:, rows]
        bias = pair_bias(place_ref, rows, low, high, start, own_at, own)
        groups = 3
        width = heads // groups * query_block
        wide_bias = repeat_lanes(bias, heads // groups)
        raws = [dot(keys, queries[:, g * width : (g + 1) * width]) for g in range(groups)]
        for group, raw in enumerate(raws):
            at = slice(group * width, (group + 1) * width)
            scores = raw * (scale * log2_e) + wide_bias
            old = max_s[:, at]
            new = jnp.maximum(old, jnp.max(scores, axis=0, keepdims=True))
            weights = jnp.exp2(scores - new)
            fade = jnp.exp2(old - new)
            sum_s[:, at] = sum_s[:, at] * fade + jnp.sum(weights, axis=0, keepdims=True)
            max_s[:, at] = new
            mix_s[:, at] = mix_s[:, at] * fade + dot(values, weights.astype(low_type))

    over_keys(first_ref, step, own_at, query_block, key_block, tile)
    total = sum_s[...]
    mixed = mix_s[...] * (1.0 / total)
    logs = max_s[...] + jnp.log2(total)
    for head in range(heads):
        at = slice(head * query_block, (head + 1) * query_block)
        out_ref[head] = mixed[:, at]
        mixed_ref[:, head * depth : (head + 1) * depth] = mixed[:, at].T.astype(low_type)
        log_ref[head] = logs[:, at]
    part_ref[...] = dot(mixed_ref[...], weight_ref[...]).astype(low_type)


def tile_of(query_block):
    def column(shape):
        return pl.BlockSpec(
            shape[:-1] + (query_block,), lambda tile, *rest: (0,) * (len(shape) - 1) + (tile,)
        )

    return column


def attend(first, queries, pieces, place, low, out_weight, query_block, key_block):
    heads, depth, rows = queries.shape
    column = tile_of(query_block)
    count = heads * query_block
    span = place.shape[0]
    return kernel_call(
        lambda *refs: mix_kernel(*refs, key_block=key_block, own_at=span - rows, scale=depth**-0.5),
        grid_spec=pltpu.PrefetchScalarGridSpec(
            num_scalar_prefetch=1,
            grid=(rows // query_block,),
            in_specs=[column(queries.shape), whole(place.shape), column(low.shape), whole(out_weight.shape)]
            + [whole(piece.shape) for piece in pieces],
            out_specs=[
                column(queries.shape),
                by_rows(query_block, (rows, heads * depth)),
                column((heads, 1, rows)),
                by_rows(query_block, (rows, out_weight.shape[1])),
            ],
            scratch_shapes=[
                pltpu.VMEM((span, depth), low_type),
                pltpu.VMEM((depth, span), low_type),
                pltpu.VMEM((1, count), sum_type),
                pltpu.VMEM((1, count), sum_type),
                pltpu.VMEM((depth, count), sum_type),
            ],
        ),
        out_shape=[
            like(queries.shape, sum_type),
            like((rows, heads * depth)),
            like((heads, 1, rows), sum_type),
            like((rows, out_weight.shape[1])),
        ],
        compiler_params=settings(62),
        name="attention",
    )(first, queries, place, low, out_weight, *pieces)


def mix_back_kernel(
    first_ref, query_ref, place_ref, low_ref, mixed_ref, grad_ref, log_ref, cos_ref, sin_ref, *refs,
    reach, key_block, own_at, scale, tiles, offset, final,
):
    pieces, refs = refs[:reach], refs[reach:]
    earlier, refs = (refs[:2], refs[3:]) if offset else ((), refs)
    out_ref, *end_refs = refs[:-6]
    key_s, turned_s, value_s, query_sum, key_sum, value_sum = refs[-6:]
    heads, depth, query_block = query_ref.shape
    tile = pl.program_id(0) + offset
    queries, grads, logs = join_heads(query_ref), join_heads(grad_ref), join_heads(log_ref)
    delta = jnp.sum(grads.astype(sum_type) * join_heads(mixed_ref), axis=0, keepdims=True)
    low = low_ref[...]
    high = tile * query_block + lax.broadcasted_iota(jnp.int32, (1, query_block), 1)

    @pl.when(pl.program_id(0) == 0)
    def gather():
        for number, piece in enumerate(pieces):
            at = slice(number * piece.shape[0], (number + 1) * piece.shape[0])
            key_s[at, :] = piece[:, :depth]
            turned_s[:, at] = piece[:, :depth].astype(sum_type).T.astype(low_type)
            value_s[at, :] = piece[:, depth:]
        if offset:
            key_sum[...] = earlier[0][...]
            value_sum[...] = earlier[1][...]
        else:
            key_sum[...] = jnp.zeros(key_sum.shape, sum_type)
            value_sum[...] = jnp.zeros(value_sum.shape, sum_type)

    query_sum[...] = jnp.zeros(query_sum.shape, sum_type)

    def step(index, own):
        start = pl.multiple_of(index * key_block, key_block)
        rows = pl.ds(start, key_block)
        keys, values, turned = key_s[rows, :], value_s[rows, :], turned_s[:, rows]
        bias = pair_bias(place_ref, rows, low, high, start, own_at, own)
        groups = 3
        width = heads // groups * query_block
        wide_bias = repeat_lanes(bias, heads // groups)
        parts = [slice(g * width, (g + 1) * width) for g in range(groups)]
        raws = [(dot(keys, queries[:, at]), dot(values, grads[:, at])) for at in parts]
        for at, (raw, grad_weights) in zip(parts, raws):
            weights = jnp.exp2(raw * (scale * log2_e) + (wide_bias - logs[:, at]))
            grad_scores = (weights * (grad_weights - delta[:, at])).astype(low_type)
            value_sum[rows, :] += dot_rows(weights.astype(low_type), grads[:, at])
            key_sum[rows, :] += dot_rows(grad_scores, queries[:, at])
            query_sum[:, at] += dot(turned, grad_scores)

    over_keys(first_ref, step, own_at, query_block, key_block, tile)
    half = depth // 2
    cosine, sine = repeat_lanes(cos_ref[...], heads), repeat_lanes(sin_ref[...], heads)
    grad_query = query_sum[...] * scale
    one, two = grad_query[:half], grad_query[half:]
    turned = jnp.concatenate([one * cosine + two * sine, two * cosine - one * sine], axis=0)
    for head in range(heads):
        part = turned[:, head * query_block : (head + 1) * query_block]
        out_ref[:, head * depth : (head + 1) * depth] = part.T.astype(low_type)

    @pl.when(pl.program_id(0) == tiles - 1)
    def finish():
        if final:
            for number, ref in enumerate(end_refs):
                at = slice(number * ref.shape[0], (number + 1) * ref.shape[0])
                ref[:, :depth] = (key_sum[at, :] * scale).astype(ref.dtype)
                ref[:, depth:] = value_sum[at, :].astype(ref.dtype)
        else:
            end_refs[0][...] = key_sum[...]
            end_refs[1][...] = value_sum[...]


def attend_back(
    first, queries, pieces, place, low, mixed, grads, logs, cosine, sine, query_block, key_block, part, earlier
):
    heads, depth, rows = queries.shape
    span = place.shape[0]
    offset, tiles = part[0], part[1] - part[0]
    final = part[1] * query_block == rows

    def column(shape):
        return pl.BlockSpec(
            shape[:-1] + (query_block,),
            lambda tile, *rest: (0,) * (len(shape) - 1) + (tile + offset,),
        )

    extra = [whole((span, depth)), whole((span, depth)), any_space] if offset else []
    ends = (
        [like((rows, 2 * depth))] * (len(pieces) - 1) + [like((rows, 2 * depth), sum_type)]
        if final
        else [like((span, depth), sum_type)] * 2
    )
    operands = [queries, place, low, mixed, grads, logs, cosine, sine, *pieces]
    return kernel_call(
        lambda *refs: mix_back_kernel(
            *refs,
            reach=len(pieces),
            key_block=key_block,
            own_at=span - rows,
            scale=depth**-0.5,
            tiles=tiles,
            offset=offset,
            final=final,
        ),
        grid_spec=pltpu.PrefetchScalarGridSpec(
            num_scalar_prefetch=1,
            grid=(tiles,),
            in_specs=[
                column(queries.shape),
                whole(place.shape),
                column(low.shape),
                column(mixed.shape),
                column(grads.shape),
                column(logs.shape),
                column(cosine.shape),
                column(sine.shape),
            ]
            + [whole(piece.shape) for piece in pieces]
            + extra,
            out_specs=[
                pl.BlockSpec((query_block, heads * depth), lambda tile, *rest: (tile + offset, 0)),
                *[whole(end.shape) for end in ends],
            ],
            scratch_shapes=[
                pltpu.VMEM((span, depth), low_type),
                pltpu.VMEM((depth, span), low_type),
                pltpu.VMEM((span, depth), low_type),
                pltpu.VMEM((depth, heads * query_block), sum_type),
                pltpu.VMEM((span, depth), sum_type),
                pltpu.VMEM((span, depth), sum_type),
            ],
        ),
        out_shape=[like((rows, heads * depth)), *ends],
        input_output_aliases={len(operands) + 3: 0} if offset else {},
        compiler_params=settings(62),
        name="attention_back",
    )(first, *operands, *(((earlier[1], earlier[2], earlier[0])) if offset else ()))


def residual_of(token_ref, own_ref, other_ref):
    mixed = own_ref[...].astype(sum_type) + other_ref[...].astype(sum_type)
    return token_ref[...].astype(sum_type) + mixed


def second_norm_kernel(token_ref, own_ref, other_ref, gain_ref, act_ref):
    residual = residual_of(token_ref, own_ref, other_ref)
    act_ref[...] = (normalize(residual)[0] * gain_ref[...]).astype(low_type)


def second_norm(tokens, own, other, gain, block=256):
    rows = by_rows(block, tokens.shape)
    return kernel_call(
        second_norm_kernel,
        grid=(tokens.shape[0] // block,),
        in_specs=[rows, rows, rows, whole(gain.shape)],
        out_specs=rows,
        out_shape=like(tokens.shape),
        compiler_params=settings(62),
        name="residual_norm",
    )(tokens, own, other, gain)


def second_back_kernel(
    own_ref, other_ref, token_ref, part_ref, part_other_ref, grad_ref, gain_ref, weight_ref,
    total_ref, low_ref, heads_ref,
):
    grad_act = own_ref[...].astype(sum_type) + other_ref[...].astype(sum_type)
    normed, factor = normalize(residual_of(token_ref, part_ref, part_other_ref))

    total = grad_ref[...].astype(sum_type) + normalize_back(
        grad_act * gain_ref[...], normed, factor
    )
    total_ref[...] = total
    low = total.astype(low_type)
    low_ref[...] = low
    turned = dot_rows(weight_ref[...], low).astype(low_type)
    heads_ref[...] = turned.reshape(heads_ref.shape)


def second_back(own, other, residual_parts, cotangent, gain, out_weight, block=256):
    rows = by_rows(block, own.shape)
    heads = out_weight.shape[0] // HEAD_DIMENSION
    shape = (heads, HEAD_DIMENSION, own.shape[0])
    return kernel_call(
        second_back_kernel,
        grid=(own.shape[0] // block,),
        in_specs=[rows] * 6 + [whole(gain.shape), whole(out_weight.shape)],
        out_specs=[rows, rows, tile_of(block)(shape)],
        out_shape=[like(own.shape, sum_type), like(own.shape), like(shape)],
        compiler_params=settings(62),
        name="residual_back",
    )(own, other, *residual_parts, cotangent, gain, out_weight)


def act_back_kernel(query_ref, pair_ref, query_weight_ref, key_weight_ref, value_weight_ref, out_ref):
    width = key_weight_ref.shape[1]
    total = dot_rows(query_ref[...], query_weight_ref[...])
    total += dot_rows(pair_ref[:, :width], key_weight_ref[...])
    total += dot_rows(pair_ref[:, width:], value_weight_ref[...])
    out_ref[...] = total.astype(low_type)


def act_back(queries, pairs, query_weight, key_weight, value_weight, block=256):
    out = (queries.shape[0], query_weight.shape[0])
    return kernel_call(
        act_back_kernel,
        grid=(out[0] // block,),
        in_specs=[
            by_rows(block, queries.shape),
            by_rows(block, pairs.shape),
            whole(query_weight.shape),
            whole(key_weight.shape),
            whole(value_weight.shape),
        ],
        out_specs=by_rows(block, out),
        out_shape=like(out),
        compiler_params=settings(32),
        name="activation_back",
    )(queries, pairs, query_weight, key_weight, value_weight)


def last_rows_kernel(
    own_ref, other_ref, total_ref, gain_ref, token_ref, part_ref, part_other_ref, out_own_ref, out_other_ref,
    grad_ref, out_ref,
):
    grad_act = own_ref[...].astype(sum_type) + other_ref[...].astype(sum_type)
    normed, factor = normalize(token_ref[...].astype(sum_type))
    grad_ref[...] = total_ref[...] + normalize_back(grad_act * gain_ref[...], normed, factor)
    mixed = out_own_ref[...].astype(sum_type) + out_other_ref[...].astype(sum_type)
    out_ref[...] = (residual_of(token_ref, part_ref, part_other_ref) + mixed).astype(low_type)


def last_rows(own, other, total, gain, residual_parts, out_own, out_other, block=256):
    rows = by_rows(block, own.shape)
    return kernel_call(
        last_rows_kernel,
        grid=(own.shape[0] // block,),
        in_specs=[rows] * 3 + [whole(gain.shape)] + [rows] * 5,
        out_specs=[rows, rows],
        out_shape=[like(own.shape, sum_type), like(own.shape)],
        compiler_params=settings(62),
        name="last_rows",
    )(own, other, total, gain, *residual_parts, out_own, out_other)


def slot_of(rest, bit, first):
    return ((rest >> first) << (first + 1)) | (bit << first) | (rest & ((1 << first) - 1))


def place_slots(me, total_ref, send_ref, keep_ref, first, columns=slice(None)):
    for rest in range(send_ref.shape[0]):
        for bit, ref in ((1, send_ref), (0, keep_ref)):
            ref[rest] = total_ref[slot_of(rest, bit, first) ^ me, :, columns].astype(low_type)


def grad_kernel(me_ref, left_ref, right_ref, *refs, firsts):
    total_s = refs[-1]
    total_s[...] = dot_columns(left_ref[...], right_ref[...]).reshape(total_s.shape)
    width = total_s.shape[2] // len(firsts)
    for index, first in enumerate(firsts):
        columns = slice(index * width, (index + 1) * width)
        place_slots(me_ref[0], total_s, refs[2 * index], refs[2 * index + 1], first, columns)


def grad_parts(me, left, right, devices, firsts, name):
    rows, width = left.shape[1] // devices, right.shape[1]
    half = (devices // 2, rows, width // len(firsts))
    return kernel_call(
        lambda *refs: grad_kernel(*refs, firsts=firsts),
        grid_spec=pltpu.PrefetchScalarGridSpec(
            num_scalar_prefetch=1,
            grid=(1,),
            in_specs=[whole(left.shape), whole(right.shape)],
            out_specs=[whole(half)] * (2 * len(firsts)),
            scratch_shapes=[pltpu.VMEM((devices, rows, width), sum_type)],
        ),
        out_shape=[like(half)] * (2 * len(firsts)),
        compiler_params=settings(62),
        name=name,
    )(me, left, right)


def pair_grad_kernel(me_ref, act_ref, own_ref, cos_ref, sin_ref, *refs, reach, firsts):
    pieces, refs = refs[:reach], refs[reach:]
    out_ref, total_s = refs[0], refs[-1]
    total = own_ref[...]
    for piece in pieces:
        total += piece[...].astype(sum_type)
    width = HEAD_DIMENSION
    keys = total[:, :width]
    cosine, sine = full_tables(cos_ref, sin_ref)
    turned = pltpu.roll(keys, width // 2, 1)
    pairs = jnp.concatenate([keys * cosine - turned * sine, total[:, width:]], axis=1).astype(low_type)
    out_ref[...] = pairs
    total_s[...] = dot_columns(act_ref[...], pairs).reshape(total_s.shape)
    for index, first in enumerate(firsts):
        columns = slice(index * width, (index + 1) * width)
        place_slots(me_ref[0], total_s, refs[2 * index + 1], refs[2 * index + 2], first, columns)


def pair_grads(me, act, own, pieces, cosine, sine, devices, firsts):
    rows = act.shape[1] // devices
    half = (devices // 2, rows, HEAD_DIMENSION)
    operands = (act, own, cosine, sine, *pieces)
    return kernel_call(
        lambda *refs: pair_grad_kernel(*refs, reach=len(pieces), firsts=firsts),
        grid_spec=pltpu.PrefetchScalarGridSpec(
            num_scalar_prefetch=1,
            grid=(1,),
            in_specs=[whole(operand.shape) for operand in operands],
            out_specs=[whole(own.shape)] + [whole(half)] * 4,
            scratch_shapes=[pltpu.VMEM((devices, rows, 2 * HEAD_DIMENSION), sum_type)],
        ),
        out_shape=[like(own.shape)] + [like(half)] * 4,
        compiler_params=settings(62),
        name="key_value_grad",
    )(me, *operands)


def expert_kernel(
    me_ref, act_hbm, grad_hbm, gates_ref, gate_hbm, up_hbm, down_hbm, *refs, experts, firsts, later
):
    refs = refs[2:] if later else refs
    outs, (hidden_hbm, inner_hbm), refs = refs[:6], refs[6:8], refs[8:]
    act_s, grad_s, wide_s, down_s, raw_s, back_s, hidden_s, inner_s, stage_s = refs[:9]
    act_sem, wide_sems, down_sems, pass_sems, out_sems, *total_s = refs[9:]
    rows, hidden, me = act_s.shape[0], gate_hbm.shape[2], me_ref[0]
    first_expert, count = experts

    def fetch(source, target, sem):
        copy = pltpu.make_async_copy(source, target, sem)
        copy.start()
        return copy

    def fetch_wide(expert):
        slot = expert % 2
        return [
            fetch(gate_hbm.at[first_expert + expert], wide_s.at[slot, :, :hidden], wide_sems.at[expert, 0]),
            fetch(up_hbm.at[first_expert + expert], wide_s.at[slot, :, hidden:], wide_sems.at[expert, 1]),
        ]

    def fetch_down(expert):
        pair, at = expert // 2, expert % 2 * hidden
        target = down_s.at[pair % 2, at : at + hidden]
        return [fetch(down_hbm.at[first_expert + expert], target, down_sems.at[expert])]

    def arrive(copies):
        for copy in copies:
            copy.wait()

    def pointwise(expert):
        slot = expert % 2
        at = slice(slot * hidden, (slot + 1) * hidden)
        for start in range(0, rows, 256):
            block = pl.ds(start, 256)
            inner = raw_s[slot, block, :hidden]
            up = raw_s[slot, block, hidden:]
            lane = lax.broadcasted_iota(jnp.int32, (256, LANES), 1)
            mine = lane == first_expert + expert
            gate = jnp.sum(jnp.where(mine, gates_ref[block, :], 0.0), axis=1, keepdims=True)
            square = inner * inner
            bent = jnp.tanh(tanh_scale * inner * (1.0 + tanh_cubic * square))
            half = 0.5 * (1.0 + bent)
            gelu = inner * half
            slope = half + (0.5 * tanh_scale) * inner * (1.0 - bent * bent) * (
                1.0 + (3.0 * tanh_cubic) * square
            )
            back = back_s[block, at] * gate
            hidden_s[block, at] = (gelu * up * gate).astype(low_type)
            inner_s[slot, block, :hidden] = (back * up * slope).astype(low_type)
            inner_s[slot, block, hidden:] = (back * gelu).astype(low_type)

    given = []

    def gradient(left_s, right, chain, part):
        total = dot_columns(left_s[...], right)
        columns = pl.ds(part * 2 * hidden, 2 * hidden)
        if not total_s:
            stage_s[chain, part] = total.astype(low_type).reshape(stage_s.shape[2:])
            for rest in range(stage_s.shape[2] // 2):
                for side, bit in enumerate((1, 0)):
                    source = stage_s.at[chain, part, slot_of(rest, bit, firsts[chain]) ^ me]
                    target = outs[2 * chain + side].at[rest, :, columns]
                    given.append(fetch(source, target, out_sems.at[chain, part, side]))
            return
        total_s[0][...] = total.reshape(total_s[0].shape)
        send_s, keep_s = stage_s.at[chain, part, 0], stage_s.at[chain, part, 1]
        place_slots(me, total_s[0], send_s, keep_s, firsts[chain])
        for side, source in enumerate((send_s, keep_s)):
            target = outs[2 * chain + side].at[:, :, columns]
            given.append(fetch(source, target, out_sems.at[chain, part, side]))

    wide_in = {0: fetch_wide(0)}
    head, tail = pl.ds(0, rows // 4), pl.ds(rows // 4, rows - rows // 4)
    act_in = [
        fetch(act_hbm.at[part], act_s.at[part], act_sem.at[number])
        for number, part in enumerate((head, tail))
    ]
    grad_in = [fetch(grad_hbm, grad_s, act_sem.at[2])]
    down_in = {expert: fetch_down(expert) for expert in range(2)}
    wide_in[1] = fetch_wide(1)
    for expert in range(2, min(4, count)):
        down_in[expert] = fetch_down(expert)
    passed = []
    for pair in range(count // 2):
        one, two = 2 * pair, 2 * pair + 1
        arrive(wide_in[one])
        if pair == 0:
            for part, copy in zip((head, tail), act_in):
                copy.wait()
                raw_s[0, part, :] = dot(act_s[part, :], wide_s[0])
        else:
            raw_s[0] = dot(act_s[...], wide_s[0])
        if one + 2 < count:
            wide_in[one + 2] = fetch_wide(one + 2)
        if pair == 0:
            arrive(grad_in)
        arrive(down_in[one] + down_in[two])
        back_s[...] = dot_rows(grad_s[...], down_s[pair % 2])
        arrive(wide_in[two])
        raw_s[1] = dot(act_s[...], wide_s[1])
        if two + 2 < count:
            wide_in[two + 2] = fetch_wide(two + 2)
        arrive(passed)
        pointwise(0 + one)
        chain = min(one // (count // 2), 1)
        gradient(act_s, inner_s[0], chain, one % (count // 2))
        pointwise(two)
        at = first_expert // 2 + pair
        passed = [
            fetch(hidden_s, hidden_hbm.at[at], pass_sems.at[pair, 0]),
            fetch(inner_s, inner_hbm.at[pl.ds(2 * at, 2)], pass_sems.at[pair, 1]),
        ]
        chain = min(two // (count // 2), 1)
        gradient(act_s, inner_s[1], chain, two % (count // 2))
        gradient(grad_s, hidden_s[...], 2, pair)
    arrive(passed)
    arrive(given)


def expert_group(
    experts, me, act, cotangent, gates, gate_weight, up_weight, down_weight, earlier, devices, firsts
):
    rows, model = act.shape
    hidden = gate_weight.shape[2]
    parts = experts[1] // 2
    half = (devices // 2, model // devices, 2 * hidden)
    joined = half[:2] + (parts * 2 * hidden,)
    hidden_all = like((EXPERTS // 2, rows, 2 * hidden))
    inner_all = like((EXPERTS, rows, 2 * hidden))
    later = earlier is not None
    if half[1] % 16:
        stage, totals = (3, parts, 2) + half, [pltpu.VMEM((devices,) + half[1:], sum_type)]
    else:
        stage, totals = (3, parts, devices) + half[1:], []
    return kernel_call(
        lambda *refs: expert_kernel(*refs, experts=experts, firsts=firsts, later=later),
        grid_spec=pltpu.PrefetchScalarGridSpec(
            num_scalar_prefetch=1,
            grid=(1,),
            in_specs=[any_space, any_space, whole(gates.shape)]
            + [any_space] * (3 + (2 if later else 0)),
            out_specs=[any_space] * 8,
            scratch_shapes=[
                pltpu.VMEM((rows, model), low_type),
                pltpu.VMEM((rows, model), low_type),
                pltpu.VMEM((2, model, 2 * hidden), low_type),
                pltpu.VMEM((2, 2 * hidden, model), low_type),
                pltpu.VMEM((2, rows, 2 * hidden), sum_type),
                pltpu.VMEM((rows, 2 * hidden), sum_type),
                pltpu.VMEM((rows, 2 * hidden), low_type),
                pltpu.VMEM((2, rows, 2 * hidden), low_type),
                pltpu.VMEM(stage, low_type),
                pltpu.SemaphoreType.DMA((3,)),
                pltpu.SemaphoreType.DMA((experts[1], 2)),
                pltpu.SemaphoreType.DMA((experts[1],)),
                pltpu.SemaphoreType.DMA((parts, 2)),
                pltpu.SemaphoreType.DMA((3, parts, 2)),
            ]
            + totals,
        ),
        out_shape=[like(joined)] * 6 + [hidden_all, inner_all],
        input_output_aliases={7: 6, 8: 7} if later else {},
        compiler_params=settings(62),
        name="experts",
    )(me, act, cotangent, gates, gate_weight, up_weight, down_weight, *(earlier or ()))


def inner_back_kernel(inner_ref, gate_ref, up_ref, out_ref, total_s):
    expert = pl.program_id(0)
    hidden = gate_ref.shape[2]

    @pl.when(expert == 0)
    def clear():
        total_s[...] = jnp.zeros(total_s.shape, sum_type)

    weight = jnp.concatenate([gate_ref[0], up_ref[0]], axis=1)
    total_s[...] += dot_rows(inner_ref[0], weight)

    @pl.when(expert == EXPERTS - 1)
    def finish():
        out_ref[...] = total_s[...].astype(low_type)


def inner_back(inner, gate_weight, up_weight):
    rows, model = inner.shape[1], gate_weight.shape[1]
    one = lambda shape: pl.BlockSpec((1,) + shape[1:], lambda expert: (expert, 0, 0))
    return kernel_call(
        inner_back_kernel,
        grid=(EXPERTS,),
        in_specs=[one(inner.shape), one(gate_weight.shape), one(up_weight.shape)],
        out_specs=whole((rows, model)),
        out_shape=like((rows, model)),
        scratch_shapes=[pltpu.VMEM((rows, model), sum_type)],
        compiler_params=settings(62),
        name="expert_back",
    )(inner, gate_weight, up_weight)


def expert_out_kernel(hidden_ref, down_ref, out_ref, total_s):
    pair = pl.program_id(0)

    @pl.when(pair == 0)
    def clear():
        total_s[...] = jnp.zeros(total_s.shape, sum_type)

    total_s[...] += dot(hidden_ref[0], down_ref[...])

    @pl.when(pair == EXPERTS // 2 - 1)
    def finish():
        out_ref[...] = total_s[...].astype(low_type)


def expert_out(hidden, down_weight):
    rows, model = hidden.shape[1], down_weight.shape[2]
    flat = down_weight.reshape(-1, model)
    return kernel_call(
        expert_out_kernel,
        grid=(EXPERTS // 2,),
        in_specs=[
            pl.BlockSpec((1,) + hidden.shape[1:], lambda pair: (pair, 0, 0)),
            pl.BlockSpec((hidden.shape[2], model), lambda pair: (pair, 0)),
        ],
        out_specs=whole((rows, model)),
        out_shape=like((rows, model)),
        scratch_shapes=[pltpu.VMEM((rows, model), sum_type)],
        compiler_params=settings(62),
        name="expert_out",
    )(hidden, flat)


def shifted(shard, by):
    size = lax.axis_size("ctx")
    return lax.ppermute(
        shard, "ctx", [(i, i + by) for i in range(size) if 0 <= i + by < size]
    )


def swapped(part):
    return lax.ppermute(part, "ws", [(0, 1), (1, 0)])


def without(slot, bits):
    for bit in sorted(bits, reverse=True):
        slot = ((slot >> (bit + 1)) << bit) | (slot & ((1 << bit) - 1))
    return slot


def with_zeros(index, bits):
    for bit in sorted(bits):
        index = ((index >> bit) << (bit + 1)) | (index & ((1 << bit) - 1))
    return index


def flip(array, bit):
    size = lax.axis_size("ctx")
    return lax.ppermute(array, "ctx", [(i, i ^ (1 << bit)) for i in range(size)])


class Chains:
    def __init__(self, orders):
        self.orders = orders
        self.sections = [[] for _ in orders]
        self.joined = [[] for _ in orders]
        self.done = 1
        self.waiting = None

    def first_steps(self, sends, keeps):
        self.keeps = keeps
        return [flip(send, order[0]) for send, order in zip(sends, self.orders)]

    def land(self, arrived):
        for chain, part in enumerate(arrived):
            held = self.orders[chain][:1]
            self.sections[chain].append([(self.keeps[chain], held, 0), (part, held, 0)])

    def widths(self, chain):
        return [parts[0][0].shape[2] for parts in self.sections[chain]]

    def ending(self):
        return self.done == len(self.orders[0])

    def arrays(self, chains=None):
        flat = []
        for chain in range(len(self.orders)) if chains is None else chains:
            for parts in self.sections[chain]:
                flat += parts
            flat += self.joined[chain]
        return flat

    def replace(self, arrays, chains=None):
        arrays = iter(arrays)
        fresh = lambda parts: [(next(arrays), held, column) for _, held, column in parts]
        for chain in range(len(self.orders)) if chains is None else chains:
            self.sections[chain] = [fresh(parts) for parts in self.sections[chain]]
            self.joined[chain] = fresh(self.joined[chain])

    @staticmethod
    def totals(refs, sections, joined):
        own = [[next(refs) for _ in parts] for parts in sections]
        shared = [(next(refs), column) for _, _, column in joined]
        at, found = 0, []
        for parts, refs_of in zip(sections, own):
            width = parts[0][0].shape[2]
            total = refs_of[0][0].astype(sum_type)
            for ref, (_, _, column) in zip(refs_of[1:], parts[1:]):
                total += ref[0, :, column : column + width].astype(sum_type)
            for ref, column in shared:
                total += ref[0, :, column + at : column + at + width].astype(sum_type)
            found.append(total)
            at += width
        return found

    def sums(self, refs, chains=None):
        refs = iter(refs)
        return [
            self.totals(refs, self.sections[chain], self.joined[chain])
            for chain in (range(len(self.orders)) if chains is None else chains)
        ]

    @staticmethod
    def sum_call(groups, parts_of, done_count, bits, done_bits):
        slots = lax.axis_size("ctx") >> (done_count + 1)
        specs, operands, shapes, chain = [], [], [], 0
        for group in groups:
            width = 0
            for sections, joined in group:
                for array, held, _ in parts_of[chain]:

                    def index(tile, done=done_bits[chain], bit=bits[chain], held=held):
                        slot = with_zeros(tile, list(done) + [bit]) | (1 << bit)
                        return (without(slot, held), 0, 0)

                    specs.append(pl.BlockSpec((1,) + array.shape[1:], index))
                    operands.append(array)
                width += sum(parts[0][0].shape[2] for parts in sections)
                rows = sections[0][0][0].shape[1]
                chain += 1
            shapes.append((slots, rows, width))

        def run(*refs):
            reading, outs = iter(refs[: len(operands)]), refs[len(operands) :]
            for out, group in zip(outs, groups):
                at = 0
                for sections, joined in group:
                    for total in Chains.totals(reading, sections, joined):
                        out[0, :, at : at + total.shape[1]] = total.astype(low_type)
                        at += total.shape[1]

        return kernel_call(
            run,
            grid=(slots,),
            in_specs=specs,
            out_specs=[pl.BlockSpec((1,) + shape[1:], lambda tile: (tile, 0, 0)) for shape in shapes],
            out_shape=[like(shape) for shape in shapes],
            compiler_params=settings(62),
            name="sum_parts",
        )(*operands)

    def alike(self, chains):
        bits = [self.orders[chain][self.done] for chain in chains]
        return [
            (bit, [chain for chain, other in zip(chains, bits) if other == bit])
            for bit in dict.fromkeys(bits)
        ]

    def prepare(self, apart=False):
        chains = range(len(self.orders))
        self.groups = self.alike(chains)
        if apart:
            self.groups = [(self.orders[chain][self.done], [chain]) for chain in chains]
        order = [chain for _, group in self.groups for chain in group]
        self.waiting = self.sum_call(
            [[(self.sections[chain], self.joined[chain]) for chain in group] for _, group in self.groups],
            [self.arrays([chain]) for chain in order],
            self.done,
            [self.orders[chain][self.done] for chain in order],
            [self.orders[chain][: self.done] for chain in order],
        )

    def launch(self, count=None):
        count = len(self.waiting) if count is None else count
        for send, (bit, group) in zip(self.waiting[:count], self.groups[:count]):
            array, column = flip(send, bit), 0
            for chain in group:
                held = self.orders[chain][: self.done + 1]
                self.joined[chain].append((array, held, column))
                column += sum(self.widths(chain))
        self.waiting, self.groups = self.waiting[count:], self.groups[count:]
        if not self.groups:
            self.done += 1


def end_experts(chains, hidden):
    parts = chains.arrays()
    rows = parts[0][0].shape[1]
    shapes = [(EXPERTS, rows, hidden)] * 3

    def run(*refs):
        gate_ref, up_ref, down_ref = refs[len(parts) :]
        totals = chains.sums(refs[: len(parts)])
        for pair in range(EXPERTS // 2):
            for chain in range(2):
                gate_ref[2 * pair + chain] = totals[chain][pair][:, :hidden]
                up_ref[2 * pair + chain] = totals[chain][pair][:, hidden:]
                columns = slice(chain * hidden, (chain + 1) * hidden)
                down_ref[2 * pair + chain] = totals[2][pair][:, columns]

    return kernel_call(
        run,
        grid=(1,),
        in_specs=[
            pl.BlockSpec((1,) + array.shape[1:], lambda tile: (0, 0, 0)) for array, _, _ in parts
        ],
        out_specs=[whole(shape) for shape in shapes],
        out_shape=[like(shape, sum_type) for shape in shapes],
        compiler_params=settings(62),
        name="expert_gradients",
    )(*[array for array, _, _ in parts])


def end_others(chains):
    parts = chains.arrays()
    rows = parts[0][0].shape[1]
    count = len(chains.orders)
    out_width = sum(chains.widths(chain)[0] for chain in range(count))
    shapes = [
        (rows, out_width),
        (rows, sum(chains.widths(chain)[1] for chain in range(count))),
        (rows, chains.widths(0)[2]),
        (rows, chains.widths(1)[2]),
    ]

    def run(*refs):
        out_ref, query_ref, key_ref, value_ref = refs[len(parts) :]
        totals = chains.sums(refs[: len(parts)])
        at = 0
        for found in totals:
            width = found[0].shape[1]
            out_ref[:, at : at + width] = found[0]
            query_ref[:, at : at + width] = found[1]
            at += width
        key_ref[...] = totals[0][2]
        value_ref[...] = totals[1][2]

    return kernel_call(
        run,
        grid=(1,),
        in_specs=[
            pl.BlockSpec((1,) + array.shape[1:], lambda tile: (0, 0, 0)) for array, _, _ in parts
        ],
        out_specs=[whole(shape) for shape in shapes],
        out_shape=[like(shape, sum_type) for shape in shapes],
        compiler_params=settings(62),
        name="other_gradients",
    )(*[array for array, _, _ in parts])


def tie(*values):
    return lax.optimization_barrier(values)


def advance(chains, anchor):
    if chains.ending():
        return anchor
    anchor = settle(chains, anchor)
    chains.prepare()
    anchor, chains.waiting = tie(anchor, chains.waiting)
    chains.launch()
    return anchor


def chain_arrays(chains, some=None):
    return [array for array, _, _ in chains.arrays(some)]


def settle(chains, anchor, some=None):
    anchor, arrays = tie(anchor, chain_arrays(chains, some))
    chains.replace(arrays, some)
    return anchor


def chain_orders(bits):
    rest = tuple(range(3, bits))
    return ((0, 1, 2) + rest, (1, 2, 0) + rest, (2, 0, 1) + rest)


def body(
    tokens,
    cotangent,
    first_gain,
    query_weight,
    key_projection_weight,
    value_projection_weight,
    out_weight,
    second_gain,
    gate_weight,
    up_weight,
    down_weight,
    segments,
    live_mask,
    routes,
    gate_values,
):
    rows, model = tokens.shape
    devices = lax.axis_size("ctx")
    bits = devices.bit_length() - 1
    index = lax.axis_index("ctx")
    me = index.astype(jnp.int32).reshape(1)
    first_row = index * rows
    query_block, key_block = 256, 256
    gain_one, gain_two = first_gain[None, :], second_gain[None, :]
    orders = chain_orders(bits)
    firsts = tuple(order[0] for order in orders)

    half = HEAD_DIMENSION // 2
    frequency = rope_base ** (-2.0 * jnp.arange(half, dtype=sum_type) / HEAD_DIMENSION)
    positions = (first_row + jnp.arange(rows, dtype=jnp.int32)).astype(sum_type)
    angles = frequency[:, None] * positions[None, :]
    cosine, sine = jnp.cos(angles), jnp.sin(angles)

    activation, own_pair = project_keys(
        tokens, gain_one, key_projection_weight, value_projection_weight, cosine, sine
    )
    reach = min(devices, (DOC_MAX + rows - 2) // rows + 1)
    pieces = [shifted(own_pair, by) for by in range(reach - 1, 0, -1)] + [own_pair]
    queries = project_queries(activation, query_weight, cosine, sine)
    span = reach * rows
    own_at = span - rows
    padded_segments = jnp.concatenate([jnp.full((own_at,), -1, jnp.int32), segments])
    padded_live = jnp.concatenate([jnp.zeros((own_at,), jnp.int32), live_mask])
    key_segments = lax.dynamic_slice_in_dim(padded_segments, first_row, span, 0)
    key_live = lax.dynamic_slice_in_dim(padded_live, first_row, span, 0)
    place, low, gates = tables(
        key_segments[:, None], key_segments[None, own_at:], key_live[:, None], routes, gate_values
    )
    first_block = (low[0, ::query_block] + own_at) // key_block
    queries, gates, low, place, first_block = tie(queries, gates, low, place, first_block)

    mixed_turned, mixed, logs, part = attend(
        first_block, queries, pieces, place, low, out_weight, query_block, key_block
    )
    residual_parts = (tokens, part, swapped(part))
    act_two = second_norm(*residual_parts, gain_two)

    hidden = gate_weight.shape[2]
    experts = Chains(orders)
    earlier, flying = None, []
    for pair in range(EXPERTS // 2):
        outs = expert_group(
            (2 * pair, 2), me, act_two, cotangent, gates, gate_weight, up_weight, down_weight, earlier,
            devices, firsts,
        )
        earlier = outs[-2:]
        act_two, earlier, sends, landed = tie(act_two, earlier, outs[0:6:2], flying)
        if pair:
            experts.land(landed)
        flying = experts.first_steps(sends, outs[1:6:2])
    hidden_all, inner_all = earlier
    back = inner_back(inner_all, gate_weight, up_weight)
    back, landed = tie(back, flying)
    experts.land(landed)
    back_other = swapped(back)
    back = advance(experts, back)
    total, total_low, grad_heads = second_back(
        back, back_other, residual_parts, cotangent, gain_two, out_weight
    )
    rest = tuple(range(3, bits))
    others = Chains(((0, 1, 2) + rest, (1, 0, 2) + rest))
    other_firsts = (0, 1)
    out_outs = grad_parts(me, total_low, mixed, devices, other_firsts, "out_grad")
    grad_heads, out_outs = tie(grad_heads, out_outs)

    tiles = rows // query_block
    back_args = (
        queries, pieces, place, low, mixed_turned, grad_heads, logs, cosine, sine, query_block, key_block
    )
    sums = attend_back(first_block, *back_args, (0, tiles // 2), None)
    sums = advance(experts, sums)
    grad_queries, *far, own = attend_back(first_block, *back_args, (tiles // 2, tiles), sums)
    returned = [shifted(piece, at + 1 - reach) for at, piece in enumerate(far)]
    query_outs = grad_parts(me, activation, grad_queries, devices, other_firsts, "query_grad")
    grad_queries = settle(experts, grad_queries)
    while experts.done + 1 < bits:
        grad_queries = advance(experts, grad_queries)
    experts.prepare(apart=True)
    own, returned, query_outs, experts.waiting = tie(own, returned, query_outs, experts.waiting)
    out_flying = others.first_steps(out_outs[0:4:2], out_outs[1:4:2])
    out_keeps = others.keeps
    flying = others.first_steps(query_outs[0:4:2], query_outs[1:4:2])
    query_keeps = others.keeps
    experts.launch(1)
    grad_pairs, *outs = pair_grads(
        me, activation, own, returned, cosine, sine, devices, other_firsts
    )
    grad_pairs, outs, landed = tie(grad_pairs, outs, out_flying)
    others.keeps = out_keeps
    others.land(landed)
    pair_flying = others.first_steps(outs[0:4:2], outs[1:4:2])
    pair_keeps = others.keeps
    grad_act = act_back(
        grad_queries, grad_pairs, query_weight, key_projection_weight, value_projection_weight
    )
    grad_act, landed, pair_landed = tie(grad_act, flying, pair_flying)
    others.keeps = query_keeps
    others.land(landed)
    others.keeps = pair_keeps
    others.land(pair_landed)
    grad_act = settle(experts, grad_act, (0,))
    grad_act, experts.waiting = tie(grad_act, experts.waiting)
    experts.launch(1)
    act_other = swapped(grad_act)
    hidden_all = advance(others, hidden_all)
    out_part = expert_out(hidden_all, down_weight)
    out_part = settle(experts, out_part, (1,))
    out_part, grad_act, act_other, other_arrays = tie(
        out_part, grad_act, act_other, chain_arrays(others)
    )
    others.replace(other_arrays)
    out_part, experts.waiting = tie(out_part, experts.waiting)
    experts.launch()
    out_other = swapped(out_part)
    out_part = advance(others, out_part)
    token_grad, output = last_rows(
        grad_act, act_other, total, gain_one, residual_parts, out_part, out_other
    )
    token_grad = settle(experts, token_grad)
    token_grad = advance(others, token_grad)
    own_rows = model // devices
    gate_grad, up_grad, down_grad = end_experts(experts, hidden)
    while not others.ending():
        token_grad = advance(others, token_grad)
    down_grad = down_grad.transpose(0, 2, 1)
    out_turned, query_grad, key_grad, value_grad = end_others(others)
    out_grad = out_turned.T

    def own_part(weight, dimension=0):
        return lax.dynamic_slice_in_dim(weight, index * own_rows, own_rows, dimension).astype(sum_type)

    first_part = (
        jnp.sum(query_grad * own_part(query_weight), axis=1)
        + jnp.sum(key_grad * own_part(key_projection_weight), axis=1)
        + jnp.sum(value_grad * own_part(value_projection_weight), axis=1)
    )
    second_part = jnp.sum(
        gate_grad * own_part(gate_weight, 1) + up_grad * own_part(up_weight, 1), axis=(0, 2)
    )
    gain_parts = jnp.stack([first_part, second_part])
    gains = jnp.stack([first_gain, second_gain])
    gain_grads = (gain_parts + swapped(gain_parts)) / lax.dynamic_slice_in_dim(
        gains, index * own_rows, own_rows, 1
    )
    grad_first, grad_second = gain_grads[0], gain_grads[1]
    return (
        output,
        token_grad,
        grad_first,
        query_grad,
        key_grad,
        value_grad,
        out_grad,
        grad_second,
        gate_grad,
        up_grad,
        down_grad,
    )


def solution(mesh):
    return jax.shard_map(
        body,
        mesh=mesh,
        in_specs=(
            P("ctx", None),
            P("ctx", None),
            P(),
            P(None, "ws"),
            P(None, "ws"),
            P(None, "ws"),
            P("ws", None),
            P(),
            P(None, None, "ws"),
            P(None, None, "ws"),
            P(None, "ws", None),
            P(),
            P(),
            P("ctx", None),
            P("ctx", None),
        ),
        out_specs=(
            P("ctx", None),
            P("ctx", None),
            P("ctx"),
            P("ctx", "ws"),
            P("ctx", "ws"),
            P("ctx", "ws"),
            P("ws", "ctx"),
            P("ctx"),
            P(None, "ctx", "ws"),
            P(None, "ctx", "ws"),
            P(None, "ws", "ctx"),
        ),
        check_vma=False,
    )
```

```python
import jax
import jax.numpy as jnp
from jax import lax
from jax.experimental import pallas as pl
from jax.experimental.pallas import tpu as pltpu
from jax.sharding import PartitionSpec as P

HEAD_DIMENSION = 128
EXPERTS = 8
DOC_MAX = 2000
CAP = 640
LANES = 128

eps = 1e-06
rope_base = 1000000.0
masked_score = -1e30
far_position = 1 << 30
log2_e = 1.4426950408889634
tanh_scale = 0.7978845608028654
tanh_cubic = 0.044715

low_type = jnp.bfloat16
sum_type = jnp.float32
any_space = pl.BlockSpec(memory_space=pl.ANY)


def dot(left, right):
    return jnp.dot(left, right, preferred_element_type=sum_type)


def dot_rows(left, right):
    return lax.dot_general(left, right, (((1,), (1,)), ((), ())), preferred_element_type=sum_type)


def dot_columns(left, right):
    return lax.dot_general(left, right, (((0,), (0,)), ((), ())), preferred_element_type=sum_type)


def whole(shape):
    return pl.BlockSpec(shape, lambda *index: (0,) * len(shape))


def by_rows(block, shape):
    return pl.BlockSpec((block,) + shape[1:], lambda row, *rest: (row,) + (0,) * (len(shape) - 1))


def like(shape, kind=low_type):
    return jax.ShapeDtypeStruct(shape, kind)


def settings(megabytes):
    return pltpu.CompilerParams(vmem_limit_bytes=megabytes * 2**20)


light = pl.CostEstimate(flops=1000, transcendentals=0, bytes_accessed=1000)


def kernel_call(body, **options):
    return pl.pallas_call(body, cost_estimate=light, **options)


def normalize(value):
    factor = lax.rsqrt(jnp.mean(value * value, axis=-1, keepdims=True) + eps)
    return value * factor, factor


def normalize_back(grad_normed, normed, factor):
    return factor * (grad_normed - normed * jnp.mean(grad_normed * normed, axis=-1, keepdims=True))


def table_kernel(
    segment_ref, own_segment_ref, live_ref, route_ref, value_ref, place_ref, low_ref, gates_ref
):
    span, own_at = segment_ref.shape[0], segment_ref.shape[0] - own_segment_ref.shape[1]
    rows = own_segment_ref.shape[1]
    before = (segment_ref[...] < own_segment_ref[...]).astype(jnp.int32)
    low_ref[...] = jnp.sum(before, axis=0, keepdims=True) - own_at
    position = lax.broadcasted_iota(jnp.int32, (span, LANES), 0) - own_at
    live = jnp.broadcast_to(live_ref[...], (span, LANES)) == 1
    place_ref[...] = jnp.where(live, position, far_position)
    lane = lax.broadcasted_iota(jnp.int32, (rows, LANES), 1)
    chosen = jnp.zeros((rows, LANES), sum_type)
    gates = jnp.zeros((rows, LANES), sum_type)
    for top in range(route_ref.shape[1]):
        here = lane == route_ref[:, top : top + 1]
        chosen = jnp.where(here, 1.0, chosen)
        gates = jnp.where(here, value_ref[:, top : top + 1], gates)
    chosen = jnp.where(live[own_at:], chosen, 0.0)
    earlier = lax.broadcasted_iota(jnp.int32, (rows, rows), 1) < lax.broadcasted_iota(
        jnp.int32, (rows, rows), 0
    )
    rank = dot(earlier.astype(low_type), chosen.astype(low_type))
    gates_ref[...] = jnp.where((chosen > 0.5) & (rank < CAP), gates, 0.0)


def tables(key_segments, own_segments, key_live, routes, gate_values):
    span, rows = key_segments.shape[0], own_segments.shape[1]
    shapes = [like((span, LANES), jnp.int32), like((1, rows), jnp.int32), like((rows, LANES), sum_type)]
    operands = (key_segments, own_segments, key_live, routes, gate_values)
    return kernel_call(
        table_kernel,
        grid=(1,),
        in_specs=[whole(operand.shape) for operand in operands],
        out_specs=[whole(shape.shape) for shape in shapes],
        out_shape=shapes,
        compiler_params=settings(32),
        name="tables",
    )(*operands)


def full_tables(cos_ref, sin_ref):
    cosine, sine = cos_ref[...].T, sin_ref[...].T
    return jnp.concatenate([cosine, cosine], axis=1), jnp.concatenate([-sine, sine], axis=1)


def key_value_kernel(token_ref, gain_ref, key_ref, value_ref, cos_ref, sin_ref, act_ref, out_ref):
    normed, factor = normalize(token_ref[...].astype(sum_type))
    act = (normed * gain_ref[...]).astype(low_type)
    act_ref[...] = act
    keys = dot(act, key_ref[...])
    width = keys.shape[1]
    cosine, sine = full_tables(cos_ref, sin_ref)
    turned = pltpu.roll(keys, HEAD_DIMENSION // 2, 1)
    out_ref[:, :width] = (keys * cosine + turned * sine).astype(low_type)
    out_ref[:, width:] = dot(act, value_ref[...]).astype(low_type)


def project_keys(tokens, gain, key_weight, value_weight, cosine, sine, block=256):
    rows, width = tokens.shape
    joined = key_weight.shape[1] + value_weight.shape[1]
    columns = pl.BlockSpec((cosine.shape[0], block), lambda row: (0, row))
    return kernel_call(
        key_value_kernel,
        grid=(rows // block,),
        in_specs=[
            by_rows(block, tokens.shape),
            whole((1, width)),
            whole(key_weight.shape),
            whole(value_weight.shape),
            columns,
            columns,
        ],
        out_specs=[by_rows(block, (rows, width)), by_rows(block, (rows, joined))],
        out_shape=[like((rows, width)), like((rows, joined))],
        compiler_params=settings(62),
        name="norm_keys_values",
    )(tokens, gain, key_weight, value_weight, cosine, sine)


def query_kernel(act_ref, weight_ref, cos_ref, sin_ref, out_ref):
    raw = dot(act_ref[...], weight_ref[...])
    half = HEAD_DIMENSION // 2
    cosine, sine = cos_ref[...], sin_ref[...]
    for head in range(out_ref.shape[0]):
        part = raw[:, head * HEAD_DIMENSION : (head + 1) * HEAD_DIMENSION].T
        one, two = part[:half], part[half:]
        out_ref[head, :half] = (one * cosine - two * sine).astype(low_type)
        out_ref[head, half:] = (two * cosine + one * sine).astype(low_type)


def project_queries(act, weight, cosine, sine, block=256):
    rows, width = act.shape
    heads = weight.shape[1] // HEAD_DIMENSION
    half = HEAD_DIMENSION // 2
    columns = pl.BlockSpec((half, block), lambda row: (0, row))
    return kernel_call(
        query_kernel,
        grid=(rows // block,),
        in_specs=[by_rows(block, act.shape), whole(weight.shape), columns, columns],
        out_specs=pl.BlockSpec((heads, HEAD_DIMENSION, block), lambda row: (0, 0, row)),
        out_shape=like((heads, HEAD_DIMENSION, rows)),
        compiler_params=settings(32),
        name="queries",
    )(act, weight, cosine, sine)


def repeat_lanes(block, times):
    return jnp.concatenate([block] * times, axis=1) if times > 1 else block


def join_heads(ref):
    return jnp.concatenate([ref[head] for head in range(ref.shape[0])], axis=1)


def pair_bias(place_ref, rows, low, high, start, own_at, own):
    place = repeat_lanes(place_ref[rows, :], low.shape[1] // LANES)
    allowed = (place >= low) & (place <= high)
    if own:
        position = start - own_at + lax.broadcasted_iota(jnp.int32, place.shape, 0)
        allowed = allowed | (position == high)
    return jnp.where(allowed, 0.0, masked_score)


def over_keys(first_ref, step, own_at, query_block, key_block, tile):
    own_first = (own_at + tile * query_block) // key_block
    for extra in range(max(1, query_block // key_block)):
        step(own_first + extra, True)

    def loop(index, carried):
        step(index, False)
        return carried

    lax.fori_loop(first_ref[tile], own_first, loop, 0)


def mix_kernel(
    first_ref, query_ref, place_ref, low_ref, weight_ref, *refs, key_block, own_at, scale,
):
    pieces, (out_ref, mixed_ref, log_ref, part_ref) = refs[:-9], refs[-9:-5]
    key_s, value_s, max_s, sum_s, mix_s = refs[-5:]
    heads, depth, query_block = query_ref.shape
    count = heads * query_block
    tile = pl.program_id(0)

    @pl.when(tile == 0)
    def gather():
        for number, piece in enumerate(pieces):
            at = slice(number * piece.shape[0], (number + 1) * piece.shape[0])
            key_s[at, :] = piece[:, :depth]
            value_s[:, at] = piece[:, depth:].astype(sum_type).T.astype(low_type)

    queries = join_heads(query_ref)
    low = low_ref[...]
    high = tile * query_block + lax.broadcasted_iota(jnp.int32, (1, query_block), 1)
    max_s[...] = jnp.full(max_s.shape, masked_score, sum_type)
    sum_s[...] = jnp.zeros(sum_s.shape, sum_type)
    mix_s[...] = jnp.zeros(mix_s.shape, sum_type)

    def step(index, own):
        start = pl.multiple_of(index * key_block, key_block)
        rows = pl.ds(start, key_block)
        keys, values = key_s[rows, :], value_s[:, rows]
        bias = pair_bias(place_ref, rows, low, high, start, own_at, own)
        groups = 3
        width = heads // groups * query_block
        wide_bias = repeat_lanes(bias, heads // groups)
        raws = [dot(keys, queries[:, g * width : (g + 1) * width]) for g in range(groups)]
        for group, raw in enumerate(raws):
            at = slice(group * width, (group + 1) * width)
            scores = raw * (scale * log2_e) + wide_bias
            old = max_s[:, at]
            new = jnp.maximum(old, jnp.max(scores, axis=0, keepdims=True))
            weights = jnp.exp2(scores - new)
            fade = jnp.exp2(old - new)
            sum_s[:, at] = sum_s[:, at] * fade + jnp.sum(weights, axis=0, keepdims=True)
            max_s[:, at] = new
            mix_s[:, at] = mix_s[:, at] * fade + dot(values, weights.astype(low_type))

    over_keys(first_ref, step, own_at, query_block, key_block, tile)
    total = sum_s[...]
    mixed = mix_s[...] * (1.0 / total)
    logs = max_s[...] + jnp.log2(total)
    for head in range(heads):
        at = slice(head * query_block, (head + 1) * query_block)
        out_ref[head] = mixed[:, at]
        mixed_ref[:, head * depth : (head + 1) * depth] = mixed[:, at].T.astype(low_type)
        log_ref[head] = logs[:, at]
    part_ref[...] = dot(mixed_ref[...], weight_ref[...]).astype(low_type)


def tile_of(query_block):
    def column(shape):
        return pl.BlockSpec(
            shape[:-1] + (query_block,), lambda tile, *rest: (0,) * (len(shape) - 1) + (tile,)
        )

    return column


def attend(first, queries, pieces, place, low, out_weight, query_block, key_block):
    heads, depth, rows = queries.shape
    column = tile_of(query_block)
    count = heads * query_block
    span = place.shape[0]
    return kernel_call(
        lambda *refs: mix_kernel(*refs, key_block=key_block, own_at=span - rows, scale=depth**-0.5),
        grid_spec=pltpu.PrefetchScalarGridSpec(
            num_scalar_prefetch=1,
            grid=(rows // query_block,),
            in_specs=[column(queries.shape), whole(place.shape), column(low.shape), whole(out_weight.shape)]
            + [whole(piece.shape) for piece in pieces],
            out_specs=[
                column(queries.shape),
                by_rows(query_block, (rows, heads * depth)),
                column((heads, 1, rows)),
                by_rows(query_block, (rows, out_weight.shape[1])),
            ],
            scratch_shapes=[
                pltpu.VMEM((span, depth), low_type),
                pltpu.VMEM((depth, span), low_type),
                pltpu.VMEM((1, count), sum_type),
                pltpu.VMEM((1, count), sum_type),
                pltpu.VMEM((depth, count), sum_type),
            ],
        ),
        out_shape=[
            like(queries.shape, sum_type),
            like((rows, heads * depth)),
            like((heads, 1, rows), sum_type),
            like((rows, out_weight.shape[1])),
        ],
        compiler_params=settings(62),
        name="attention",
    )(first, queries, place, low, out_weight, *pieces)


def mix_back_kernel(
    first_ref, query_ref, place_ref, low_ref, mixed_ref, grad_ref, log_ref, cos_ref, sin_ref, *refs,
    reach, key_block, own_at, scale, tiles, offset, final,
):
    pieces, refs = refs[:reach], refs[reach:]
    earlier, refs = (refs[:2], refs[3:]) if offset else ((), refs)
    out_ref, *end_refs = refs[:-6]
    key_s, turned_s, value_s, query_sum, key_sum, value_sum = refs[-6:]
    heads, depth, query_block = query_ref.shape
    tile = pl.program_id(0) + offset
    queries, grads, logs = join_heads(query_ref), join_heads(grad_ref), join_heads(log_ref)
    delta = jnp.sum(grads.astype(sum_type) * join_heads(mixed_ref), axis=0, keepdims=True)
    low = low_ref[...]
    high = tile * query_block + lax.broadcasted_iota(jnp.int32, (1, query_block), 1)

    @pl.when(pl.program_id(0) == 0)
    def gather():
        for number, piece in enumerate(pieces):
            at = slice(number * piece.shape[0], (number + 1) * piece.shape[0])
            key_s[at, :] = piece[:, :depth]
            turned_s[:, at] = piece[:, :depth].astype(sum_type).T.astype(low_type)
            value_s[at, :] = piece[:, depth:]
        if offset:
            key_sum[...] = earlier[0][...]
            value_sum[...] = earlier[1][...]
        else:
            key_sum[...] = jnp.zeros(key_sum.shape, sum_type)
            value_sum[...] = jnp.zeros(value_sum.shape, sum_type)

    query_sum[...] = jnp.zeros(query_sum.shape, sum_type)

    def step(index, own):
        start = pl.multiple_of(index * key_block, key_block)
        rows = pl.ds(start, key_block)
        keys, values, turned = key_s[rows, :], value_s[rows, :], turned_s[:, rows]
        bias = pair_bias(place_ref, rows, low, high, start, own_at, own)
        groups = 3
        width = heads // groups * query_block
        wide_bias = repeat_lanes(bias, heads // groups)
        parts = [slice(g * width, (g + 1) * width) for g in range(groups)]
        raws = [(dot(keys, queries[:, at]), dot(values, grads[:, at])) for at in parts]
        for at, (raw, grad_weights) in zip(parts, raws):
            weights = jnp.exp2(raw * (scale * log2_e) + (wide_bias - logs[:, at]))
            grad_scores = (weights * (grad_weights - delta[:, at])).astype(low_type)
            value_sum[rows, :] += dot_rows(weights.astype(low_type), grads[:, at])
            key_sum[rows, :] += dot_rows(grad_scores, queries[:, at])
            query_sum[:, at] += dot(turned, grad_scores)

    over_keys(first_ref, step, own_at, query_block, key_block, tile)
    half = depth // 2
    cosine, sine = repeat_lanes(cos_ref[...], heads), repeat_lanes(sin_ref[...], heads)
    grad_query = query_sum[...] * scale
    one, two = grad_query[:half], grad_query[half:]
    turned = jnp.concatenate([one * cosine + two * sine, two * cosine - one * sine], axis=0)
    for head in range(heads):
        part = turned[:, head * query_block : (head + 1) * query_block]
        out_ref[:, head * depth : (head + 1) * depth] = part.T.astype(low_type)

    @pl.when(pl.program_id(0) == tiles - 1)
    def finish():
        if final:
            for number, ref in enumerate(end_refs):
                at = slice(number * ref.shape[0], (number + 1) * ref.shape[0])
                ref[:, :depth] = (key_sum[at, :] * scale).astype(ref.dtype)
                ref[:, depth:] = value_sum[at, :].astype(ref.dtype)
        else:
            end_refs[0][...] = key_sum[...]
            end_refs[1][...] = value_sum[...]


def attend_back(
    first, queries, pieces, place, low, mixed, grads, logs, cosine, sine, query_block, key_block, part, earlier
):
    heads, depth, rows = queries.shape
    span = place.shape[0]
    offset, tiles = part[0], part[1] - part[0]
    final = part[1] * query_block == rows

    def column(shape):
        return pl.BlockSpec(
            shape[:-1] + (query_block,),
            lambda tile, *rest: (0,) * (len(shape) - 1) + (tile + offset,),
        )

    extra = [whole((span, depth)), whole((span, depth)), any_space] if offset else []
    ends = (
        [like((rows, 2 * depth))] * (len(pieces) - 1) + [like((rows, 2 * depth), sum_type)]
        if final
        else [like((span, depth), sum_type)] * 2
    )
    operands = [queries, place, low, mixed, grads, logs, cosine, sine, *pieces]
    return kernel_call(
        lambda *refs: mix_back_kernel(
            *refs,
            reach=len(pieces),
            key_block=key_block,
            own_at=span - rows,
            scale=depth**-0.5,
            tiles=tiles,
            offset=offset,
            final=final,
        ),
        grid_spec=pltpu.PrefetchScalarGridSpec(
            num_scalar_prefetch=1,
            grid=(tiles,),
            in_specs=[
                column(queries.shape),
                whole(place.shape),
                column(low.shape),
                column(mixed.shape),
                column(grads.shape),
                column(logs.shape),
                column(cosine.shape),
                column(sine.shape),
            ]
            + [whole(piece.shape) for piece in pieces]
            + extra,
            out_specs=[
                pl.BlockSpec((query_block, heads * depth), lambda tile, *rest: (tile + offset, 0)),
                *[whole(end.shape) for end in ends],
            ],
            scratch_shapes=[
                pltpu.VMEM((span, depth), low_type),
                pltpu.VMEM((depth, span), low_type),
                pltpu.VMEM((span, depth), low_type),
                pltpu.VMEM((depth, heads * query_block), sum_type),
                pltpu.VMEM((span, depth), sum_type),
                pltpu.VMEM((span, depth), sum_type),
            ],
        ),
        out_shape=[like((rows, heads * depth)), *ends],
        input_output_aliases={len(operands) + 3: 0} if offset else {},
        compiler_params=settings(62),
        name="attention_back",
    )(first, *operands, *(((earlier[1], earlier[2], earlier[0])) if offset else ()))


def residual_of(token_ref, own_ref, other_ref):
    mixed = own_ref[...].astype(sum_type) + other_ref[...].astype(sum_type)
    return token_ref[...].astype(sum_type) + mixed


def second_norm_kernel(token_ref, own_ref, other_ref, gain_ref, act_ref):
    residual = residual_of(token_ref, own_ref, other_ref)
    act_ref[...] = (normalize(residual)[0] * gain_ref[...]).astype(low_type)


def second_norm(tokens, own, other, gain, block=256):
    rows = by_rows(block, tokens.shape)
    return kernel_call(
        second_norm_kernel,
        grid=(tokens.shape[0] // block,),
        in_specs=[rows, rows, rows, whole(gain.shape)],
        out_specs=rows,
        out_shape=like(tokens.shape),
        compiler_params=settings(62),
        name="residual_norm",
    )(tokens, own, other, gain)


def second_back_kernel(
    own_ref, other_ref, token_ref, part_ref, part_other_ref, grad_ref, gain_ref, weight_ref,
    total_ref, low_ref, heads_ref,
):
    grad_act = own_ref[...].astype(sum_type) + other_ref[...].astype(sum_type)
    normed, factor = normalize(residual_of(token_ref, part_ref, part_other_ref))

    total = grad_ref[...].astype(sum_type) + normalize_back(
        grad_act * gain_ref[...], normed, factor
    )
    total_ref[...] = total
    low = total.astype(low_type)
    low_ref[...] = low
    turned = dot_rows(weight_ref[...], low).astype(low_type)
    heads_ref[...] = turned.reshape(heads_ref.shape)


def second_back(own, other, residual_parts, cotangent, gain, out_weight, block=256):
    rows = by_rows(block, own.shape)
    heads = out_weight.shape[0] // HEAD_DIMENSION
    shape = (heads, HEAD_DIMENSION, own.shape[0])
    return kernel_call(
        second_back_kernel,
        grid=(own.shape[0] // block,),
        in_specs=[rows] * 6 + [whole(gain.shape), whole(out_weight.shape)],
        out_specs=[rows, rows, tile_of(block)(shape)],
        out_shape=[like(own.shape, sum_type), like(own.shape), like(shape)],
        compiler_params=settings(62),
        name="residual_back",
    )(own, other, *residual_parts, cotangent, gain, out_weight)


def act_back_kernel(query_ref, pair_ref, query_weight_ref, key_weight_ref, value_weight_ref, out_ref):
    width = key_weight_ref.shape[1]
    total = dot_rows(query_ref[...], query_weight_ref[...])
    total += dot_rows(pair_ref[:, :width], key_weight_ref[...])
    total += dot_rows(pair_ref[:, width:], value_weight_ref[...])
    out_ref[...] = total.astype(low_type)


def act_back(queries, pairs, query_weight, key_weight, value_weight, block=256):
    out = (queries.shape[0], query_weight.shape[0])
    return kernel_call(
        act_back_kernel,
        grid=(out[0] // block,),
        in_specs=[
            by_rows(block, queries.shape),
            by_rows(block, pairs.shape),
            whole(query_weight.shape),
            whole(key_weight.shape),
            whole(value_weight.shape),
        ],
        out_specs=by_rows(block, out),
        out_shape=like(out),
        compiler_params=settings(32),
        name="activation_back",
    )(queries, pairs, query_weight, key_weight, value_weight)


def last_rows_kernel(
    own_ref, other_ref, total_ref, gain_ref, token_ref, part_ref, part_other_ref, out_own_ref, out_other_ref,
    grad_ref, out_ref,
):
    grad_act = own_ref[...].astype(sum_type) + other_ref[...].astype(sum_type)
    normed, factor = normalize(token_ref[...].astype(sum_type))
    grad_ref[...] = total_ref[...] + normalize_back(grad_act * gain_ref[...], normed, factor)
    mixed = out_own_ref[...].astype(sum_type) + out_other_ref[...].astype(sum_type)
    out_ref[...] = (residual_of(token_ref, part_ref, part_other_ref) + mixed).astype(low_type)


def last_rows(own, other, total, gain, residual_parts, out_own, out_other, block=256):
    rows = by_rows(block, own.shape)
    return kernel_call(
        last_rows_kernel,
        grid=(own.shape[0] // block,),
        in_specs=[rows] * 3 + [whole(gain.shape)] + [rows] * 5,
        out_specs=[rows, rows],
        out_shape=[like(own.shape, sum_type), like(own.shape)],
        compiler_params=settings(62),
        name="last_rows",
    )(own, other, total, gain, *residual_parts, out_own, out_other)


def slot_of(rest, bit, first):
    return ((rest >> first) << (first + 1)) | (bit << first) | (rest & ((1 << first) - 1))


def place_slots(me, total_ref, send_ref, keep_ref, first, columns=slice(None)):
    for rest in range(send_ref.shape[0]):
        for bit, ref in ((1, send_ref), (0, keep_ref)):
            ref[rest] = total_ref[slot_of(rest, bit, first) ^ me, :, columns].astype(low_type)


def grad_kernel(me_ref, left_ref, right_ref, *refs, firsts):
    total_s = refs[-1]
    total_s[...] = dot_columns(left_ref[...], right_ref[...]).reshape(total_s.shape)
    width = total_s.shape[2] // len(firsts)
    for index, first in enumerate(firsts):
        columns = slice(index * width, (index + 1) * width)
        place_slots(me_ref[0], total_s, refs[2 * index], refs[2 * index + 1], first, columns)


def grad_parts(me, left, right, devices, firsts, name):
    rows, width = left.shape[1] // devices, right.shape[1]
    half = (devices // 2, rows, width // len(firsts))
    return kernel_call(
        lambda *refs: grad_kernel(*refs, firsts=firsts),
        grid_spec=pltpu.PrefetchScalarGridSpec(
            num_scalar_prefetch=1,
            grid=(1,),
            in_specs=[whole(left.shape), whole(right.shape)],
            out_specs=[whole(half)] * (2 * len(firsts)),
            scratch_shapes=[pltpu.VMEM((devices, rows, width), sum_type)],
        ),
        out_shape=[like(half)] * (2 * len(firsts)),
        compiler_params=settings(62),
        name=name,
    )(me, left, right)


def pair_grad_kernel(me_ref, act_ref, own_ref, cos_ref, sin_ref, *refs, reach, firsts):
    pieces, refs = refs[:reach], refs[reach:]
    out_ref, total_s = refs[0], refs[-1]
    total = own_ref[...]
    for piece in pieces:
        total += piece[...].astype(sum_type)
    width = HEAD_DIMENSION
    keys = total[:, :width]
    cosine, sine = full_tables(cos_ref, sin_ref)
    turned = pltpu.roll(keys, width // 2, 1)
    pairs = jnp.concatenate([keys * cosine - turned * sine, total[:, width:]], axis=1).astype(low_type)
    out_ref[...] = pairs
    total_s[...] = dot_columns(act_ref[...], pairs).reshape(total_s.shape)
    for index, first in enumerate(firsts):
        columns = slice(index * width, (index + 1) * width)
        place_slots(me_ref[0], total_s, refs[2 * index + 1], refs[2 * index + 2], first, columns)


def pair_grads(me, act, own, pieces, cosine, sine, devices, firsts):
    rows = act.shape[1] // devices
    half = (devices // 2, rows, HEAD_DIMENSION)
    operands = (act, own, cosine, sine, *pieces)
    return kernel_call(
        lambda *refs: pair_grad_kernel(*refs, reach=len(pieces), firsts=firsts),
        grid_spec=pltpu.PrefetchScalarGridSpec(
            num_scalar_prefetch=1,
            grid=(1,),
            in_specs=[whole(operand.shape) for operand in operands],
            out_specs=[whole(own.shape)] + [whole(half)] * 4,
            scratch_shapes=[pltpu.VMEM((devices, rows, 2 * HEAD_DIMENSION), sum_type)],
        ),
        out_shape=[like(own.shape)] + [like(half)] * 4,
        compiler_params=settings(62),
        name="key_value_grad",
    )(me, *operands)


def expert_kernel(
    me_ref, act_hbm, grad_hbm, gates_ref, gate_hbm, up_hbm, down_hbm, *refs, experts, firsts, later
):
    refs = refs[2:] if later else refs
    outs, (hidden_hbm, inner_hbm), refs = refs[:6], refs[6:8], refs[8:]
    act_s, grad_s, wide_s, down_s, raw_s, back_s, hidden_s, inner_s, stage_s = refs[:9]
    act_sem, wide_sems, down_sems, pass_sems, out_sems, *total_s = refs[9:]
    rows, hidden, me = act_s.shape[0], gate_hbm.shape[2], me_ref[0]
    first_expert, count = experts

    def fetch(source, target, sem):
        copy = pltpu.make_async_copy(source, target, sem)
        copy.start()
        return copy

    def fetch_wide(expert):
        slot = expert % 2
        return [
            fetch(gate_hbm.at[first_expert + expert], wide_s.at[slot, :, :hidden], wide_sems.at[expert, 0]),
            fetch(up_hbm.at[first_expert + expert], wide_s.at[slot, :, hidden:], wide_sems.at[expert, 1]),
        ]

    def fetch_down(expert):
        pair, at = expert // 2, expert % 2 * hidden
        target = down_s.at[pair % 2, at : at + hidden]
        return [fetch(down_hbm.at[first_expert + expert], target, down_sems.at[expert])]

    def arrive(copies):
        for copy in copies:
            copy.wait()

    def pointwise(expert):
        slot = expert % 2
        at = slice(slot * hidden, (slot + 1) * hidden)
        for start in range(0, rows, 256):
            block = pl.ds(start, 256)
            inner = raw_s[slot, block, :hidden]
            up = raw_s[slot, block, hidden:]
            lane = lax.broadcasted_iota(jnp.int32, (256, LANES), 1)
            mine = lane == first_expert + expert
            gate = jnp.sum(jnp.where(mine, gates_ref[block, :], 0.0), axis=1, keepdims=True)
            square = inner * inner
            bent = jnp.tanh(tanh_scale * inner * (1.0 + tanh_cubic * square))
            half = 0.5 * (1.0 + bent)
            gelu = inner * half
            slope = half + (0.5 * tanh_scale) * inner * (1.0 - bent * bent) * (
                1.0 + (3.0 * tanh_cubic) * square
            )
            back = back_s[block, at] * gate
            hidden_s[block, at] = (gelu * up * gate).astype(low_type)
            inner_s[slot, block, :hidden] = (back * up * slope).astype(low_type)
            inner_s[slot, block, hidden:] = (back * gelu).astype(low_type)

    given = []

    def gradient(left_s, right, chain, part):
        total = dot_columns(left_s[...], right)
        columns = pl.ds(part * 2 * hidden, 2 * hidden)
        if not total_s:
            stage_s[chain, part] = total.astype(low_type).reshape(stage_s.shape[2:])
            for rest in range(stage_s.shape[2] // 2):
                for side, bit in enumerate((1, 0)):
                    source = stage_s.at[chain, part, slot_of(rest, bit, firsts[chain]) ^ me]
                    target = outs[2 * chain + side].at[rest, :, columns]
                    given.append(fetch(source, target, out_sems.at[chain, part, side]))
            return
        total_s[0][...] = total.reshape(total_s[0].shape)
        send_s, keep_s = stage_s.at[chain, part, 0], stage_s.at[chain, part, 1]
        place_slots(me, total_s[0], send_s, keep_s, firsts[chain])
        for side, source in enumerate((send_s, keep_s)):
            target = outs[2 * chain + side].at[:, :, columns]
            given.append(fetch(source, target, out_sems.at[chain, part, side]))

    wide_in = {0: fetch_wide(0)}
    head, tail = pl.ds(0, rows // 4), pl.ds(rows // 4, rows - rows // 4)
    act_in = [
        fetch(act_hbm.at[part], act_s.at[part], act_sem.at[number])
        for number, part in enumerate((head, tail))
    ]
    grad_in = [fetch(grad_hbm, grad_s, act_sem.at[2])]
    down_in = {expert: fetch_down(expert) for expert in range(2)}
    wide_in[1] = fetch_wide(1)
    for expert in range(2, min(4, count)):
        down_in[expert] = fetch_down(expert)
    passed = []
    for pair in range(count // 2):
        one, two = 2 * pair, 2 * pair + 1
        arrive(wide_in[one])
        if pair == 0:
            for part, copy in zip((head, tail), act_in):
                copy.wait()
                raw_s[0, part, :] = dot(act_s[part, :], wide_s[0])
        else:
            raw_s[0] = dot(act_s[...], wide_s[0])
        if one + 2 < count:
            wide_in[one + 2] = fetch_wide(one + 2)
        if pair == 0:
            arrive(grad_in)
        arrive(down_in[one] + down_in[two])
        back_s[...] = dot_rows(grad_s[...], down_s[pair % 2])
        arrive(wide_in[two])
        raw_s[1] = dot(act_s[...], wide_s[1])
        if two + 2 < count:
            wide_in[two + 2] = fetch_wide(two + 2)
        arrive(passed)
        pointwise(0 + one)
        chain = min(one // (count // 2), 1)
        gradient(act_s, inner_s[0], chain, one % (count // 2))
        pointwise(two)
        at = first_expert // 2 + pair
        passed = [
            fetch(hidden_s, hidden_hbm.at[at], pass_sems.at[pair, 0]),
            fetch(inner_s, inner_hbm.at[pl.ds(2 * at, 2)], pass_sems.at[pair, 1]),
        ]
        chain = min(two // (count // 2), 1)
        gradient(act_s, inner_s[1], chain, two % (count // 2))
        gradient(grad_s, hidden_s[...], 2, pair)
    arrive(passed)
    arrive(given)


def expert_group(
    experts, me, act, cotangent, gates, gate_weight, up_weight, down_weight, earlier, devices, firsts
):
    rows, model = act.shape
    hidden = gate_weight.shape[2]
    parts = experts[1] // 2
    half = (devices // 2, model // devices, 2 * hidden)
    joined = half[:2] + (parts * 2 * hidden,)
    hidden_all = like((EXPERTS // 2, rows, 2 * hidden))
    inner_all = like((EXPERTS, rows, 2 * hidden))
    later = earlier is not None
    if half[1] % 16:
        stage, totals = (3, parts, 2) + half, [pltpu.VMEM((devices,) + half[1:], sum_type)]
    else:
        stage, totals = (3, parts, devices) + half[1:], []
    return kernel_call(
        lambda *refs: expert_kernel(*refs, experts=experts, firsts=firsts, later=later),
        grid_spec=pltpu.PrefetchScalarGridSpec(
            num_scalar_prefetch=1,
            grid=(1,),
            in_specs=[any_space, any_space, whole(gates.shape)]
            + [any_space] * (3 + (2 if later else 0)),
            out_specs=[any_space] * 8,
            scratch_shapes=[
                pltpu.VMEM((rows, model), low_type),
                pltpu.VMEM((rows, model), low_type),
                pltpu.VMEM((2, model, 2 * hidden), low_type),
                pltpu.VMEM((2, 2 * hidden, model), low_type),
                pltpu.VMEM((2, rows, 2 * hidden), sum_type),
                pltpu.VMEM((rows, 2 * hidden), sum_type),
                pltpu.VMEM((rows, 2 * hidden), low_type),
                pltpu.VMEM((2, rows, 2 * hidden), low_type),
                pltpu.VMEM(stage, low_type),
                pltpu.SemaphoreType.DMA((3,)),
                pltpu.SemaphoreType.DMA((experts[1], 2)),
                pltpu.SemaphoreType.DMA((experts[1],)),
                pltpu.SemaphoreType.DMA((parts, 2)),
                pltpu.SemaphoreType.DMA((3, parts, 2)),
            ]
            + totals,
        ),
        out_shape=[like(joined)] * 6 + [hidden_all, inner_all],
        input_output_aliases={7: 6, 8: 7} if later else {},
        compiler_params=settings(62),
        name="experts",
    )(me, act, cotangent, gates, gate_weight, up_weight, down_weight, *(earlier or ()))


def inner_back_kernel(inner_ref, gate_ref, up_ref, out_ref, total_s):
    expert = pl.program_id(0)
    hidden = gate_ref.shape[2]

    @pl.when(expert == 0)
    def clear():
        total_s[...] = jnp.zeros(total_s.shape, sum_type)

    weight = jnp.concatenate([gate_ref[0], up_ref[0]], axis=1)
    total_s[...] += dot_rows(inner_ref[0], weight)

    @pl.when(expert == EXPERTS - 1)
    def finish():
        out_ref[...] = total_s[...].astype(low_type)


def inner_back(inner, gate_weight, up_weight):
    rows, model = inner.shape[1], gate_weight.shape[1]
    one = lambda shape: pl.BlockSpec((1,) + shape[1:], lambda expert: (expert, 0, 0))
    return kernel_call(
        inner_back_kernel,
        grid=(EXPERTS,),
        in_specs=[one(inner.shape), one(gate_weight.shape), one(up_weight.shape)],
        out_specs=whole((rows, model)),
        out_shape=like((rows, model)),
        scratch_shapes=[pltpu.VMEM((rows, model), sum_type)],
        compiler_params=settings(62),
        name="expert_back",
    )(inner, gate_weight, up_weight)


def expert_out_kernel(hidden_ref, down_ref, out_ref, total_s):
    pair = pl.program_id(0)

    @pl.when(pair == 0)
    def clear():
        total_s[...] = jnp.zeros(total_s.shape, sum_type)

    total_s[...] += dot(hidden_ref[0], down_ref[...])

    @pl.when(pair == EXPERTS // 2 - 1)
    def finish():
        out_ref[...] = total_s[...].astype(low_type)


def expert_out(hidden, down_weight):
    rows, model = hidden.shape[1], down_weight.shape[2]
    flat = down_weight.reshape(-1, model)
    return kernel_call(
        expert_out_kernel,
        grid=(EXPERTS // 2,),
        in_specs=[
            pl.BlockSpec((1,) + hidden.shape[1:], lambda pair: (pair, 0, 0)),
            pl.BlockSpec((hidden.shape[2], model), lambda pair: (pair, 0)),
        ],
        out_specs=whole((rows, model)),
        out_shape=like((rows, model)),
        scratch_shapes=[pltpu.VMEM((rows, model), sum_type)],
        compiler_params=settings(62),
        name="expert_out",
    )(hidden, flat)


def shifted(shard, by):
    size = lax.axis_size("ctx")
    return lax.ppermute(
        shard, "ctx", [(i, i + by) for i in range(size) if 0 <= i + by < size]
    )


def swapped(part):
    return lax.ppermute(part, "ws", [(0, 1), (1, 0)])


def without(slot, bits):
    for bit in sorted(bits, reverse=True):
        slot = ((slot >> (bit + 1)) << bit) | (slot & ((1 << bit) - 1))
    return slot


def with_zeros(index, bits):
    for bit in sorted(bits):
        index = ((index >> bit) << (bit + 1)) | (index & ((1 << bit) - 1))
    return index


def flip(array, bit):
    size = lax.axis_size("ctx")
    return lax.ppermute(array, "ctx", [(i, i ^ (1 << bit)) for i in range(size)])


class Chains:
    def __init__(self, orders):
        self.orders = orders
        self.sections = [[] for _ in orders]
        self.joined = [[] for _ in orders]
        self.done = 1
        self.waiting = None

    def first_steps(self, sends, keeps):
        self.keeps = keeps
        return [flip(send, order[0]) for send, order in zip(sends, self.orders)]

    def land(self, arrived):
        for chain, part in enumerate(arrived):
            held = self.orders[chain][:1]
            self.sections[chain].append([(self.keeps[chain], held, 0), (part, held, 0)])

    def widths(self, chain):
        return [parts[0][0].shape[2] for parts in self.sections[chain]]

    def ending(self):
        return self.done == len(self.orders[0])

    def arrays(self, chains=None):
        flat = []
        for chain in range(len(self.orders)) if chains is None else chains:
            for parts in self.sections[chain]:
                flat += parts
            flat += self.joined[chain]
        return flat

    def replace(self, arrays, chains=None):
        arrays = iter(arrays)
        fresh = lambda parts: [(next(arrays), held, column) for _, held, column in parts]
        for chain in range(len(self.orders)) if chains is None else chains:
            self.sections[chain] = [fresh(parts) for parts in self.sections[chain]]
            self.joined[chain] = fresh(self.joined[chain])

    @staticmethod
    def totals(refs, sections, joined):
        own = [[next(refs) for _ in parts] for parts in sections]
        shared = [(next(refs), column) for _, _, column in joined]
        at, found = 0, []
        for parts, refs_of in zip(sections, own):
            width = parts[0][0].shape[2]
            total = refs_of[0][0].astype(sum_type)
            for ref, (_, _, column) in zip(refs_of[1:], parts[1:]):
                total += ref[0, :, column : column + width].astype(sum_type)
            for ref, column in shared:
                total += ref[0, :, column + at : column + at + width].astype(sum_type)
            found.append(total)
            at += width
        return found

    def sums(self, refs, chains=None):
        refs = iter(refs)
        return [
            self.totals(refs, self.sections[chain], self.joined[chain])
            for chain in (range(len(self.orders)) if chains is None else chains)
        ]

    @staticmethod
    def sum_call(groups, parts_of, done_count, bits, done_bits):
        slots = lax.axis_size("ctx") >> (done_count + 1)
        specs, operands, shapes, chain = [], [], [], 0
        for group in groups:
            width = 0
            for sections, joined in group:
                for array, held, _ in parts_of[chain]:

                    def index(tile, done=done_bits[chain], bit=bits[chain], held=held):
                        slot = with_zeros(tile, list(done) + [bit]) | (1 << bit)
                        return (without(slot, held), 0, 0)

                    specs.append(pl.BlockSpec((1,) + array.shape[1:], index))
                    operands.append(array)
                width += sum(parts[0][0].shape[2] for parts in sections)
                rows = sections[0][0][0].shape[1]
                chain += 1
            shapes.append((slots, rows, width))

        def run(*refs):
            reading, outs = iter(refs[: len(operands)]), refs[len(operands) :]
            for out, group in zip(outs, groups):
                at = 0
                for sections, joined in group:
                    for total in Chains.totals(reading, sections, joined):
                        out[0, :, at : at + total.shape[1]] = total.astype(low_type)
                        at += total.shape[1]

        return kernel_call(
            run,
            grid=(slots,),
            in_specs=specs,
            out_specs=[pl.BlockSpec((1,) + shape[1:], lambda tile: (tile, 0, 0)) for shape in shapes],
            out_shape=[like(shape) for shape in shapes],
            compiler_params=settings(62),
            name="sum_parts",
        )(*operands)

    def alike(self, chains):
        bits = [self.orders[chain][self.done] for chain in chains]
        return [
            (bit, [chain for chain, other in zip(chains, bits) if other == bit])
            for bit in dict.fromkeys(bits)
        ]

    def prepare(self, apart=False):
        chains = range(len(self.orders))
        self.groups = self.alike(chains)
        if apart:
            self.groups = [(self.orders[chain][self.done], [chain]) for chain in chains]
        order = [chain for _, group in self.groups for chain in group]
        self.waiting = self.sum_call(
            [[(self.sections[chain], self.joined[chain]) for chain in group] for _, group in self.groups],
            [self.arrays([chain]) for chain in order],
            self.done,
            [self.orders[chain][self.done] for chain in order],
            [self.orders[chain][: self.done] for chain in order],
        )

    def launch(self, count=None):
        count = len(self.waiting) if count is None else count
        for send, (bit, group) in zip(self.waiting[:count], self.groups[:count]):
            array, column = flip(send, bit), 0
            for chain in group:
                held = self.orders[chain][: self.done + 1]
                self.joined[chain].append((array, held, column))
                column += sum(self.widths(chain))
        self.waiting, self.groups = self.waiting[count:], self.groups[count:]
        if not self.groups:
            self.done += 1


def end_experts(chains, hidden):
    parts = chains.arrays()
    rows = parts[0][0].shape[1]
    shapes = [(EXPERTS, rows, hidden)] * 3

    def run(*refs):
        gate_ref, up_ref, down_ref = refs[len(parts) :]
        totals = chains.sums(refs[: len(parts)])
        for pair in range(EXPERTS // 2):
            for chain in range(2):
                gate_ref[2 * pair + chain] = totals[chain][pair][:, :hidden]
                up_ref[2 * pair + chain] = totals[chain][pair][:, hidden:]
                columns = slice(chain * hidden, (chain + 1) * hidden)
                down_ref[2 * pair + chain] = totals[2][pair][:, columns]

    return kernel_call(
        run,
        grid=(1,),
        in_specs=[
            pl.BlockSpec((1,) + array.shape[1:], lambda tile: (0, 0, 0)) for array, _, _ in parts
        ],
        out_specs=[whole(shape) for shape in shapes],
        out_shape=[like(shape, sum_type) for shape in shapes],
        compiler_params=settings(62),
        name="expert_gradients",
    )(*[array for array, _, _ in parts])


def end_others(chains):
    parts = chains.arrays()
    rows = parts[0][0].shape[1]
    count = len(chains.orders)
    out_width = sum(chains.widths(chain)[0] for chain in range(count))
    shapes = [
        (rows, out_width),
        (rows, sum(chains.widths(chain)[1] for chain in range(count))),
        (rows, chains.widths(0)[2]),
        (rows, chains.widths(1)[2]),
    ]

    def run(*refs):
        out_ref, query_ref, key_ref, value_ref = refs[len(parts) :]
        totals = chains.sums(refs[: len(parts)])
        at = 0
        for found in totals:
            width = found[0].shape[1]
            out_ref[:, at : at + width] = found[0]
            query_ref[:, at : at + width] = found[1]
            at += width
        key_ref[...] = totals[0][2]
        value_ref[...] = totals[1][2]

    return kernel_call(
        run,
        grid=(1,),
        in_specs=[
            pl.BlockSpec((1,) + array.shape[1:], lambda tile: (0, 0, 0)) for array, _, _ in parts
        ],
        out_specs=[whole(shape) for shape in shapes],
        out_shape=[like(shape, sum_type) for shape in shapes],
        compiler_params=settings(62),
        name="other_gradients",
    )(*[array for array, _, _ in parts])


def tie(*values):
    return lax.optimization_barrier(values)


def advance(chains, anchor, apart=False):
    if chains.ending():
        return anchor
    anchor = settle(chains, anchor)
    chains.prepare(apart)
    anchor, chains.waiting = tie(anchor, chains.waiting)
    chains.launch()
    return anchor


def chain_arrays(chains, some=None):
    return [array for array, _, _ in chains.arrays(some)]


def settle(chains, anchor, some=None):
    anchor, arrays = tie(anchor, chain_arrays(chains, some))
    chains.replace(arrays, some)
    return anchor


def chain_orders(bits):
    rest = tuple(range(3, bits))
    return ((0, 1, 2) + rest, (1, 2, 0) + rest, (2, 0, 1) + rest)


def body(
    tokens,
    cotangent,
    first_gain,
    query_weight,
    key_projection_weight,
    value_projection_weight,
    out_weight,
    second_gain,
    gate_weight,
    up_weight,
    down_weight,
    segments,
    live_mask,
    routes,
    gate_values,
):
    rows, model = tokens.shape
    devices = lax.axis_size("ctx")
    bits = devices.bit_length() - 1
    index = lax.axis_index("ctx")
    me = index.astype(jnp.int32).reshape(1)
    first_row = index * rows
    query_block, key_block = 256, 256
    gain_one, gain_two = first_gain[None, :], second_gain[None, :]
    orders = chain_orders(bits)
    firsts = tuple(order[0] for order in orders)

    half = HEAD_DIMENSION // 2
    frequency = rope_base ** (-2.0 * jnp.arange(half, dtype=sum_type) / HEAD_DIMENSION)
    positions = (first_row + jnp.arange(rows, dtype=jnp.int32)).astype(sum_type)
    angles = frequency[:, None] * positions[None, :]
    cosine, sine = jnp.cos(angles), jnp.sin(angles)

    activation, own_pair = project_keys(
        tokens, gain_one, key_projection_weight, value_projection_weight, cosine, sine
    )
    reach = min(devices, (DOC_MAX + rows - 2) // rows + 1)
    pieces = [shifted(own_pair, by) for by in range(reach - 1, 0, -1)] + [own_pair]
    queries = project_queries(activation, query_weight, cosine, sine)
    span = reach * rows
    own_at = span - rows
    padded_segments = jnp.concatenate([jnp.full((own_at,), -1, jnp.int32), segments])
    padded_live = jnp.concatenate([jnp.zeros((own_at,), jnp.int32), live_mask])
    key_segments = lax.dynamic_slice_in_dim(padded_segments, first_row, span, 0)
    key_live = lax.dynamic_slice_in_dim(padded_live, first_row, span, 0)
    place, low, gates = tables(
        key_segments[:, None], key_segments[None, own_at:], key_live[:, None], routes, gate_values
    )
    first_block = (low[0, ::query_block] + own_at) // key_block
    queries, gates, low, place, first_block = tie(queries, gates, low, place, first_block)

    mixed_turned, mixed, logs, part = attend(
        first_block, queries, pieces, place, low, out_weight, query_block, key_block
    )
    residual_parts = (tokens, part, swapped(part))
    act_two = second_norm(*residual_parts, gain_two)

    hidden = gate_weight.shape[2]
    experts = Chains(orders)
    earlier, flying = None, []
    for pair in range(EXPERTS // 2):
        outs = expert_group(
            (2 * pair, 2), me, act_two, cotangent, gates, gate_weight, up_weight, down_weight, earlier,
            devices, firsts,
        )
        earlier = outs[-2:]
        act_two, earlier, sends, landed = tie(act_two, earlier, outs[0:6:2], flying)
        if pair:
            experts.land(landed)
        flying = experts.first_steps(sends, outs[1:6:2])
    hidden_all, inner_all = earlier
    back = inner_back(inner_all, gate_weight, up_weight)
    back, landed = tie(back, flying)
    experts.land(landed)
    back_other = swapped(back)
    back = advance(experts, back)
    total, total_low, grad_heads = second_back(
        back, back_other, residual_parts, cotangent, gain_two, out_weight
    )
    rest = tuple(range(3, bits))
    others = Chains(((0, 1, 2) + rest, (1, 0, 2) + rest))
    other_firsts = (0, 1)
    out_outs = grad_parts(me, total_low, mixed, devices, other_firsts, "out_grad")
    grad_heads, out_outs = tie(grad_heads, out_outs)

    tiles = rows // query_block
    back_args = (
        queries, pieces, place, low, mixed_turned, grad_heads, logs, cosine, sine, query_block, key_block
    )
    sums = attend_back(first_block, *back_args, (0, tiles // 2), None)
    sums = advance(experts, sums)
    grad_queries, *far, own = attend_back(first_block, *back_args, (tiles // 2, tiles), sums)
    returned = [shifted(piece, at + 1 - reach) for at, piece in enumerate(far)]
    query_outs = grad_parts(me, activation, grad_queries, devices, other_firsts, "query_grad")
    grad_queries = settle(experts, grad_queries)
    while experts.done + 1 < bits:
        grad_queries = advance(experts, grad_queries)
    experts.prepare(apart=True)
    own, returned, query_outs, experts.waiting = tie(own, returned, query_outs, experts.waiting)
    out_flying = others.first_steps(out_outs[0:4:2], out_outs[1:4:2])
    out_keeps = others.keeps
    flying = others.first_steps(query_outs[0:4:2], query_outs[1:4:2])
    query_keeps = others.keeps
    experts.launch(1)
    grad_pairs, *outs = pair_grads(
        me, activation, own, returned, cosine, sine, devices, other_firsts
    )
    grad_pairs, outs, landed = tie(grad_pairs, outs, out_flying)
    others.keeps = out_keeps
    others.land(landed)
    pair_flying = others.first_steps(outs[0:4:2], outs[1:4:2])
    pair_keeps = others.keeps
    grad_act = act_back(
        grad_queries, grad_pairs, query_weight, key_projection_weight, value_projection_weight
    )
    grad_act, landed, pair_landed = tie(grad_act, flying, pair_flying)
    others.keeps = query_keeps
    others.land(landed)
    others.keeps = pair_keeps
    others.land(pair_landed)
    grad_act = settle(experts, grad_act, (0,))
    grad_act, experts.waiting = tie(grad_act, experts.waiting)
    experts.launch(1)
    act_other = swapped(grad_act)
    hidden_all = advance(others, hidden_all)
    out_part = expert_out(hidden_all, down_weight)
    out_part = settle(experts, out_part, (1,))
    out_part, grad_act, act_other, other_arrays = tie(
        out_part, grad_act, act_other, chain_arrays(others)
    )
    others.replace(other_arrays)
    out_part, experts.waiting = tie(out_part, experts.waiting)
    experts.launch()
    out_other = swapped(out_part)
    out_part = advance(others, out_part, apart=True)
    token_grad, output = last_rows(
        grad_act, act_other, total, gain_one, residual_parts, out_part, out_other
    )
    token_grad = settle(experts, token_grad)
    token_grad = advance(others, token_grad)
    own_rows = model // devices
    gate_grad, up_grad, down_grad = end_experts(experts, hidden)
    while not others.ending():
        token_grad = advance(others, token_grad)
    down_grad = down_grad.transpose(0, 2, 1)
    out_turned, query_grad, key_grad, value_grad = end_others(others)
    out_grad = out_turned.T

    def own_part(weight, dimension=0):
        return lax.dynamic_slice_in_dim(weight, index * own_rows, own_rows, dimension).astype(sum_type)

    first_part = (
        jnp.sum(query_grad * own_part(query_weight), axis=1)
        + jnp.sum(key_grad * own_part(key_projection_weight), axis=1)
        + jnp.sum(value_grad * own_part(value_projection_weight), axis=1)
    )
    second_part = jnp.sum(
        gate_grad * own_part(gate_weight, 1) + up_grad * own_part(up_weight, 1), axis=(0, 2)
    )
    gain_parts = jnp.stack([first_part, second_part])
    gains = jnp.stack([first_gain, second_gain])
    gain_grads = (gain_parts + swapped(gain_parts)) / lax.dynamic_slice_in_dim(
        gains, index * own_rows, own_rows, 1
    )
    grad_first, grad_second = gain_grads[0], gain_grads[1]
    return (
        output,
        token_grad,
        grad_first,
        query_grad,
        key_grad,
        value_grad,
        out_grad,
        grad_second,
        gate_grad,
        up_grad,
        down_grad,
    )


def solution(mesh):
    return jax.shard_map(
        body,
        mesh=mesh,
        in_specs=(
            P("ctx", None),
            P("ctx", None),
            P(),
            P(None, "ws"),
            P(None, "ws"),
            P(None, "ws"),
            P("ws", None),
            P(),
            P(None, None, "ws"),
            P(None, None, "ws"),
            P(None, "ws", None),
            P(),
            P(),
            P("ctx", None),
            P("ctx", None),
        ),
        out_specs=(
            P("ctx", None),
            P("ctx", None),
            P("ctx"),
            P("ctx", "ws"),
            P("ctx", "ws"),
            P("ctx", "ws"),
            P("ws", "ctx"),
            P("ctx"),
            P(None, "ctx", "ws"),
            P(None, "ctx", "ws"),
            P(None, "ws", "ctx"),
        ),
        check_vma=False,
    )
```
